32 devices in a mesh: dp: 16 (over z, x, core), tp: 2 (over y).
Axes of the slice: x: 2, y: 2, z: 4, core: 2. Of those that a mesh axis runs over, the one named last changes fastest.
Arguments:
- tokens: bfloat16 [24576, 1024], P(('dp', 'tp')), may hold values from -6 to 6
- carried: float32 [16, 512, 1024], P('dp', None, 'tp'), may hold values from -6 to 6
- restart: int32 [16], P('dp'), may hold values from 0 to 1
- lengths: int32 [16], P('dp'), may hold values from 1024 to 1536, as said below
- gain_attend: bfloat16 [1024], P('dp'), may hold values from 0.5 to 1.5
- input_weights: bfloat16 [3, 1024, 1024], P(None, 'dp', 'tp'), may hold values from -0.125 to 0.125
- state_weights: bfloat16 [8, 128, 384], P('tp', 'dp'), may hold values from -0.35355339 to 0.35355339
- update_weights: bfloat16 [8, 128, 128], P('tp', 'dp'), may hold values from -1 to 1
- gate_bias: bfloat16 [8, 128], P('tp', 'dp'), may hold values from -3 to 3
- initial_state: bfloat16 [512, 1024], P('dp', 'tp'), may hold values from -6 to 6
- output_weights: bfloat16 [1024, 1024], P('tp', 'dp'), may hold values from -4 to 4
- gain_feed: bfloat16 [1024], P('dp'), may hold values from 0.5 to 1.5
- feed_up: bfloat16 [1024, 4096], P('dp', 'tp'), may hold values from -0.1875 to 0.1875
- feed_down: bfloat16 [4096, 1024], P('tp', 'dp'), may hold values from -0.09375 to 0.09375
- grad_mixed: bfloat16 [24576, 1024], P(('dp', 'tp')), may hold values from -6 to 6
- grad_final: bfloat16 [16, 512, 1024], P('dp', None, 'tp'), may hold values from -6 to 6
Outputs:
- mixed: bfloat16 [24576, 1024], P(('dp', 'tp'))
- final_memory: float32 [16, 512, 1024], P('dp', None, 'tp')
- grad_tokens: float32 [24576, 1024], P(('dp', 'tp'))
- grad_carried: float32 [16, 512, 1024], P('dp', None, 'tp')
- grad_gain_attend: float32 [1024], P('dp')
- grad_input_weights: float32 [3, 1024, 1024], P(None, 'dp', 'tp')
- grad_state_weights: float32 [8, 128, 384], P('tp', 'dp')
- grad_update_weights: float32 [8, 128, 128], P('tp', 'dp')
- grad_gate_bias: float32 [8, 128], P('tp', 'dp')
- grad_initial_state: float32 [512, 1024], P('dp', 'tp')
- grad_output_weights: float32 [1024, 1024], P('tp', 'dp')
- grad_gain_feed: float32 [1024], P('dp')
- grad_feed_up: float32 [1024, 4096], P('dp', 'tp')
- grad_feed_down: float32 [4096, 1024], P('tp', 'dp')
The draws below stay inside these ranges and needn't reach their ends.
Inputs may be any that keep to these rules, and one draw needn't show every extreme that they name: `lengths`: of each two consecutive sequences (0 and 1, 2 and 3, and so on) one, drawn from the seed, is exactly 1536 tokens long.
All inputs are finite; a program needn't handle non-finite values.
Results may differ from the reference program's by a relative error of at most 0.012.
Values may be sent and summed in bfloat16 or wider, within the bound.
A program may use at most 256 MiB of HBM per device.

```python
from functools import partial
import jax
import jax.numpy as jnp
from jax import lax

D = 1024
H = 8
HD = 128
FF = 4096
S = 512
BLK = 512
LEN = 1536
MINLEN = 1024
NB = 3
SEQS = 16
TOKENS = 24576


def draw_lengths(key, part):
    key = jax.random.fold_in(key, 7)
    key_one, key_two, key_three, key_four = jax.random.split(key, 4)
    spread = LEN - MINLEN + 1
    shortest = jnp.minimum(jnp.minimum(jax.random.randint(key_one, (SEQS,), 0, spread, dtype=jnp.int32), jax.random.randint(key_two, (SEQS,), 0, spread, dtype=jnp.int32)), jax.random.randint(key_three, (SEQS,), 0, spread, dtype=jnp.int32))
    chosen = jax.random.randint(key_four, (SEQS // 2,), 0, 2, dtype=jnp.int32)
    position = jnp.arange(SEQS, dtype=jnp.int32) % 2
    full_row = position == jnp.repeat(chosen, 2, total_repeat_length=SEQS)
    return jnp.where(full_row, LEN, MINLEN + shortest).astype(jnp.int32)


def draw_tokens(key, part):
    key = jax.random.fold_in(key, 11)
    key_one = jax.random.fold_in(key, 0)
    values = jnp.clip(jax.random.normal(key_one, (TOKENS, D), jnp.float32), -6.0, 6.0)
    return values.astype(jnp.bfloat16)


def draw_carried(key, part):
    key = jax.random.fold_in(key, 13)
    values = jnp.clip(jax.random.normal(key, (SEQS, S, D), jnp.float32), -6.0, 6.0)
    return values.astype(jnp.float32)


def draw_initial_state(key, part):
    key = jax.random.fold_in(key, 17)
    values = jnp.clip(jax.random.normal(key, (S, D), jnp.float32), -6.0, 6.0)
    return values.astype(jnp.bfloat16)


def draw_input_weights(key, part):
    key = jax.random.fold_in(key, 19)
    factor = D ** (-0.5)
    values = jnp.clip(jax.random.normal(key, (3, D, D), jnp.float32), -4.0, 4.0) * factor
    return values.astype(jnp.bfloat16)


def draw_state_weights(key, part):
    key = jax.random.fold_in(key, 23)
    factor = HD ** (-0.5)
    values = jnp.clip(jax.random.normal(key, (H, HD, 3 * HD), jnp.float32), -4.0, 4.0) * factor
    return values.astype(jnp.bfloat16)


def set_ends(values, rng, least, largest):
    index_at = [jax.random.randint(jax.random.fold_in(rng, axis), (), 0, length) for axis, length in enumerate(values.shape)]
    longest = values.shape.index(max(values.shape))
    neighbour = index_at[:longest] + [(index_at[longest] + 1) % values.shape[longest]] + index_at[longest + 1:]
    return values.at[tuple(index_at)].set(least).at[tuple(neighbour)].set(largest)


def steps_of(rng, extent, shards, least, high):
    level = 1.0
    for dim, shards_of in shards:
        heights = jax.random.uniform(jax.random.fold_in(jax.random.fold_in(rng, 6), dim), (shards_of,), jnp.float32, least / len(shards), high / len(shards))
        level = level * jnp.repeat(jnp.exp(heights), extent[dim] // shards_of).reshape((-1,) + (1,) * (len(extent) - 1 - dim))
    return level


def gaussian(stream_key, shape, width, most, pieces=(), kind=jnp.bfloat16):
    array = width * jax.random.normal(stream_key, shape, jnp.float32)
    if pieces:
        array = array * steps_of(stream_key, shape, pieces, -0.22, 0.18)
    return jnp.clip(array, -most, most).astype(kind)


def setup_inputs(seed: int = 0) -> dict:
    keys = jax.random.split(jax.random.key(seed), 17)
    return {
        "tokens": draw_tokens(jax.random.fold_in(keys[16], 71), 0),
        "carried": draw_carried(jax.random.fold_in(keys[16], 71), 0),
        "restart": set_ends(jax.random.randint(keys[2], (SEQS,), 0, 2), jax.random.fold_in(keys[2], 1), 0, 1).astype(jnp.int32),
        "lengths": draw_lengths(jax.random.fold_in(keys[16], 71), 0),
        "gain_attend": jnp.clip(1.0 + 0.1 * jax.random.normal(keys[4], (D,), jnp.float32), 0.5, 1.5).astype(jnp.bfloat16),
        "input_weights": draw_input_weights(jax.random.fold_in(keys[16], 71), 0),
        "state_weights": draw_state_weights(jax.random.fold_in(keys[16], 71), 0),
        "update_weights": gaussian(keys[7], (H, HD, HD), (HD // 4) ** -0.5, 1.0, ((0, 2), (1, 16))),
        "gate_bias": jnp.clip(jax.random.uniform(keys[8], (H, HD), jnp.float32, -3.0, 3.0) * steps_of(keys[8], (H, HD), ((0, 2), (1, 16)), -0.4, 0.0), -3.0, 3.0).astype(jnp.bfloat16),
        "initial_state": draw_initial_state(jax.random.fold_in(keys[16], 71), 0),
        "output_weights": gaussian(keys[10], (D, D), (D // BLK) ** -0.5, 4.0, ((0, 2), (1, 16))),
        "gain_feed": jnp.clip(1.0 + 0.1 * jax.random.normal(keys[11], (D,), jnp.float32), 0.5, 1.5).astype(jnp.bfloat16),
        "feed_up": gaussian(keys[12], (D, FF), D ** -0.5, 0.1875, ((0, 16), (1, 2))),
        "feed_down": gaussian(keys[13], (FF, D), FF ** -0.5, 0.09375, ((0, 2), (1, 16))),
        "grad_mixed": gaussian(keys[14], (TOKENS, D), 1.0, 6.0, ((0, 32),)),
        "grad_final": gaussian(keys[15], (SEQS, S, D), 1.0, 6.0, ((0, 16), (2, 2))),
    }


EPSILON = 1e-06
NEGATIVE = -1e+30
HIGHEST = lax.Precision.HIGHEST

@jax.custom_vjp
def low(v):
    return lax.optimization_barrier(v.astype(jnp.bfloat16)).astype(jnp.float32)

@jax.custom_vjp
def low_back(v):
    return v

def low_keep(v):
    return (low(v), None)

def low_pass(kept, grad):
    return (grad,)

def back_keep(v):
    return (v, None)

def back_low(kept, grad):
    return (low(grad),)
low.defvjp(low_keep, low_pass)
low_back.defvjp(back_keep, back_low)

def product(form, left, right):
    return jnp.einsum(form, left, right, precision=HIGHEST)

def rms_scale(values, gain):
    return values * lax.rsqrt(lax.optimization_barrier(jnp.mean(values * values, axis=-1, keepdims=True)) + EPSILON) * gain

def softmax_rows(scores, allowed):
    scores = jnp.where(allowed, scores, NEGATIVE)
    peak_val = lax.optimization_barrier(jnp.max(scores, axis=-1, keepdims=True))
    powers = jnp.exp(scores - peak_val)
    return powers / lax.optimization_barrier(jnp.sum(powers, axis=-1, keepdims=True))

def block_masks(block_id, length, block_len, state_count):
    row_ids = jnp.arange(block_len, dtype=jnp.int32)
    places = block_id.astype(jnp.int32) * block_len + row_ids
    limit = length.astype(jnp.int32)
    key_places = jnp.concatenate([places - block_len, places])
    allowed = (key_places[None, :] >= 0) & (key_places[None, :] < limit) & (key_places[None, :] <= places[:, None]) & (key_places[None, :] > places[:, None] - block_len)
    state_open = jnp.ones((block_len, state_count), dtype=bool)
    allowed = jnp.concatenate([allowed, state_open], axis=1)
    usable = jnp.concatenate([places < limit, jnp.ones((state_count,), dtype=bool)])
    return (allowed, usable)

def block_step(state_weights, update_weights, gate_bias, length, memory, entries):
    queries, keys_now, values_now, keys_before, values_before, block_id = entries
    head_dim = queries.shape[-1]
    block_len = queries.shape[0]
    state_count = memory.shape[0]
    scaling = head_dim ** (-0.5)
    state_proj = low_back(low(product('shd,hde->she', low(memory), state_weights)))
    state_q = state_proj[..., :head_dim]
    state_k = state_proj[..., head_dim:2 * head_dim]
    state_v = state_proj[..., 2 * head_dim:]
    allowed, usable = block_masks(block_id, length, block_len, state_count)
    key_set = jnp.concatenate([keys_before, keys_now], axis=0)
    value_set = jnp.concatenate([values_before, values_now], axis=0)
    scores = jnp.concatenate([product('ihd,jhd->hij', queries, key_set), product('ihd,shd->his', queries, state_k)], axis=2) * scaling
    shares = low(softmax_rows(low_back(scores), allowed[None]))
    outputs = product('hij,jhd->ihd', shares[:, :, :2 * block_len], value_set) + product('his,shd->ihd', shares[:, :, 2 * block_len:], state_v)
    outputs = low_back(low(outputs))
    state_scores = jnp.concatenate([product('shd,jhd->hsj', state_q, keys_now), product('shd,thd->hst', state_q, state_k)], axis=2) * scaling
    state_shares = low(softmax_rows(low_back(state_scores), usable[None, None]))
    state_out = product('hsj,jhd->shd', state_shares[:, :, :block_len], values_now) + product('hst,thd->shd', state_shares[:, :, block_len:], state_v)
    state_out = low_back(low(state_out))
    update = low_back(product('shd,hde->she', state_out, update_weights))
    retain = jax.nn.sigmoid(gate_bias)
    blended = retain * memory + (1.0 - retain) * update
    active = block_id.astype(jnp.int32) * block_len < length.astype(jnp.int32)
    memory_next = jnp.where(active, blended, memory).astype(memory.dtype)
    return (memory_next, outputs)

def sequence(weight_set, tokens_seq, carried_seq, restart_flag, length):
    gain_attend, input_weights, state_weights, update_weights, gate_bias, initial_state, output_weights, gain_feed, feed_up, feed_down = weight_set
    normed = low(rms_scale(tokens_seq, gain_attend))
    projected = low_back(low(product('rd,kdc->krc', normed, input_weights)))
    blocked = projected.reshape(3, NB, BLK, H, HD)
    earlier = jnp.concatenate([jnp.zeros((3, 1, BLK, H, HD), blocked.dtype), blocked[:, :-1]], axis=1)
    memory = jnp.where(restart_flag > 0, initial_state, carried_seq).astype(carried_seq.dtype).reshape(S, H, HD)
    stepper = jax.checkpoint(partial(block_step, state_weights, update_weights, gate_bias, length))
    memory, outputs = lax.scan(stepper, memory, (blocked[0], blocked[1], blocked[2], earlier[1], earlier[2], jnp.arange(NB, dtype=jnp.int32)))
    attended = outputs.reshape(LEN, H * HD)
    branch = low_back(product('rc,cd->rd', attended, output_weights))
    middle = tokens_seq + branch
    normed_mid = low(rms_scale(middle, gain_feed))
    hidden_pre = low_back(product('rd,df->rf', normed_mid, feed_up))
    hidden = low(jax.nn.gelu(hidden_pre))
    feed = low_back(product('rf,fd->rd', hidden, feed_down))
    return (middle + feed, memory.reshape(S, H * HD))

def reference(tokens, carried, restart, lengths, gain_attend, input_weights, state_weights, update_weights, gate_bias, initial_state, output_weights, gain_feed, feed_up, feed_down, grad_mixed, grad_final):
    weight_set = tuple((member.astype(jnp.float32) for member in (gain_attend, input_weights, state_weights, update_weights, gate_bias, initial_state, output_weights, gain_feed, feed_up, feed_down)))
    restart_ids = restart.astype(jnp.int32)
    length_ids = lengths.astype(jnp.int32)

    def forward(weights_now, token_rows, carried_all):

        def one_sequence(entries):
            tokens_seq, carried_seq, restart_flag, length = entries
            return jax.checkpoint(partial(sequence, weights_now))(tokens_seq, carried_seq, restart_flag, length)
        mixed_rows, memory = lax.map(one_sequence, (token_rows.reshape(SEQS, LEN, D), carried_all, restart_ids, length_ids))
        return (mixed_rows.reshape(TOKENS, D), memory)
    (mixed, memory), pullback = jax.vjp(forward, weight_set, tokens.astype(jnp.float32), carried.astype(jnp.float32))
    gradients, grad_tokens, grad_carried = pullback((grad_mixed.astype(jnp.float32), grad_final.astype(jnp.float32)))
    return (mixed.astype(jnp.bfloat16), memory, grad_tokens, grad_carried, gradients[0], gradients[1], gradients[2], gradients[3], gradients[4], gradients[5], gradients[6], gradients[7], gradients[8], gradients[9])
```

```python
import functools
import math

import jax
import jax.numpy as jnp
from jax import lax
from jax.experimental import pallas as pl
from jax.experimental.pallas import tpu as pltpu
from jax.sharding import PartitionSpec as P

S = 512
BLK = 512
LEN = 1536
NB = 3


EPSILON = 1e-06
NEGATIVE = -1e30


def rms_scale(values, gain):
    return values * lax.rsqrt(jnp.mean(values * values, axis=-1, keepdims=True) + EPSILON) * gain


def block_masks(block_id, length, block_len, state_count):
    row_ids = jnp.arange(block_len, dtype=jnp.int32)
    places = block_id * block_len + row_ids
    key_places = jnp.concatenate([places - block_len, places])
    allowed = (
        (key_places[None, :] >= 0)
        & (key_places[None, :] < length)
        & (key_places[None, :] <= places[:, None])
        & (key_places[None, :] > places[:, None] - block_len)
    )
    state_open = jnp.ones((block_len, state_count), dtype=bool)
    allowed = jnp.concatenate([allowed, state_open], axis=1)
    usable = jnp.concatenate([places < length, jnp.ones((state_count,), dtype=bool)])
    return (allowed, usable)


def masked_softmax(scores, allowed):
    scores = jnp.where(allowed, scores, NEGATIVE)
    peak_val = jnp.max(scores, axis=-1, keepdims=True)
    powers = jnp.exp(scores - peak_val)
    totals = jnp.sum(powers, axis=-1, keepdims=True)
    return (powers / totals, peak_val + jnp.log(totals))


def recall_softmax(scores, allowed, log_total):
    return jnp.exp(jnp.where(allowed, scores, NEGATIVE) - log_total)


def state_project(memory, state_weights):
    head_dim = memory.shape[-1]
    projected = jnp.einsum(
        "shd,hde->she",
        memory.astype(jnp.bfloat16),
        state_weights,
        preferred_element_type=jnp.float32,
    ).astype(jnp.bfloat16)
    return (
        projected[..., :head_dim],
        projected[..., head_dim : 2 * head_dim],
        projected[..., 2 * head_dim :],
    )


def block_forward(
    state_weights,
    update_weights,
    retain,
    memory,
    queries,
    keys_now,
    values_now,
    keys_before,
    values_before,
    block_id,
    length,
):
    head_dim = queries.shape[-1]
    block_len = queries.shape[0]
    state_count = memory.shape[0]
    scaling = head_dim ** (-0.5)
    state_q, state_k, state_v = state_project(memory, state_weights)
    allowed, usable = block_masks(block_id, length, block_len, state_count)
    key_set = jnp.concatenate([keys_before, keys_now, state_k], axis=0)
    value_set = jnp.concatenate([values_before, values_now, state_v], axis=0)
    scores = (
        jnp.einsum("ihd,jhd->hij", queries, key_set, preferred_element_type=jnp.float32) * scaling
    )
    shares, log_total = masked_softmax(scores, allowed[None])
    outputs = jnp.einsum(
        "hij,jhd->ihd", shares.astype(jnp.bfloat16), value_set, preferred_element_type=jnp.float32
    ).astype(jnp.bfloat16)
    state_keys = jnp.concatenate([keys_now, state_k], axis=0)
    state_values = jnp.concatenate([values_now, state_v], axis=0)
    state_scores = (
        jnp.einsum("shd,jhd->hsj", state_q, state_keys, preferred_element_type=jnp.float32)
        * scaling
    )
    state_shares, state_log = masked_softmax(state_scores, usable[None, None])
    state_out = jnp.einsum(
        "hsj,jhd->shd",
        state_shares.astype(jnp.bfloat16),
        state_values,
        preferred_element_type=jnp.float32,
    ).astype(jnp.bfloat16)
    update = jnp.einsum(
        "shd,hde->she", state_out, update_weights, preferred_element_type=jnp.float32
    )
    blended = retain * memory + (1.0 - retain) * update
    active = block_id * block_len < length
    memory_next = jnp.where(active, blended, memory)
    return (memory_next, (outputs, state_out, log_total, state_log))


def block_backward(
    state_weights,
    update_weights,
    retain,
    memory,
    queries,
    keys_now,
    values_now,
    keys_before,
    values_before,
    grad_out,
    state_out,
    log_total,
    state_log,
    block_id,
    length,
    grad_next,
):
    head_dim = queries.shape[-1]
    block_len = queries.shape[0]
    state_count = memory.shape[0]
    scaling = head_dim ** (-0.5)
    span_end = 2 * block_len
    state_q, state_k, state_v = state_project(memory, state_weights)
    allowed, usable = block_masks(block_id, length, block_len, state_count)
    active = block_id * block_len < length
    update = jnp.einsum(
        "shd,hde->she", state_out, update_weights, preferred_element_type=jnp.float32
    )
    grad_blend = jnp.where(active, grad_next, 0.0)
    grad_memory = jnp.where(active, retain * grad_next, grad_next)
    grad_update = ((1.0 - retain) * grad_blend).astype(jnp.bfloat16)
    grad_gate = jnp.sum(grad_blend * (memory - update), axis=0) * retain * (1.0 - retain)
    grad_update_w = jnp.einsum(
        "shd,she->hde", state_out, grad_update, preferred_element_type=jnp.float32
    )
    grad_state_out = jnp.einsum(
        "she,hde->shd", grad_update, update_weights, preferred_element_type=jnp.float32
    ).astype(jnp.bfloat16)
    state_keys = jnp.concatenate([keys_now, state_k], axis=0)
    state_values = jnp.concatenate([values_now, state_v], axis=0)
    state_scores = (
        jnp.einsum("shd,jhd->hsj", state_q, state_keys, preferred_element_type=jnp.float32)
        * scaling
    )
    state_shares = recall_softmax(state_scores, usable[None, None], state_log)
    grad_state_shares = jnp.einsum(
        "shd,jhd->hsj", grad_state_out, state_values, preferred_element_type=jnp.float32
    )
    grad_state_scores = (
        state_shares
        * (grad_state_shares - jnp.sum(state_shares * grad_state_shares, axis=-1, keepdims=True))
    ).astype(jnp.bfloat16)
    grad_state_values = jnp.einsum(
        "hsj,shd->jhd",
        state_shares.astype(jnp.bfloat16),
        grad_state_out,
        preferred_element_type=jnp.float32,
    )
    grad_state_q = (
        jnp.einsum(
            "hsj,jhd->shd", grad_state_scores, state_keys, preferred_element_type=jnp.float32
        )
        * scaling
    )
    grad_state_keys = (
        jnp.einsum("hsj,shd->jhd", grad_state_scores, state_q, preferred_element_type=jnp.float32)
        * scaling
    )
    key_set = jnp.concatenate([keys_before, keys_now, state_k], axis=0)
    value_set = jnp.concatenate([values_before, values_now, state_v], axis=0)
    scores = (
        jnp.einsum("ihd,jhd->hij", queries, key_set, preferred_element_type=jnp.float32) * scaling
    )
    shares = recall_softmax(scores, allowed[None], log_total)
    grad_shares = jnp.einsum(
        "ihd,jhd->hij", grad_out, value_set, preferred_element_type=jnp.float32
    )
    grad_scores = (
        shares * (grad_shares - jnp.sum(shares * grad_shares, axis=-1, keepdims=True))
    ).astype(jnp.bfloat16)
    grad_values = jnp.einsum(
        "hij,ihd->jhd", shares.astype(jnp.bfloat16), grad_out, preferred_element_type=jnp.float32
    )
    grad_queries = (
        jnp.einsum("hij,jhd->ihd", grad_scores, key_set, preferred_element_type=jnp.float32)
        * scaling
    )
    grad_keys = (
        jnp.einsum("hij,ihd->jhd", grad_scores, queries, preferred_element_type=jnp.float32)
        * scaling
    )
    grad_keys_now = grad_keys[block_len:span_end] + grad_state_keys[:block_len]
    grad_values_now = grad_values[block_len:span_end] + grad_state_values[:block_len]
    grad_state_k = grad_keys[span_end:] + grad_state_keys[block_len:]
    grad_state_v = grad_values[span_end:] + grad_state_values[block_len:]
    grad_proj = jnp.concatenate([grad_state_q, grad_state_k, grad_state_v], axis=-1).astype(
        jnp.bfloat16
    )
    grad_memory = grad_memory + jnp.einsum(
        "she,hde->shd", grad_proj, state_weights, preferred_element_type=jnp.float32
    )
    grad_state_w = jnp.einsum(
        "shd,she->hde", memory.astype(jnp.bfloat16), grad_proj, preferred_element_type=jnp.float32
    )
    return (
        grad_memory,
        grad_queries,
        grad_keys_now,
        grad_values_now,
        grad_keys[:block_len],
        grad_values[:block_len],
        grad_state_w,
        grad_update_w,
        grad_gate,
    )


def general_body(
    tokens,
    carried,
    restart,
    lengths,
    gain_attend,
    input_weights,
    state_weights,
    update_weights,
    gate_bias,
    initial_state,
    output_weights,
    gain_feed,
    feed_up,
    feed_down,
    grad_mixed,
    grad_final,
):
    seq_count = lengths.shape[0]
    heads_here = gate_bias.shape[0]
    head_dim = update_weights.shape[-1]
    width_here = heads_here * head_dim
    group_rows = seq_count * LEN
    gathered = (
        lax.all_gather(gain_attend, "dp", axis=0, tiled=True),
        lax.all_gather(gain_feed, "dp", axis=0, tiled=True),
        lax.all_gather(input_weights, "dp", axis=1, tiled=True),
        lax.all_gather(output_weights, "dp", axis=1, tiled=True),
        lax.all_gather(state_weights, "dp", axis=1, tiled=True),
        lax.all_gather(update_weights, "dp", axis=1, tiled=True),
        lax.all_gather(gate_bias, "dp", axis=1, tiled=True),
        lax.all_gather(initial_state, "dp", axis=0, tiled=True),
        lax.all_gather(feed_up, "dp", axis=0, tiled=True),
        lax.all_gather(feed_down, "dp", axis=1, tiled=True),
    )
    (
        gain_attend_all,
        gain_feed_all,
        input_all,
        output_all,
        state_all,
        update_all,
        gate_all,
        initial_all,
        up_all,
        down_all,
    ) = gathered
    tokens_wide = tokens.astype(jnp.float32)
    gain_one = gain_attend_all.astype(jnp.float32)
    gain_two = gain_feed_all.astype(jnp.float32)
    normed = rms_scale(tokens_wide, gain_one).astype(jnp.bfloat16)
    normed_all = lax.all_gather(normed, "tp", axis=0, tiled=True)
    projected = jnp.einsum(
        "rd,kdc->krc", normed_all, input_all, preferred_element_type=jnp.float32
    ).astype(jnp.bfloat16)
    blocked = jnp.moveaxis(projected.reshape(3, seq_count, NB, BLK, heads_here, head_dim), 2, 1)
    earlier = jnp.concatenate([jnp.zeros_like(blocked[:, :1]), blocked[:, :-1]], axis=1)
    retain = jax.nn.sigmoid(gate_all.astype(jnp.float32))
    memory_start = jnp.where(
        restart[:, None, None] > 0, initial_all.astype(jnp.float32)[None], carried
    ).reshape(seq_count, S, heads_here, head_dim)
    forward_block = jax.vmap(block_forward, in_axes=(None, None, None, 0, 0, 0, 0, 0, 0, None, 0))
    block_ids = jnp.arange(NB, dtype=jnp.int32)

    def forward_step(memory, entries):
        queries, keys_now, values_now, keys_before, values_before, block_id = entries
        memory_next, saved = forward_block(
            state_all,
            update_all,
            retain,
            memory,
            queries,
            keys_now,
            values_now,
            keys_before,
            values_before,
            block_id,
            lengths,
        )
        return (memory_next, (memory, saved))

    memory_end, (memories, saved_all) = lax.scan(
        forward_step,
        memory_start,
        (blocked[0], blocked[1], blocked[2], earlier[1], earlier[2], block_ids),
    )
    outputs, state_outs, log_totals, state_logs = saved_all
    attended = jnp.moveaxis(outputs, 0, 1).reshape(group_rows, width_here)
    middle = tokens_wide + lax.psum_scatter(
        jnp.dot(attended, output_all, preferred_element_type=jnp.float32),
        "tp",
        scatter_dimension=0,
        tiled=True,
    )
    normed_mid = rms_scale(middle, gain_two).astype(jnp.bfloat16)
    mid_all = lax.all_gather(normed_mid, "tp", axis=0, tiled=True)
    hidden_pre = jnp.dot(mid_all, up_all, preferred_element_type=jnp.float32)
    hidden = jax.nn.gelu(hidden_pre).astype(jnp.bfloat16)
    mixed = middle + lax.psum_scatter(
        jnp.dot(hidden, down_all, preferred_element_type=jnp.float32),
        "tp",
        scatter_dimension=0,
        tiled=True,
    )
    grad_rows = lax.all_gather(grad_mixed, "tp", axis=0, tiled=True)
    grad_hidden = jnp.einsum("rd,fd->rf", grad_rows, down_all, preferred_element_type=jnp.float32)
    grad_pre = jax.vjp(jax.nn.gelu, hidden_pre)[1](grad_hidden)[0].astype(jnp.bfloat16)
    grad_down = jnp.einsum("rf,rd->fd", hidden, grad_rows, preferred_element_type=jnp.float32)
    grad_up = jnp.einsum("rd,rf->df", mid_all, grad_pre, preferred_element_type=jnp.float32)
    grad_mid_normed = lax.psum_scatter(
        jnp.einsum("rf,df->rd", grad_pre, up_all, preferred_element_type=jnp.float32),
        "tp",
        scatter_dimension=0,
        tiled=True,
    )
    grad_middle_part, grad_gain_two = jax.vjp(rms_scale, middle, gain_two)[1](grad_mid_normed)
    grad_middle = grad_mixed.astype(jnp.float32) + grad_middle_part
    grad_branch = lax.all_gather(grad_middle.astype(jnp.bfloat16), "tp", axis=0, tiled=True)
    grad_output = jnp.einsum("rc,rd->cd", attended, grad_branch, preferred_element_type=jnp.float32)
    grad_attended = jnp.einsum(
        "rd,cd->rc", grad_branch, output_all, preferred_element_type=jnp.float32
    ).astype(jnp.bfloat16)
    grad_blocks = jnp.moveaxis(
        grad_attended.reshape(seq_count, NB, BLK, heads_here, head_dim), 1, 0
    )
    backward_block = jax.vmap(
        block_backward, in_axes=(None, None, None, 0, 0, 0, 0, 0, 0, 0, 0, 0, 0, None, 0, 0)
    )

    def backward_step(carried_in, entries):
        grad_memory, keys_later, values_later, sum_state, sum_update, sum_gate = carried_in
        (
            memory,
            queries,
            keys_now,
            values_now,
            keys_before,
            values_before,
            grad_out,
            state_out,
            log_total,
            state_log,
            block_id,
        ) = entries
        results = backward_block(
            state_all,
            update_all,
            retain,
            memory,
            queries,
            keys_now,
            values_now,
            keys_before,
            values_before,
            grad_out,
            state_out,
            log_total,
            state_log,
            block_id,
            lengths,
            grad_memory,
        )
        (
            grad_prior,
            grad_queries,
            grad_keys,
            grad_values,
            grad_keys_before,
            grad_values_before,
            part_state,
            part_update,
            part_gate,
        ) = results
        carried_out = (
            grad_prior,
            grad_keys_before,
            grad_values_before,
            sum_state + jnp.sum(part_state, axis=0),
            sum_update + jnp.sum(part_update, axis=0),
            sum_gate + jnp.sum(part_gate, axis=0),
        )
        return (carried_out, (grad_queries, grad_keys + keys_later, grad_values + values_later))

    zero_block = jnp.zeros((seq_count, BLK, heads_here, head_dim), jnp.float32)
    start_carry = (
        grad_final.astype(jnp.float32).reshape(seq_count, S, heads_here, head_dim),
        zero_block,
        zero_block,
        jnp.zeros(state_all.shape, jnp.float32),
        jnp.zeros(update_all.shape, jnp.float32),
        jnp.zeros(retain.shape, jnp.float32),
    )
    final_carry, grad_parts = lax.scan(
        backward_step,
        start_carry,
        (
            memories,
            blocked[0],
            blocked[1],
            blocked[2],
            earlier[1],
            earlier[2],
            grad_blocks,
            state_outs,
            log_totals,
            state_logs,
            block_ids,
        ),
        reverse=True,
    )
    grad_memory_start, unused_keys, unused_values, grad_state_w, grad_update_w, grad_gate_w = (
        final_carry
    )
    grad_qkv = jnp.stack(
        [jnp.moveaxis(member, 0, 1).reshape(group_rows, width_here) for member in grad_parts]
    ).astype(jnp.bfloat16)
    grad_memory_start = grad_memory_start.reshape(seq_count, S, width_here)
    restarted = restart[:, None, None] > 0
    grad_carried = jnp.where(restarted, 0.0, grad_memory_start)
    grad_initial = jnp.sum(jnp.where(restarted, grad_memory_start, 0.0), axis=0)
    grad_input = jnp.einsum("rd,krc->kdc", normed_all, grad_qkv, preferred_element_type=jnp.float32)
    grad_normed = lax.psum_scatter(
        jnp.einsum("krc,kdc->rd", grad_qkv, input_all, preferred_element_type=jnp.float32),
        "tp",
        scatter_dimension=0,
        tiled=True,
    )
    grad_tokens_part, grad_gain_one = jax.vjp(rms_scale, tokens_wide, gain_one)[1](grad_normed)
    grad_tokens = grad_middle + grad_tokens_part
    gain_one_sum, gain_two_sum = lax.psum((grad_gain_one, grad_gain_two), "tp")
    summed = (
        lax.psum_scatter(gain_one_sum, "dp", scatter_dimension=0, tiled=True),
        lax.psum_scatter(gain_two_sum, "dp", scatter_dimension=0, tiled=True),
        lax.psum_scatter(grad_input, "dp", scatter_dimension=1, tiled=True),
        lax.psum_scatter(grad_output, "dp", scatter_dimension=1, tiled=True),
        lax.psum_scatter(grad_state_w, "dp", scatter_dimension=1, tiled=True),
        lax.psum_scatter(grad_update_w, "dp", scatter_dimension=1, tiled=True),
        lax.psum_scatter(grad_gate_w, "dp", scatter_dimension=1, tiled=True),
        lax.psum_scatter(grad_initial, "dp", scatter_dimension=0, tiled=True),
        lax.psum_scatter(grad_up, "dp", scatter_dimension=0, tiled=True),
        lax.psum_scatter(grad_down, "dp", scatter_dimension=1, tiled=True),
    )
    (
        out_gain_one,
        out_gain_two,
        out_input,
        out_output,
        out_state,
        out_update,
        out_gate,
        out_initial,
        out_up,
        out_down,
    ) = summed
    return (
        mixed.astype(jnp.bfloat16),
        memory_end.reshape(seq_count, S, width_here),
        grad_tokens,
        grad_carried,
        out_gain_one,
        out_input,
        out_state,
        out_update,
        out_gate,
        out_initial,
        out_output,
        out_gain_two,
        out_up,
        out_down,
    )


BF16 = jnp.bfloat16
F32 = jnp.float32
HD = 128
TILE = 256
LOG2E = math.log2(math.e)
SCALING = HD ** (-0.5)
TO_POWER = SCALING * LOG2E
VMEM_BYTES = 60 * 1024 * 1024


def dot_nn(left, right):
    return jnp.dot(left, right, preferred_element_type=F32)


def dot_nt(left, right):
    return lax.dot_general(left, right, (((1,), (1,)), ((), ())), preferred_element_type=F32)


def call_params(**more):
    return pltpu.CompilerParams(vmem_limit_bytes=VMEM_BYTES, **more)


def cost(macs, moved, powers=0):
    return pl.CostEstimate(flops=2 * macs, bytes_accessed=moved, transcendentals=powers)


def whole(shape):
    return pl.BlockSpec(shape, lambda *_: (0,) * len(shape), pipeline_mode=pl.Buffered(1))


def natural_rows(ref, place, lead):
    return jnp.concatenate([ref[(p, s) + lead] for p in place for s in range(2)], axis=0)


def project_kernel(place, x_ref, gain_ref, w_ref, normed_t_ref, out_ref, w_full):
    depth = w_ref.shape[2] // 3

    @pl.when(pl.program_id(0) == 0)
    def _():
        for i in range(3):
            w_full[i] = natural_rows(w_ref, place, (slice(i * depth, (i + 1) * depth),))

    x = x_ref[...].astype(F32)
    scale = lax.rsqrt(jnp.mean(x * x, axis=-1, keepdims=True) + EPSILON)
    normed = (x * scale * gain_ref[...]).astype(BF16)
    normed_t_ref[...] = normed.T
    for i in range(3):
        out_ref[i] = dot_nn(normed, w_full[i]).astype(BF16)


def project(place, x, gain, packs, depth):
    rows, width = x.shape
    cols = packs.shape[3]
    return pl.pallas_call(
        functools.partial(project_kernel, place),
        grid=(rows // TILE,),
        in_specs=[
            pl.BlockSpec((TILE, width), lambda r: (r, 0)),
            whole((1, width)),
            whole(packs.shape[:2] + (3 * depth, cols)),
        ],
        out_specs=[
            pl.BlockSpec((width, TILE), lambda r: (0, r)),
            pl.BlockSpec((3, TILE, cols), lambda r: (0, r, 0)),
        ],
        out_shape=[
            jax.ShapeDtypeStruct((width, rows), BF16),
            jax.ShapeDtypeStruct((3, rows, cols), BF16),
        ],
        scratch_shapes=[pltpu.VMEM((3, width, cols), BF16)],
        compiler_params=call_params(),
        cost_estimate=cost(rows * width * 3 * cols, 6 * rows * width),
        name="project",
    )(x, gain, packs)


def tile_masks():
    key = lax.broadcasted_iota(jnp.int32, (TILE, TILE), 0)
    query = lax.broadcasted_iota(jnp.int32, (TILE, TILE), 1)
    return key, query


def token_tiles(t):
    return [(j, t - j) for j in range(max(0, t - 2), t + 1)]


def masked_scores(scores, tile, behind, length, key, query):
    if behind == 0:
        scores = jnp.where(key <= query, scores, NEGATIVE)
    elif behind == 2:
        scores = jnp.where(key > query, scores, NEGATIVE)
    if tile >= 2 * (NB - 1):
        scores = jnp.where(key + tile * TILE < length, scores, NEGATIVE)
    return scores


def softmax_columns(tiles):
    peak = functools.reduce(jnp.maximum, [jnp.max(s, axis=0, keepdims=True) for s in tiles])
    peak = peak * TO_POWER
    powers = [jnp.exp2(s * TO_POWER - peak) for s in tiles]
    total = functools.reduce(jnp.add, [jnp.sum(p, axis=0, keepdims=True) for p in powers])
    return [p.astype(BF16) for p in powers], total, peak + jnp.log2(total)


def attend_kernel(
    length_ref,
    q_ref,
    k_ref,
    v_ref,
    memory_ref,
    ws_ref,
    wu_ref,
    gate_ref,
    out_ref,
    state_out_ref,
    log_ref,
    state_log_ref,
    final_ref,
    vt_ref,
):
    length = length_ref[0]
    key, query = tile_masks()
    retain = jax.nn.sigmoid(gate_ref[0])
    memory = memory_ref[...]
    vt_ref[...] = v_ref[0].T
    for c in range(NB):
        lo = c * BLK
        state = dot_nn(memory.astype(BF16), ws_ref[0]).astype(BF16)
        sq, sk, sv = state[:, :HD], state[:, HD : 2 * HD], state[:, 2 * HD :]
        svt = sv.T
        for t in range(2 * c, 2 * c + 2):
            rows = slice(t * TILE, (t + 1) * TILE)
            q = q_ref[0, rows]
            spans = token_tiles(t)
            tiles = [
                masked_scores(
                    dot_nt(k_ref[0, j * TILE : (j + 1) * TILE], q), j, behind, length, key, query
                )
                for j, behind in spans
            ]
            tiles.append(dot_nt(sk, q))
            powers, total, logs = softmax_columns(tiles)
            first = spans[0][0] * TILE
            out = dot_nn(vt_ref[:, first : (t + 1) * TILE], jnp.concatenate(powers[:-1], axis=0))
            out = out + dot_nn(svt, powers[-1])
            out_ref[rows] = (out / total).T.astype(BF16)
            log_ref[0, :, rows] = logs
        for u in range(2):
            part = slice(u * TILE, (u + 1) * TILE)
            q = sq[part]
            tiles = []
            for j in range(2):
                s = dot_nt(k_ref[0, lo + j * TILE : lo + (j + 1) * TILE], q)
                if c == NB - 1:
                    s = jnp.where(key + (lo + j * TILE) < length, s, NEGATIVE)
                tiles.append(s)
            tiles.append(dot_nt(sk, q))
            powers, total, logs = softmax_columns(tiles)
            out = dot_nn(vt_ref[:, lo : lo + BLK], jnp.concatenate(powers[:-1], axis=0))
            out = out + dot_nn(svt, powers[-1])
            rows = slice(lo + u * TILE, lo + (u + 1) * TILE)
            state_out_ref[rows] = (out / total).T.astype(BF16)
            state_log_ref[0, :, rows] = logs
        update = dot_nn(state_out_ref[lo : lo + BLK], wu_ref[0])
        blended = retain * memory + (1.0 - retain) * update
        memory = jnp.where(lo < length, blended, memory)
    final_ref[...] = memory


def head_block(rows):
    return pl.BlockSpec((rows, HD), lambda h: (0, h))


def attend(length, projected, memory, ws, wu, gate):
    rows = projected.shape[1]
    heads = ws.shape[0]
    return pl.pallas_call(
        attend_kernel,
        grid=(heads,),
        in_specs=[
            pl.BlockSpec(memory_space=pltpu.SMEM),
            pl.BlockSpec((1, rows, HD), lambda h: (0, 0, h)),
            pl.BlockSpec((1, rows, HD), lambda h: (1, 0, h)),
            pl.BlockSpec((1, rows, HD), lambda h: (2, 0, h)),
            head_block(S),
            pl.BlockSpec((1, HD, 3 * HD), lambda h: (h, 0, 0)),
            pl.BlockSpec((1, HD, HD), lambda h: (h, 0, 0)),
            pl.BlockSpec((1, 1, HD), lambda h: (h, 0, 0)),
        ],
        out_specs=[
            head_block(rows),
            head_block(NB * S),
            pl.BlockSpec((1, 1, rows), lambda h: (h, 0, 0)),
            pl.BlockSpec((1, 1, NB * S), lambda h: (h, 0, 0)),
            head_block(S),
        ],
        out_shape=[
            jax.ShapeDtypeStruct((rows, heads * HD), BF16),
            jax.ShapeDtypeStruct((NB * S, heads * HD), BF16),
            jax.ShapeDtypeStruct((heads, 1, rows), F32),
            jax.ShapeDtypeStruct((heads, 1, NB * S), F32),
            jax.ShapeDtypeStruct((S, heads * HD), F32),
        ],
        scratch_shapes=[pltpu.VMEM((HD, rows), BF16)],
        compiler_params=call_params(),
        cost_estimate=cost(
            heads * NB * BLK * HD * 2 * (1152 + 1024),
            heads * HD * (rows * 10 + S * 8),
            heads * NB * BLK * 2176,
        ),
        name="attend",
    )(length, projected, projected, projected, memory, ws, wu, gate)


def attend_back_kernel(
    length_ref,
    q_ref,
    k_ref,
    v_ref,
    memory_ref,
    ws_ref,
    wu_ref,
    gate_ref,
    out_ref,
    state_out_ref,
    log_ref,
    state_log_ref,
    go_ref,
    grad_final_ref,
    dqkv_ref,
    dws_ref,
    dwu_ref,
    dgate_ref,
    dmemory_ref,
    kt_ref,
    dk_ref,
    dv_ref,
):
    length = length_ref[0]
    key, query = tile_masks()
    retain = jax.nn.sigmoid(gate_ref[0])
    ws = ws_ref[0]
    wu = wu_ref[0]
    kt_ref[...] = k_ref[0].T
    dk_ref[...] = jnp.zeros_like(dk_ref)
    dv_ref[...] = jnp.zeros_like(dv_ref)
    memories = [memory_ref[...]]
    for c in range(NB - 1):
        update = dot_nn(state_out_ref[c * S : (c + 1) * S], wu)
        blended = retain * memories[c] + (1.0 - retain) * update
        memories.append(jnp.where(c * BLK < length, blended, memories[c]))
    grad_memory = grad_final_ref[...].astype(F32)
    dws = jnp.zeros(ws.shape, F32)
    dwu = jnp.zeros(wu.shape, F32)
    dgate = jnp.zeros(retain.shape, F32)
    for c in reversed(range(NB)):
        lo = c * BLK
        active = lo < length
        memory = memories[c]
        memory_low = memory.astype(BF16)
        state = dot_nn(memory_low, ws).astype(BF16)
        sq, sk, sv = state[:, :HD], state[:, HD : 2 * HD], state[:, 2 * HD :]
        skt = sk.T
        state_out = state_out_ref[lo : lo + S]
        update = dot_nn(state_out, wu)
        grad_blend = jnp.where(active, grad_memory, 0.0)
        grad_update = ((1.0 - retain) * grad_blend).astype(BF16)
        dgate = dgate + jnp.sum(grad_blend * (memory - update), axis=0, keepdims=True)
        dwu = dwu + dot_nn(state_out.T, grad_update)
        grad_state_out = dot_nt(grad_update, wu).astype(BF16)
        grad_memory = jnp.where(active, retain * grad_memory, grad_memory)
        deltas = jnp.sum((grad_state_out.astype(F32) * state_out.astype(F32)).T, axis=0, keepdims=True)
        dsk = jnp.zeros((S, HD), F32)
        dsv = jnp.zeros((S, HD), F32)
        dsq = []
        for u in range(2):
            part = slice(u * TILE, (u + 1) * TILE)
            q = sq[part]
            go = grad_state_out[part]
            logs = state_log_ref[0, :, lo + u * TILE : lo + (u + 1) * TILE]
            delta = deltas[:, part]
            dq = jnp.zeros((HD, TILE), F32)
            for j in range(2):
                rows = slice(lo + j * TILE, lo + (j + 1) * TILE)
                s = dot_nt(k_ref[0, rows], q)
                if c == NB - 1:
                    s = jnp.where(key + (lo + j * TILE) < length, s, NEGATIVE)
                p = jnp.exp2(s * TO_POWER - logs)
                ds = (p * (dot_nt(v_ref[0, rows], go) - delta)).astype(BF16)
                dv_ref[rows] += dot_nn(p.astype(BF16), go)
                dk_ref[rows] += dot_nn(ds, q)
                dq = dq + dot_nn(kt_ref[:, rows], ds)
            p = jnp.exp2(dot_nt(sk, q) * TO_POWER - logs)
            ds = (p * (dot_nt(sv, go) - delta)).astype(BF16)
            dsv = dsv + dot_nn(p.astype(BF16), go)
            dsk = dsk + dot_nn(ds, q)
            dq = dq + dot_nn(skt, ds)
            dsq.append(dq.T)
        for t in range(2 * c, 2 * c + 2):
            here = slice(t * TILE, (t + 1) * TILE)
            q = q_ref[0, here]
            go = go_ref[here]
            logs = log_ref[0, :, here]
            delta = jnp.sum((go.astype(F32) * out_ref[here].astype(F32)).T, axis=0, keepdims=True)
            dq = jnp.zeros((HD, TILE), F32)
            for j, behind in token_tiles(t):
                rows = slice(j * TILE, (j + 1) * TILE)
                s = masked_scores(dot_nt(k_ref[0, rows], q), j, behind, length, key, query)
                p = jnp.exp2(s * TO_POWER - logs)
                ds = (p * (dot_nt(v_ref[0, rows], go) - delta)).astype(BF16)
                dv_ref[rows] += dot_nn(p.astype(BF16), go)
                dk_ref[rows] += dot_nn(ds, q)
                dq = dq + dot_nn(kt_ref[:, rows], ds)
            p = jnp.exp2(dot_nt(sk, q) * TO_POWER - logs)
            ds = (p * (dot_nt(sv, go) - delta)).astype(BF16)
            dsv = dsv + dot_nn(p.astype(BF16), go)
            dsk = dsk + dot_nn(ds, q)
            dq = dq + dot_nn(skt, ds)
            dqkv_ref[0, here] = (dq.T * SCALING).astype(BF16)
        grad_state = jnp.concatenate(
            [jnp.concatenate(dsq, axis=0) * SCALING, dsk * SCALING, dsv], axis=1
        ).astype(BF16)
        grad_memory = grad_memory + dot_nt(grad_state, ws)
        dws = dws + dot_nn(memory_low.T, grad_state)
    dqkv_ref[1] = (dk_ref[...] * SCALING).astype(BF16)
    dqkv_ref[2] = dv_ref[...].astype(BF16)
    dws_ref[0] = dws
    dwu_ref[0] = dwu
    dgate_ref[0] = dgate * retain * (1.0 - retain)
    dmemory_ref[...] = grad_memory


def attend_back(
    length, projected, memory, ws, wu, gate, out, state_out, logs, state_logs, go, grad_final
):
    rows = projected.shape[1]
    heads = ws.shape[0]
    per_head = lambda a, b: pl.BlockSpec((1, a, b), lambda h: (h, 0, 0))
    return pl.pallas_call(
        attend_back_kernel,
        grid=(heads,),
        in_specs=[
            pl.BlockSpec(memory_space=pltpu.SMEM),
            pl.BlockSpec((1, rows, HD), lambda h: (0, 0, h)),
            pl.BlockSpec((1, rows, HD), lambda h: (1, 0, h)),
            pl.BlockSpec((1, rows, HD), lambda h: (2, 0, h)),
            head_block(S),
            per_head(HD, 3 * HD),
            per_head(HD, HD),
            per_head(1, HD),
            head_block(rows),
            head_block(NB * S),
            per_head(1, rows),
            per_head(1, NB * S),
            head_block(rows),
            head_block(S),
        ],
        out_specs=[
            pl.BlockSpec((3, rows, HD), lambda h: (0, 0, h)),
            per_head(HD, 3 * HD),
            per_head(HD, HD),
            per_head(1, HD),
            head_block(S),
        ],
        out_shape=[
            jax.ShapeDtypeStruct((3, rows, heads * HD), BF16),
            jax.ShapeDtypeStruct((heads, HD, 3 * HD), F32),
            jax.ShapeDtypeStruct((heads, HD, HD), F32),
            jax.ShapeDtypeStruct((heads, 1, HD), F32),
            jax.ShapeDtypeStruct((S, heads * HD), F32),
        ],
        scratch_shapes=[
            pltpu.VMEM((HD, rows), BF16),
            pltpu.VMEM((rows, HD), F32),
            pltpu.VMEM((rows, HD), F32),
        ],
        compiler_params=call_params(),
        cost_estimate=cost(
            heads * NB * BLK * HD * 5 * (1152 + 1024),
            heads * HD * (rows * 20 + S * 16),
            heads * NB * BLK * 2176,
        ),
        name="attend_back",
    )(
        length,
        projected,
        projected,
        projected,
        memory,
        ws,
        wu,
        gate,
        out,
        state_out,
        logs,
        state_logs,
        go,
        grad_final,
    )


def middle_kernel(x_ref, own_ref, sib_ref, wo_own_ref, wo_sib_ref, gain_ref, mid_ref, n_ref, nt_ref):
    middle = x_ref[...].astype(F32) + dot_nt(own_ref[...], wo_own_ref[...])
    middle = middle + dot_nt(sib_ref[...], wo_sib_ref[...])
    scale = lax.rsqrt(jnp.mean(middle * middle, axis=-1, keepdims=True) + EPSILON)
    normed = (middle * scale * gain_ref[...]).astype(BF16)
    mid_ref[...] = middle
    n_ref[...] = normed
    nt_ref[...] = normed.T


def form_middle(x, own, sib, wo_own, wo_sib, gain):
    rows, width = x.shape
    half = own.shape[1]
    row_block = lambda cols: pl.BlockSpec((TILE, cols), lambda r: (r, 0))
    return pl.pallas_call(
        middle_kernel,
        grid=(rows // TILE,),
        in_specs=[
            row_block(width),
            row_block(half),
            row_block(half),
            whole(wo_own.shape),
            whole(wo_sib.shape),
            whole(gain.shape),
        ],
        out_specs=[
            row_block(width),
            row_block(width),
            pl.BlockSpec((width, TILE), lambda r: (0, r)),
        ],
        out_shape=[
            jax.ShapeDtypeStruct((rows, width), F32),
            jax.ShapeDtypeStruct((rows, width), BF16),
            jax.ShapeDtypeStruct((width, rows), BF16),
        ],
        compiler_params=call_params(),
        cost_estimate=cost(2 * rows * width * half, 12 * rows * width),
        name="form_middle",
    )(x, own, sib, wo_own, wo_sib, gain)


ROOT = math.sqrt(2.0 / math.pi)
CUBIC = 0.044715


def feed_kernel(
    place,
    core_ref,
    n_ref,
    nt_ref,
    g_ref,
    gt_ref,
    w_ref,
    *refs,
):
    last = len(refs) > 10
    if last:
        ff_in, gn_in, ff_own, ff_give, gn_out, dw_ref = refs[:6]
    else:
        ff_out, gn_out, dw_ref = refs[:3]
    w_full, ff_acc, gn_acc, hid_ref, grad_ref = refs[-5:]
    step = pl.program_id(0)
    rows = n_ref.shape[0]
    depth = w_ref.shape[3]

    @pl.when(step == 0)
    def _():
        if last:
            ff_acc[...] = ff_in[...].astype(F32)
            gn_acc[...] = gn_in[...].astype(F32)
        else:
            ff_acc[...] = jnp.zeros_like(ff_acc)
            gn_acc[...] = jnp.zeros_like(gn_acc)

    for i in range(2):
        w_full[i] = natural_rows(w_ref, place, (i,))
    up = w_full[0]
    dn = w_full[1]

    def rows_step(r, carry):
        here = pl.ds(pl.multiple_of(r * TILE, TILE), TILE)
        pre = dot_nn(n_ref[here, :], up)
        square = pre * pre
        bend = jnp.tanh(ROOT * pre * (1.0 + CUBIC * square))
        half = 0.5 * (1.0 + bend)
        hid = (pre * half).astype(BF16)
        slope = half + (0.5 * ROOT) * pre * (1.0 - bend * bend) * (1.0 + 3.0 * CUBIC * square)
        grad = (dot_nn(g_ref[here, :], dn) * slope).astype(BF16)
        hid_ref[here, :] = hid
        grad_ref[here, :] = grad
        ff_acc[here, :] += dot_nt(hid, dn)
        gn_acc[here, :] += dot_nt(grad, up)
        return carry

    lax.fori_loop(0, rows // TILE, rows_step, 0)
    for i, (left, right) in enumerate(((nt_ref, grad_ref), (gt_ref, hid_ref))):
        product = dot_nn(left[...], right[...]).astype(BF16)
        for chip, p in enumerate(place):
            for t in range(2):
                at = (2 * chip + t) * depth
                dw_ref[p, t, i] = product[at : at + depth]

    @pl.when(step == pl.num_programs(0) - 1)
    def _():
        if last:
            half = ff_own.shape[0]
            core = core_ref[0]
            ff_own[...] = ff_acc[pl.ds(pl.multiple_of(core * half, half), half), :].astype(BF16)
            ff_give[...] = ff_acc[
                pl.ds(pl.multiple_of((1 - core) * half, half), half), :
            ].astype(BF16)
        else:
            ff_out[...] = ff_acc[...].astype(BF16)
        gn_out[...] = gn_acc[...].astype(BF16)


def feed(place, core, normed, normed_t, grad, grad_t, weights, sums=None):
    rows, width = normed.shape
    units = weights.shape[-1]
    chunk = min(512, units)
    weight_shape = weights.shape[:-1] + (chunk,)
    weight_block = pl.BlockSpec(weight_shape, lambda j: (0, 0, 0, 0, j))
    full = jax.ShapeDtypeStruct((rows, width), BF16)
    half = jax.ShapeDtypeStruct((rows // 2, width), BF16)
    sums = () if sums is None else tuple(sums)
    outs = [half, half, full] if sums else [full, full]
    return pl.pallas_call(
        functools.partial(feed_kernel, place),
        grid=(units // chunk,),
        in_specs=[
            pl.BlockSpec(memory_space=pltpu.SMEM),
            whole(normed.shape),
            whole(normed_t.shape),
            whole(grad.shape),
            whole(grad_t.shape),
            weight_block,
        ]
        + [whole(v.shape) for v in sums],
        out_specs=[whole(v.shape) for v in outs] + [weight_block],
        out_shape=outs + [jax.ShapeDtypeStruct(weights.shape, BF16)],
        scratch_shapes=[
            pltpu.VMEM((2, width, chunk), BF16),
            pltpu.VMEM((rows, width), F32),
            pltpu.VMEM((rows, width), F32),
            pltpu.VMEM((rows, chunk), BF16),
            pltpu.VMEM((rows, chunk), BF16),
        ],
        compiler_params=call_params(),
        cost_estimate=cost(
            6 * rows * width * units, 14 * rows * width + 8 * width * units, rows * units
        ),
        name="feed",
    )(core, normed, normed_t, grad, grad_t, weights, *sums)


def norm_back(values, gain, grad):
    scale = lax.rsqrt(jnp.mean(values * values, axis=-1, keepdims=True) + EPSILON)
    weighted = grad * gain
    mean = jnp.mean(values * weighted, axis=-1, keepdims=True)
    out = scale * weighted - values * (scale * scale * scale * mean)
    return out, jnp.sum(grad * values * scale, axis=0, keepdims=True)


def middle_back_kernel(
    place, g_ref, mid_ref, own_ref, sib_ref, gain_ref, wo_ref, att_ref, gm_ref, ga_ref, dwo_ref, dgain_ref, acc
):
    step = pl.program_id(0)
    gy = own_ref[...].astype(F32) + sib_ref[...].astype(F32)
    back, dgain = norm_back(mid_ref[...], gain_ref[...], gy)
    grad_middle = g_ref[...].astype(F32) + back
    branch = grad_middle.astype(BF16)
    gm_ref[...] = grad_middle
    ga_ref[...] = dot_nn(branch, wo_ref[...]).astype(BF16)

    @pl.when(step == 0)
    def _():
        acc[...] = jnp.zeros_like(acc)
        dgain_ref[...] = jnp.zeros_like(dgain_ref)

    acc[...] += dot_nn(branch.T, att_ref[...])
    dgain_ref[...] += dgain

    @pl.when(step == pl.num_programs(0) - 1)
    def _():
        piece = dwo_ref.shape[1]
        for chip, p in enumerate(place):
            dwo_ref[p] = acc[chip * piece : (chip + 1) * piece, :].astype(BF16)


def middle_back(place, g, middle, own, sib, gain, wo, att):
    rows, width = g.shape
    half = att.shape[1]
    row_block = lambda cols: pl.BlockSpec((TILE, cols), lambda r: (r, 0))
    pieces = (len(place), width // len(place), half)
    return pl.pallas_call(
        functools.partial(middle_back_kernel, place),
        grid=(rows // TILE,),
        in_specs=[
            row_block(width),
            row_block(width),
            row_block(width),
            row_block(width),
            whole(gain.shape),
            whole(wo.shape),
            row_block(half),
        ],
        out_specs=[row_block(width), row_block(half), whole(pieces), whole((1, width))],
        out_shape=[
            jax.ShapeDtypeStruct((rows, width), F32),
            jax.ShapeDtypeStruct((rows, half), BF16),
            jax.ShapeDtypeStruct(pieces, BF16),
            jax.ShapeDtypeStruct((1, width), F32),
        ],
        scratch_shapes=[pltpu.VMEM((width, half), F32)],
        compiler_params=call_params(),
        cost_estimate=cost(2 * rows * width * half, 16 * rows * width),
        name="middle_back",
    )(g, middle, own, sib, gain, wo, att)


def project_back_kernel(place, core_ref, nt_ref, dqkv_ref, w_ref, dw_ref, own_ref, give_ref, acc):
    step = pl.program_id(0)
    part = dqkv_ref[0]
    weight = natural_rows(w_ref, place, ())
    product = dot_nn(nt_ref[...], part).astype(BF16)
    depth = dw_ref.shape[2]
    for chip, p in enumerate(place):
        for t in range(2):
            at = (2 * chip + t) * depth
            dw_ref[p, t] = product[at : at + depth]

    @pl.when(step == 0)
    def _():
        acc[...] = dot_nt(part, weight)

    @pl.when(step > 0)
    def _():
        acc[...] += dot_nt(part, weight)

    @pl.when(step == pl.num_programs(0) - 1)
    def _():
        half = own_ref.shape[0]
        core = core_ref[0]
        own_ref[...] = acc[pl.ds(pl.multiple_of(core * half, half), half), :].astype(BF16)
        give_ref[...] = acc[pl.ds(pl.multiple_of((1 - core) * half, half), half), :].astype(BF16)


def project_back(place, core, normed_t, dqkv, packs, depth):
    width, rows = normed_t.shape
    cols = packs.shape[3]
    weight_block = pl.BlockSpec(packs.shape[:2] + (depth, cols), lambda i: (0, 0, i, 0))
    return pl.pallas_call(
        functools.partial(project_back_kernel, place),
        grid=(3,),
        in_specs=[
            pl.BlockSpec(memory_space=pltpu.SMEM),
            whole(normed_t.shape),
            pl.BlockSpec((1, rows, cols), lambda i: (i, 0, 0)),
            weight_block,
        ],
        out_specs=[weight_block, whole((rows // 2, width)), whole((rows // 2, width))],
        out_shape=[
            jax.ShapeDtypeStruct(packs.shape[:2] + (3 * depth, cols), BF16),
            jax.ShapeDtypeStruct((rows // 2, width), BF16),
            jax.ShapeDtypeStruct((rows // 2, width), BF16),
        ],
        scratch_shapes=[pltpu.VMEM((rows, width), F32)],
        compiler_params=call_params(),
        cost_estimate=cost(2 * rows * width * 3 * cols, 8 * rows * width),
        name="project_back",
    )(core, normed_t, dqkv, packs)


def tokens_back_kernel(x_ref, own_ref, sib_ref, gm_ref, gain_ref, out_ref, dgain_ref):
    gy = own_ref[...].astype(F32) + sib_ref[...].astype(F32)
    back, dgain = norm_back(x_ref[...].astype(F32), gain_ref[...], gy)
    out_ref[...] = (gm_ref[...] + back).astype(out_ref.dtype)

    @pl.when(pl.program_id(0) == 0)
    def _():
        dgain_ref[...] = jnp.zeros_like(dgain_ref)

    dgain_ref[...] += dgain


def tokens_back(x, own, sib, gm, gain):
    rows, width = x.shape
    row_block = pl.BlockSpec((TILE, width), lambda r: (r, 0))
    return pl.pallas_call(
        tokens_back_kernel,
        grid=(rows // TILE,),
        in_specs=[row_block, row_block, row_block, row_block, whole(gain.shape)],
        out_specs=[row_block, whole((1, width))],
        out_shape=[
            jax.ShapeDtypeStruct((rows, width), BF16),
            jax.ShapeDtypeStruct((1, width), F32),
        ],
        compiler_params=call_params(),
        cost_estimate=cost(0, 12 * rows * width),
        name="tokens_back",
    )(x, own, sib, gm, gain)


def ring_order(count):
    evens = list(range(0, count, 2))
    odds = list(range(1, count, 2))
    return evens + odds[::-1]


class Paths:
    def __init__(self, chips):
        self.order = ring_order(chips)
        self.place = tuple(self.order.index(k) for k in range(chips))
        index = lambda k, c, y: (2 * k + c) * 2 + y
        every = [(k, c, y) for k in range(chips) for c in range(2) for y in range(2)]
        self.turned = [(index(k, c, y), index(k, y, c)) for k, c, y in every]
        self.across = [(index(k, c, y), index(k, c, 1 - y)) for k, c, y in every]
        self.sibling = [(index(k, c, y), index(k, 1 - c, y)) for k, c, y in every]
        self.rings = [[2 * k + c for k in self.order] for c in range(2)]
        self.chips = chips

    def send(self, values, pairs):
        return lax.ppermute(values, ("dp", "tp"), pairs)

    def gather(self, values):
        return lax.all_gather(values, "dp", axis=0, tiled=False, axis_index_groups=self.rings)

    def reduce(self, values):
        return lax.psum_scatter(
            values, "dp", scatter_dimension=0, tiled=False, axis_index_groups=self.rings
        )


def body(
    chips,
    tokens,
    carried,
    restart,
    lengths,
    gain_attend,
    input_weights,
    state_weights,
    update_weights,
    gate_bias,
    initial_state,
    output_weights,
    gain_feed,
    feed_up,
    feed_down,
    grad_mixed,
    grad_final,
):
    paths = Paths(chips)
    send, place = paths.send, paths.place
    y = lax.axis_index("tp")
    c = lax.axis_index("dp") % 2
    core = c.reshape(1)
    heads, state_len = gate_bias.shape
    depth = input_weights.shape[1]
    cols = heads * HD
    slices = 2 * chips
    gate_len = heads * state_len
    half_rows = tokens.shape[0]
    first = c == 0
    natural = jnp.asarray(place, jnp.int32)
    ringed = jnp.asarray(paths.order, jnp.int32)

    def both_slices(own):
        other = send(own, paths.across)
        return jnp.stack([jnp.where(y == 0, own, other), jnp.where(y == 0, other, own)])

    def in_order(own, sib):
        return jnp.concatenate([jnp.where(first, own, sib), jnp.where(first, sib, own)])

    tail = jnp.concatenate(
        [
            gate_bias.reshape(-1),
            gain_attend,
            gain_feed,
            restart.astype(BF16),
            (lengths // 128).astype(BF16),
            (lengths % 128).astype(BF16),
        ]
    )
    tail = jnp.pad(tail, (0, 16 * cols - tail.shape[0])).reshape(16, cols)
    pack = jnp.concatenate(
        [
            input_weights.reshape(3 * depth, cols),
            jnp.concatenate([state_weights, update_weights], axis=-1).reshape(-1, cols),
            initial_state,
            tail,
        ]
    )
    pack_own = send(pack, paths.turned)
    packs = paths.gather(both_slices(pack_own))
    x_own = send(tokens, paths.turned)
    x = in_order(x_own, send(x_own, paths.sibling))
    small = jnp.take(packs[:, :, 3 * depth :], natural, axis=0)
    small = small.reshape(slices, -1, cols)
    states = small[:, :gate_len].reshape(slices, heads, state_len, 4 * HD)
    states = jnp.moveaxis(states, 1, 0).reshape(heads, HD, 4 * HD)
    at = gate_len
    ws, wu = states[..., : 3 * HD], states[..., 3 * HD :]
    initial = small[:, at : at + initial_state.shape[0]].reshape(S, cols)
    at += initial_state.shape[0]
    flat = small[:, at].astype(F32)
    gate = jnp.moveaxis(flat[:, :gate_len].reshape(slices, heads, state_len), 1, 0)
    gate = gate.reshape(heads, 1, HD)
    gain_one = flat[:, gate_len : gate_len + depth].reshape(1, -1)
    gain_two = flat[:, gate_len + depth : gate_len + 2 * depth].reshape(1, -1)
    flags = pack_own[3 * depth + at, gate_len + 2 * depth : gate_len + 2 * depth + 3]
    flags = flags.astype(F32).astype(jnp.int32)
    restarted = flags[0] > 0
    length = (flags[1] * 128 + flags[2]).reshape(1)

    wo_own = paths.gather(both_slices(send(output_weights.T, paths.turned)))
    wo_own = jnp.take(wo_own, natural, axis=0).reshape(-1, cols)
    wo_sib = send(wo_own, paths.sibling)
    feed_weights = jnp.stack([feed_up, feed_down.T])
    parts = jnp.split(feed_weights, 2, axis=-1)
    feeds = [paths.gather(both_slices(send(part, paths.turned))) for part in parts]

    carried_own = send(carried[0], paths.turned)
    grad_final_own = send(grad_final[0], paths.turned)
    g_own = send(grad_mixed, paths.turned)
    g = in_order(g_own, send(g_own, paths.sibling))
    g_t = g.T

    memory = jnp.where(restarted, initial.astype(F32), carried_own)
    normed_t, projected = project(place, x, gain_one, packs, depth)
    attended, state_out, logs, state_logs, memory_end = attend(
        length, projected, memory, ws, wu, gate
    )
    final_memory = send(memory_end, paths.turned)
    attended_sib = send(attended, paths.sibling)
    middle, normed, normed_mid_t = form_middle(x, attended, attended_sib, wo_own, wo_sib, gain_two)

    sums = feed(place, core, normed, normed_mid_t, g, g_t, feeds[0])
    feed_grads = [sums[-1]]
    ff_own, ff_give, gn, feed_grad = feed(
        place, core, normed, normed_mid_t, g, g_t, feeds[1], sums[:-1]
    )
    feed_grads.append(feed_grad)
    feed_sums = [paths.reduce(grads) for grads in feed_grads]

    ff_sib = send(ff_give, paths.sibling)
    middle_own = lax.dynamic_slice_in_dim(middle, c * half_rows, half_rows)
    mixed_own = (middle_own + ff_own.astype(F32) + ff_sib.astype(F32)).astype(BF16)
    mixed = send(mixed_own, paths.turned)

    grad_middle, grad_attended, dwo, dgain_two = middle_back(
        place, g, middle, gn, send(gn, paths.sibling), gain_two, wo_own, attended
    )

    def to_shard(values):
        keep = lax.dynamic_index_in_dim(values, y, 0, keepdims=False)
        give = lax.dynamic_index_in_dim(values, 1 - y, 0, keepdims=False)
        got = send(give, paths.across)
        return send((keep.astype(F32) + got.astype(F32)).astype(BF16), paths.turned)

    feed_shard = jnp.concatenate([to_shard(v) for v in feed_sums], axis=-1).astype(F32)

    dqkv, dws, dwu, dgate, dmemory = attend_back(
        length,
        projected,
        memory,
        ws,
        wu,
        gate,
        attended,
        state_out,
        logs,
        state_logs,
        grad_attended,
        grad_final_own,
    )
    grad_carried = send(jnp.where(restarted, 0.0, dmemory), paths.turned)
    dinitial = jnp.where(restarted, dmemory, 0.0)
    dw_in, gy_own, gy_give = project_back(place, core, normed_t, dqkv, packs, depth)
    gy_sib = send(gy_give, paths.sibling)
    grad_middle_own = lax.dynamic_slice_in_dim(grad_middle, c * half_rows, half_rows)
    grad_own, dgain_one = tokens_back(x_own, gy_own, gy_sib, grad_middle_own, gain_one)
    dgain_one = dgain_one + send(dgain_one, paths.sibling)
    grad_tokens = send(grad_own, paths.turned).astype(F32)

    dstates = jnp.concatenate([dws, dwu], axis=-1).reshape(heads, slices, state_len, 4 * HD)
    dstates = jnp.moveaxis(dstates, 1, 0).reshape(slices, gate_len, cols)
    dgates = jnp.moveaxis(dgate.reshape(heads, slices, state_len), 1, 0).reshape(slices, gate_len)
    dtail = jnp.concatenate(
        [dgates, dgain_one.reshape(slices, depth), dgain_two.reshape(slices, depth)], axis=1
    )
    dtail = jnp.pad(dtail, ((0, 0), (0, 16 * cols - dtail.shape[1]))).reshape(slices, 16, cols)
    small_grads = jnp.concatenate(
        [
            dstates.astype(BF16),
            dinitial.reshape(slices, -1, cols).astype(BF16),
            dtail.astype(BF16),
        ],
        axis=1,
    )
    small_grads = jnp.take(small_grads.reshape(chips, 2, -1, cols), ringed, axis=0)
    grads = jnp.concatenate([dw_in, dwo.reshape(chips, 2, depth, cols), small_grads], axis=2)
    shard = to_shard(paths.reduce(grads)).astype(F32)
    at = 3 * depth
    out_input = shard[:at].reshape(3, depth, cols)
    out_output = shard[at : at + depth].T
    at += depth
    out_states = shard[at : at + gate_len].reshape(heads, state_len, 4 * HD)
    at += gate_len
    out_initial = shard[at : at + initial_state.shape[0]]
    at += initial_state.shape[0]
    out_tail = shard[at]
    return (
        mixed,
        final_memory[None],
        grad_tokens,
        grad_carried[None],
        out_tail[gate_len : gate_len + depth],
        out_input,
        out_states[..., : 3 * HD],
        out_states[..., 3 * HD :],
        out_tail[:gate_len].reshape(heads, state_len),
        out_initial,
        out_output,
        out_tail[gate_len + depth : gate_len + 2 * depth],
        feed_shard[0],
        feed_shard[1].T,
    )


def solution(mesh):
    ranks, groups = mesh.shape["dp"], mesh.shape["tp"]
    chosen = functools.partial(body, ranks // 2) if groups == 2 else general_body
    placed = (
        P(("dp", "tp"), None),
        P("dp", None, "tp"),
        P("dp"),
        P("dp"),
        P("dp"),
        P(None, "dp", "tp"),
        P("tp", "dp", None),
        P("tp", "dp", None),
        P("tp", "dp"),
        P("dp", "tp"),
        P("tp", "dp"),
        P("dp"),
        P("dp", "tp"),
        P("tp", "dp"),
        P(("dp", "tp"), None),
        P("dp", None, "tp"),
    )
    return jax.shard_map(
        chosen,
        mesh=mesh,
        in_specs=placed,
        out_specs=(
            P(("dp", "tp"), None),
            P("dp", None, "tp"),
            P(("dp", "tp"), None),
            P("dp", None, "tp"),
            P("dp"),
            P(None, "dp", "tp"),
            P("tp", "dp", None),
            P("tp", "dp", None),
            P("tp", "dp"),
            P("dp", "tp"),
            P("tp", "dp"),
            P("dp"),
            P("dp", "tp"),
            P("tp", "dp"),
        ),
        check_vma=False,
    )
```

```python
import functools
import math

import jax
import jax.numpy as jnp
from jax import lax
from jax.experimental import pallas as pl
from jax.experimental.pallas import tpu as pltpu
from jax.sharding import PartitionSpec as P

S = 512
BLK = 512
LEN = 1536
NB = 3


EPSILON = 1e-06
NEGATIVE = -1e30


def rms_scale(values, gain):
    return values * lax.rsqrt(jnp.mean(values * values, axis=-1, keepdims=True) + EPSILON) * gain


def block_masks(block_id, length, block_len, state_count):
    row_ids = jnp.arange(block_len, dtype=jnp.int32)
    places = block_id * block_len + row_ids
    key_places = jnp.concatenate([places - block_len, places])
    allowed = (
        (key_places[None, :] >= 0)
        & (key_places[None, :] < length)
        & (key_places[None, :] <= places[:, None])
        & (key_places[None, :] > places[:, None] - block_len)
    )
    state_open = jnp.ones((block_len, state_count), dtype=bool)
    allowed = jnp.concatenate([allowed, state_open], axis=1)
    usable = jnp.concatenate([places < length, jnp.ones((state_count,), dtype=bool)])
    return (allowed, usable)


def masked_softmax(scores, allowed):
    scores = jnp.where(allowed, scores, NEGATIVE)
    peak_val = jnp.max(scores, axis=-1, keepdims=True)
    powers = jnp.exp(scores - peak_val)
    totals = jnp.sum(powers, axis=-1, keepdims=True)
    return (powers / totals, peak_val + jnp.log(totals))


def recall_softmax(scores, allowed, log_total):
    return jnp.exp(jnp.where(allowed, scores, NEGATIVE) - log_total)


def state_project(memory, state_weights):
    head_dim = memory.shape[-1]
    projected = jnp.einsum(
        "shd,hde->she",
        memory.astype(jnp.bfloat16),
        state_weights,
        preferred_element_type=jnp.float32,
    ).astype(jnp.bfloat16)
    return (
        projected[..., :head_dim],
        projected[..., head_dim : 2 * head_dim],
        projected[..., 2 * head_dim :],
    )


def block_forward(
    state_weights,
    update_weights,
    retain,
    memory,
    queries,
    keys_now,
    values_now,
    keys_before,
    values_before,
    block_id,
    length,
):
    head_dim = queries.shape[-1]
    block_len = queries.shape[0]
    state_count = memory.shape[0]
    scaling = head_dim ** (-0.5)
    state_q, state_k, state_v = state_project(memory, state_weights)
    allowed, usable = block_masks(block_id, length, block_len, state_count)
    key_set = jnp.concatenate([keys_before, keys_now, state_k], axis=0)
    value_set = jnp.concatenate([values_before, values_now, state_v], axis=0)
    scores = (
        jnp.einsum("ihd,jhd->hij", queries, key_set, preferred_element_type=jnp.float32) * scaling
    )
    shares, log_total = masked_softmax(scores, allowed[None])
    outputs = jnp.einsum(
        "hij,jhd->ihd", shares.astype(jnp.bfloat16), value_set, preferred_element_type=jnp.float32
    ).astype(jnp.bfloat16)
    state_keys = jnp.concatenate([keys_now, state_k], axis=0)
    state_values = jnp.concatenate([values_now, state_v], axis=0)
    state_scores = (
        jnp.einsum("shd,jhd->hsj", state_q, state_keys, preferred_element_type=jnp.float32)
        * scaling
    )
    state_shares, state_log = masked_softmax(state_scores, usable[None, None])
    state_out = jnp.einsum(
        "hsj,jhd->shd",
        state_shares.astype(jnp.bfloat16),
        state_values,
        preferred_element_type=jnp.float32,
    ).astype(jnp.bfloat16)
    update = jnp.einsum(
        "shd,hde->she", state_out, update_weights, preferred_element_type=jnp.float32
    )
    blended = retain * memory + (1.0 - retain) * update
    active = block_id * block_len < length
    memory_next = jnp.where(active, blended, memory)
    return (memory_next, (outputs, state_out, log_total, state_log))


def block_backward(
    state_weights,
    update_weights,
    retain,
    memory,
    queries,
    keys_now,
    values_now,
    keys_before,
    values_before,
    grad_out,
    state_out,
    log_total,
    state_log,
    block_id,
    length,
    grad_next,
):
    head_dim = queries.shape[-1]
    block_len = queries.shape[0]
    state_count = memory.shape[0]
    scaling = head_dim ** (-0.5)
    span_end = 2 * block_len
    state_q, state_k, state_v = state_project(memory, state_weights)
    allowed, usable = block_masks(block_id, length, block_len, state_count)
    active = block_id * block_len < length
    update = jnp.einsum(
        "shd,hde->she", state_out, update_weights, preferred_element_type=jnp.float32
    )
    grad_blend = jnp.where(active, grad_next, 0.0)
    grad_memory = jnp.where(active, retain * grad_next, grad_next)
    grad_update = ((1.0 - retain) * grad_blend).astype(jnp.bfloat16)
    grad_gate = jnp.sum(grad_blend * (memory - update), axis=0) * retain * (1.0 - retain)
    grad_update_w = jnp.einsum(
        "shd,she->hde", state_out, grad_update, preferred_element_type=jnp.float32
    )
    grad_state_out = jnp.einsum(
        "she,hde->shd", grad_update, update_weights, preferred_element_type=jnp.float32
    ).astype(jnp.bfloat16)
    state_keys = jnp.concatenate([keys_now, state_k], axis=0)
    state_values = jnp.concatenate([values_now, state_v], axis=0)
    state_scores = (
        jnp.einsum("shd,jhd->hsj", state_q, state_keys, preferred_element_type=jnp.float32)
        * scaling
    )
    state_shares = recall_softmax(state_scores, usable[None, None], state_log)
    grad_state_shares = jnp.einsum(
        "shd,jhd->hsj", grad_state_out, state_values, preferred_element_type=jnp.float32
    )
    grad_state_scores = (
        state_shares
        * (grad_state_shares - jnp.sum(state_shares * grad_state_shares, axis=-1, keepdims=True))
    ).astype(jnp.bfloat16)
    grad_state_values = jnp.einsum(
        "hsj,shd->jhd",
        state_shares.astype(jnp.bfloat16),
        grad_state_out,
        preferred_element_type=jnp.float32,
    )
    grad_state_q = (
        jnp.einsum(
            "hsj,jhd->shd", grad_state_scores, state_keys, preferred_element_type=jnp.float32
        )
        * scaling
    )
    grad_state_keys = (
        jnp.einsum("hsj,shd->jhd", grad_state_scores, state_q, preferred_element_type=jnp.float32)
        * scaling
    )
    key_set = jnp.concatenate([keys_before, keys_now, state_k], axis=0)
    value_set = jnp.concatenate([values_before, values_now, state_v], axis=0)
    scores = (
        jnp.einsum("ihd,jhd->hij", queries, key_set, preferred_element_type=jnp.float32) * scaling
    )
    shares = recall_softmax(scores, allowed[None], log_total)
    grad_shares = jnp.einsum(
        "ihd,jhd->hij", grad_out, value_set, preferred_element_type=jnp.float32
    )
    grad_scores = (
        shares * (grad_shares - jnp.sum(shares * grad_shares, axis=-1, keepdims=True))
    ).astype(jnp.bfloat16)
    grad_values = jnp.einsum(
        "hij,ihd->jhd", shares.astype(jnp.bfloat16), grad_out, preferred_element_type=jnp.float32
    )
    grad_queries = (
        jnp.einsum("hij,jhd->ihd", grad_scores, key_set, preferred_element_type=jnp.float32)
        * scaling
    )
    grad_keys = (
        jnp.einsum("hij,ihd->jhd", grad_scores, queries, preferred_element_type=jnp.float32)
        * scaling
    )
    grad_keys_now = grad_keys[block_len:span_end] + grad_state_keys[:block_len]
    grad_values_now = grad_values[block_len:span_end] + grad_state_values[:block_len]
    grad_state_k = grad_keys[span_end:] + grad_state_keys[block_len:]
    grad_state_v = grad_values[span_end:] + grad_state_values[block_len:]
    grad_proj = jnp.concatenate([grad_state_q, grad_state_k, grad_state_v], axis=-1).astype(
        jnp.bfloat16
    )
    grad_memory = grad_memory + jnp.einsum(
        "she,hde->shd", grad_proj, state_weights, preferred_element_type=jnp.float32
    )
    grad_state_w = jnp.einsum(
        "shd,she->hde", memory.astype(jnp.bfloat16), grad_proj, preferred_element_type=jnp.float32
    )
    return (
        grad_memory,
        grad_queries,
        grad_keys_now,
        grad_values_now,
        grad_keys[:block_len],
        grad_values[:block_len],
        grad_state_w,
        grad_update_w,
        grad_gate,
    )


def general_body(
    tokens,
    carried,
    restart,
    lengths,
    gain_attend,
    input_weights,
    state_weights,
    update_weights,
    gate_bias,
    initial_state,
    output_weights,
    gain_feed,
    feed_up,
    feed_down,
    grad_mixed,
    grad_final,
):
    seq_count = lengths.shape[0]
    heads_here = gate_bias.shape[0]
    head_dim = update_weights.shape[-1]
    width_here = heads_here * head_dim
    group_rows = seq_count * LEN
    gathered = (
        lax.all_gather(gain_attend, "dp", axis=0, tiled=True),
        lax.all_gather(gain_feed, "dp", axis=0, tiled=True),
        lax.all_gather(input_weights, "dp", axis=1, tiled=True),
        lax.all_gather(output_weights, "dp", axis=1, tiled=True),
        lax.all_gather(state_weights, "dp", axis=1, tiled=True),
        lax.all_gather(update_weights, "dp", axis=1, tiled=True),
        lax.all_gather(gate_bias, "dp", axis=1, tiled=True),
        lax.all_gather(initial_state, "dp", axis=0, tiled=True),
        lax.all_gather(feed_up, "dp", axis=0, tiled=True),
        lax.all_gather(feed_down, "dp", axis=1, tiled=True),
    )
    (
        gain_attend_all,
        gain_feed_all,
        input_all,
        output_all,
        state_all,
        update_all,
        gate_all,
        initial_all,
        up_all,
        down_all,
    ) = gathered
    tokens_wide = tokens.astype(jnp.float32)
    gain_one = gain_attend_all.astype(jnp.float32)
    gain_two = gain_feed_all.astype(jnp.float32)
    normed = rms_scale(tokens_wide, gain_one).astype(jnp.bfloat16)
    normed_all = lax.all_gather(normed, "tp", axis=0, tiled=True)
    projected = jnp.einsum(
        "rd,kdc->krc", normed_all, input_all, preferred_element_type=jnp.float32
    ).astype(jnp.bfloat16)
    blocked = jnp.moveaxis(projected.reshape(3, seq_count, NB, BLK, heads_here, head_dim), 2, 1)
    earlier = jnp.concatenate([jnp.zeros_like(blocked[:, :1]), blocked[:, :-1]], axis=1)
    retain = jax.nn.sigmoid(gate_all.astype(jnp.float32))
    memory_start = jnp.where(
        restart[:, None, None] > 0, initial_all.astype(jnp.float32)[None], carried
    ).reshape(seq_count, S, heads_here, head_dim)
    forward_block = jax.vmap(block_forward, in_axes=(None, None, None, 0, 0, 0, 0, 0, 0, None, 0))
    block_ids = jnp.arange(NB, dtype=jnp.int32)

    def forward_step(memory, entries):
        queries, keys_now, values_now, keys_before, values_before, block_id = entries
        memory_next, saved = forward_block(
            state_all,
            update_all,
            retain,
            memory,
            queries,
            keys_now,
            values_now,
            keys_before,
            values_before,
            block_id,
            lengths,
        )
        return (memory_next, (memory, saved))

    memory_end, (memories, saved_all) = lax.scan(
        forward_step,
        memory_start,
        (blocked[0], blocked[1], blocked[2], earlier[1], earlier[2], block_ids),
    )
    outputs, state_outs, log_totals, state_logs = saved_all
    attended = jnp.moveaxis(outputs, 0, 1).reshape(group_rows, width_here)
    middle = tokens_wide + lax.psum_scatter(
        jnp.dot(attended, output_all, preferred_element_type=jnp.float32),
        "tp",
        scatter_dimension=0,
        tiled=True,
    )
    normed_mid = rms_scale(middle, gain_two).astype(jnp.bfloat16)
    mid_all = lax.all_gather(normed_mid, "tp", axis=0, tiled=True)
    hidden_pre = jnp.dot(mid_all, up_all, preferred_element_type=jnp.float32)
    hidden = jax.nn.gelu(hidden_pre).astype(jnp.bfloat16)
    mixed = middle + lax.psum_scatter(
        jnp.dot(hidden, down_all, preferred_element_type=jnp.float32),
        "tp",
        scatter_dimension=0,
        tiled=True,
    )
    grad_rows = lax.all_gather(grad_mixed, "tp", axis=0, tiled=True)
    grad_hidden = jnp.einsum("rd,fd->rf", grad_rows, down_all, preferred_element_type=jnp.float32)
    grad_pre = jax.vjp(jax.nn.gelu, hidden_pre)[1](grad_hidden)[0].astype(jnp.bfloat16)
    grad_down = jnp.einsum("rf,rd->fd", hidden, grad_rows, preferred_element_type=jnp.float32)
    grad_up = jnp.einsum("rd,rf->df", mid_all, grad_pre, preferred_element_type=jnp.float32)
    grad_mid_normed = lax.psum_scatter(
        jnp.einsum("rf,df->rd", grad_pre, up_all, preferred_element_type=jnp.float32),
        "tp",
        scatter_dimension=0,
        tiled=True,
    )
    grad_middle_part, grad_gain_two = jax.vjp(rms_scale, middle, gain_two)[1](grad_mid_normed)
    grad_middle = grad_mixed.astype(jnp.float32) + grad_middle_part
    grad_branch = lax.all_gather(grad_middle.astype(jnp.bfloat16), "tp", axis=0, tiled=True)
    grad_output = jnp.einsum("rc,rd->cd", attended, grad_branch, preferred_element_type=jnp.float32)
    grad_attended = jnp.einsum(
        "rd,cd->rc", grad_branch, output_all, preferred_element_type=jnp.float32
    ).astype(jnp.bfloat16)
    grad_blocks = jnp.moveaxis(
        grad_attended.reshape(seq_count, NB, BLK, heads_here, head_dim), 1, 0
    )
    backward_block = jax.vmap(
        block_backward, in_axes=(None, None, None, 0, 0, 0, 0, 0, 0, 0, 0, 0, 0, None, 0, 0)
    )

    def backward_step(carried_in, entries):
        grad_memory, keys_later, values_later, sum_state, sum_update, sum_gate = carried_in
        (
            memory,
            queries,
            keys_now,
            values_now,
            keys_before,
            values_before,
            grad_out,
            state_out,
            log_total,
            state_log,
            block_id,
        ) = entries
        results = backward_block(
            state_all,
            update_all,
            retain,
            memory,
            queries,
            keys_now,
            values_now,
            keys_before,
            values_before,
            grad_out,
            state_out,
            log_total,
            state_log,
            block_id,
            lengths,
            grad_memory,
        )
        (
            grad_prior,
            grad_queries,
            grad_keys,
            grad_values,
            grad_keys_before,
            grad_values_before,
            part_state,
            part_update,
            part_gate,
        ) = results
        carried_out = (
            grad_prior,
            grad_keys_before,
            grad_values_before,
            sum_state + jnp.sum(part_state, axis=0),
            sum_update + jnp.sum(part_update, axis=0),
            sum_gate + jnp.sum(part_gate, axis=0),
        )
        return (carried_out, (grad_queries, grad_keys + keys_later, grad_values + values_later))

    zero_block = jnp.zeros((seq_count, BLK, heads_here, head_dim), jnp.float32)
    start_carry = (
        grad_final.astype(jnp.float32).reshape(seq_count, S, heads_here, head_dim),
        zero_block,
        zero_block,
        jnp.zeros(state_all.shape, jnp.float32),
        jnp.zeros(update_all.shape, jnp.float32),
        jnp.zeros(retain.shape, jnp.float32),
    )
    final_carry, grad_parts = lax.scan(
        backward_step,
        start_carry,
        (
            memories,
            blocked[0],
            blocked[1],
            blocked[2],
            earlier[1],
            earlier[2],
            grad_blocks,
            state_outs,
            log_totals,
            state_logs,
            block_ids,
        ),
        reverse=True,
    )
    grad_memory_start, unused_keys, unused_values, grad_state_w, grad_update_w, grad_gate_w = (
        final_carry
    )
    grad_qkv = jnp.stack(
        [jnp.moveaxis(member, 0, 1).reshape(group_rows, width_here) for member in grad_parts]
    ).astype(jnp.bfloat16)
    grad_memory_start = grad_memory_start.reshape(seq_count, S, width_here)
    restarted = restart[:, None, None] > 0
    grad_carried = jnp.where(restarted, 0.0, grad_memory_start)
    grad_initial = jnp.sum(jnp.where(restarted, grad_memory_start, 0.0), axis=0)
    grad_input = jnp.einsum("rd,krc->kdc", normed_all, grad_qkv, preferred_element_type=jnp.float32)
    grad_normed = lax.psum_scatter(
        jnp.einsum("krc,kdc->rd", grad_qkv, input_all, preferred_element_type=jnp.float32),
        "tp",
        scatter_dimension=0,
        tiled=True,
    )
    grad_tokens_part, grad_gain_one = jax.vjp(rms_scale, tokens_wide, gain_one)[1](grad_normed)
    grad_tokens = grad_middle + grad_tokens_part
    gain_one_sum, gain_two_sum = lax.psum((grad_gain_one, grad_gain_two), "tp")
    summed = (
        lax.psum_scatter(gain_one_sum, "dp", scatter_dimension=0, tiled=True),
        lax.psum_scatter(gain_two_sum, "dp", scatter_dimension=0, tiled=True),
        lax.psum_scatter(grad_input, "dp", scatter_dimension=1, tiled=True),
        lax.psum_scatter(grad_output, "dp", scatter_dimension=1, tiled=True),
        lax.psum_scatter(grad_state_w, "dp", scatter_dimension=1, tiled=True),
        lax.psum_scatter(grad_update_w, "dp", scatter_dimension=1, tiled=True),
        lax.psum_scatter(grad_gate_w, "dp", scatter_dimension=1, tiled=True),
        lax.psum_scatter(grad_initial, "dp", scatter_dimension=0, tiled=True),
        lax.psum_scatter(grad_up, "dp", scatter_dimension=0, tiled=True),
        lax.psum_scatter(grad_down, "dp", scatter_dimension=1, tiled=True),
    )
    (
        out_gain_one,
        out_gain_two,
        out_input,
        out_output,
        out_state,
        out_update,
        out_gate,
        out_initial,
        out_up,
        out_down,
    ) = summed
    return (
        mixed.astype(jnp.bfloat16),
        memory_end.reshape(seq_count, S, width_here),
        grad_tokens,
        grad_carried,
        out_gain_one,
        out_input,
        out_state,
        out_update,
        out_gate,
        out_initial,
        out_output,
        out_gain_two,
        out_up,
        out_down,
    )


BF16 = jnp.bfloat16
F32 = jnp.float32
HD = 128
TILE = 256
LOG2E = math.log2(math.e)
SCALING = HD ** (-0.5)
TO_POWER = SCALING * LOG2E
VMEM_BYTES = 60 * 1024 * 1024


def dot_nn(left, right):
    return jnp.dot(left, right, preferred_element_type=F32)


def dot_nt(left, right):
    return lax.dot_general(left, right, (((1,), (1,)), ((), ())), preferred_element_type=F32)


def call_params(**more):
    return pltpu.CompilerParams(vmem_limit_bytes=VMEM_BYTES, **more)


def cost(macs, moved, powers=0):
    return pl.CostEstimate(flops=2 * macs, bytes_accessed=moved, transcendentals=powers)


def whole(shape):
    return pl.BlockSpec(shape, lambda *_: (0,) * len(shape), pipeline_mode=pl.Buffered(1))


def project_kernel(x_ref, gain_ref, w_ref, normed_t_ref, out_ref, w_full):
    depth = w_ref.shape[1] // 3

    @pl.when(pl.program_id(0) == 0)
    def _():
        for i in range(3):
            part = w_ref[:, i * depth : (i + 1) * depth]
            w_full[i] = part.reshape(w_full.shape[1:])

    x = x_ref[...].astype(F32)
    scale = lax.rsqrt(jnp.mean(x * x, axis=-1, keepdims=True) + EPSILON)
    normed = (x * scale * gain_ref[...]).astype(BF16)
    normed_t_ref[...] = normed.T
    for i in range(3):
        out_ref[i] = dot_nn(normed, w_full[i]).astype(BF16)


def project(x, gain, packs, depth):
    rows, width = x.shape
    cols = packs.shape[2]
    return pl.pallas_call(
        project_kernel,
        grid=(rows // TILE,),
        in_specs=[
            pl.BlockSpec((TILE, width), lambda r: (r, 0)),
            whole((1, width)),
            whole((packs.shape[0], 3 * depth, cols)),
        ],
        out_specs=[
            pl.BlockSpec((width, TILE), lambda r: (0, r)),
            pl.BlockSpec((3, TILE, cols), lambda r: (0, r, 0)),
        ],
        out_shape=[
            jax.ShapeDtypeStruct((width, rows), BF16),
            jax.ShapeDtypeStruct((3, rows, cols), BF16),
        ],
        scratch_shapes=[pltpu.VMEM((3, width, cols), BF16)],
        compiler_params=call_params(),
        cost_estimate=cost(rows * width * 3 * cols, 6 * rows * width),
        name="project",
    )(x, gain, packs)


def tile_masks():
    key = lax.broadcasted_iota(jnp.int32, (TILE, TILE), 0)
    query = lax.broadcasted_iota(jnp.int32, (TILE, TILE), 1)
    return key, query


def token_tiles(t):
    return [(j, t - j) for j in range(max(0, t - 2), t + 1)]


def masked_scores(scores, tile, behind, length, key, query):
    if behind == 0:
        scores = jnp.where(key <= query, scores, NEGATIVE)
    elif behind == 2:
        scores = jnp.where(key > query, scores, NEGATIVE)
    if tile >= 2 * (NB - 1):
        scores = jnp.where(key + tile * TILE < length, scores, NEGATIVE)
    return scores


def softmax_columns(tiles):
    peak = functools.reduce(jnp.maximum, [jnp.max(s, axis=0, keepdims=True) for s in tiles])
    peak = peak * TO_POWER
    powers = [jnp.exp2(s * TO_POWER - peak) for s in tiles]
    total = functools.reduce(jnp.add, [jnp.sum(p, axis=0, keepdims=True) for p in powers])
    return [p.astype(BF16) for p in powers], total, peak + jnp.log2(total)


def first_memory(flags_ref, carried_ref, initial_ref):
    initial = initial_ref[...].reshape(carried_ref.shape).astype(F32)
    return jnp.where(flags_ref[0, 0] > 0, initial, carried_ref[...])


def attend_kernel(
    flags_ref,
    q_ref,
    k_ref,
    v_ref,
    carried_ref,
    initial_ref,
    ws_ref,
    wu_ref,
    gate_ref,
    out_ref,
    state_out_ref,
    log_ref,
    state_log_ref,
    final_ref,
    vt_ref,
):
    length = flags_ref[0, 1]
    key, query = tile_masks()
    retain = jax.nn.sigmoid(gate_ref[0])
    memory = first_memory(flags_ref, carried_ref, initial_ref)
    vt_ref[...] = v_ref[0].T
    for c in range(NB):
        lo = c * BLK
        state = dot_nn(memory.astype(BF16), ws_ref[0]).astype(BF16)
        sq, sk, sv = state[:, :HD], state[:, HD : 2 * HD], state[:, 2 * HD :]
        svt = sv.T
        for t in range(2 * c, 2 * c + 2):
            rows = slice(t * TILE, (t + 1) * TILE)
            q = q_ref[0, rows]
            spans = token_tiles(t)
            tiles = [
                masked_scores(
                    dot_nt(k_ref[0, j * TILE : (j + 1) * TILE], q), j, behind, length, key, query
                )
                for j, behind in spans
            ]
            tiles.append(dot_nt(sk, q))
            powers, total, logs = softmax_columns(tiles)
            first = spans[0][0] * TILE
            out = dot_nn(vt_ref[:, first : (t + 1) * TILE], jnp.concatenate(powers[:-1], axis=0))
            out = out + dot_nn(svt, powers[-1])
            out_ref[rows] = (out / total).T.astype(BF16)
            log_ref[0, :, rows] = logs
        for u in range(2):
            part = slice(u * TILE, (u + 1) * TILE)
            q = sq[part]
            tiles = []
            for j in range(2):
                s = dot_nt(k_ref[0, lo + j * TILE : lo + (j + 1) * TILE], q)
                if c == NB - 1:
                    s = jnp.where(key + (lo + j * TILE) < length, s, NEGATIVE)
                tiles.append(s)
            tiles.append(dot_nt(sk, q))
            powers, total, logs = softmax_columns(tiles)
            out = dot_nn(vt_ref[:, lo : lo + BLK], jnp.concatenate(powers[:-1], axis=0))
            out = out + dot_nn(svt, powers[-1])
            rows = slice(lo + u * TILE, lo + (u + 1) * TILE)
            state_out_ref[rows] = (out / total).T.astype(BF16)
            state_log_ref[0, :, rows] = logs
        update = dot_nn(state_out_ref[lo : lo + BLK], wu_ref[0])
        blended = retain * memory + (1.0 - retain) * update
        memory = jnp.where(lo < length, blended, memory)
    final_ref[...] = memory


def head_block(rows):
    return pl.BlockSpec((rows, HD), lambda h: (0, h))


def initial_block(packs, at):
    length = S // packs.shape[0]
    return pl.BlockSpec((packs.shape[0], length, HD), lambda h: (0, at // length, h))


def attend(flags, projected, carried, packs, initial_at, states, gate):
    rows = projected.shape[1]
    heads = states.shape[0]
    return pl.pallas_call(
        attend_kernel,
        grid=(heads,),
        in_specs=[
            pl.BlockSpec(memory_space=pltpu.SMEM),
            pl.BlockSpec((1, rows, HD), lambda h: (0, 0, h)),
            pl.BlockSpec((1, rows, HD), lambda h: (1, 0, h)),
            pl.BlockSpec((1, rows, HD), lambda h: (2, 0, h)),
            head_block(S),
            initial_block(packs, initial_at),
            pl.BlockSpec((1, HD, 3 * HD), lambda h: (h, 0, 0)),
            pl.BlockSpec((1, HD, HD), lambda h: (h, 0, 3)),
            pl.BlockSpec((1, 1, HD), lambda h: (h, 0, 0)),
        ],
        out_specs=[
            head_block(rows),
            head_block(NB * S),
            pl.BlockSpec((1, 1, rows), lambda h: (h, 0, 0)),
            pl.BlockSpec((1, 1, NB * S), lambda h: (h, 0, 0)),
            head_block(S),
        ],
        out_shape=[
            jax.ShapeDtypeStruct((rows, heads * HD), BF16),
            jax.ShapeDtypeStruct((NB * S, heads * HD), BF16),
            jax.ShapeDtypeStruct((heads, 1, rows), F32),
            jax.ShapeDtypeStruct((heads, 1, NB * S), F32),
            jax.ShapeDtypeStruct((S, heads * HD), F32),
        ],
        scratch_shapes=[pltpu.VMEM((HD, rows), BF16)],
        compiler_params=call_params(),
        cost_estimate=cost(
            heads * NB * BLK * HD * 2 * (1152 + 1024),
            heads * HD * (rows * 10 + S * 8),
            heads * NB * BLK * 2176,
        ),
        name="attend",
    )(flags, projected, projected, projected, carried, packs, states, states, gate)


def attend_back_kernel(
    flags_ref,
    q_ref,
    k_ref,
    v_ref,
    carried_ref,
    initial_ref,
    ws_ref,
    wu_ref,
    gate_ref,
    out_ref,
    state_out_ref,
    log_ref,
    state_log_ref,
    go_ref,
    grad_final_ref,
    dqkv_ref,
    dws_ref,
    dwu_ref,
    dgate_ref,
    dmemory_ref,
    kt_ref,
    dk_ref,
    dv_ref,
):
    length = flags_ref[0, 1]
    key, query = tile_masks()
    retain = jax.nn.sigmoid(gate_ref[0])
    ws = ws_ref[0]
    wu = wu_ref[0]
    kt_ref[...] = k_ref[0].T
    dk_ref[...] = jnp.zeros_like(dk_ref)
    dv_ref[...] = jnp.zeros_like(dv_ref)
    memories = [first_memory(flags_ref, carried_ref, initial_ref)]
    for c in range(NB - 1):
        update = dot_nn(state_out_ref[c * S : (c + 1) * S], wu)
        blended = retain * memories[c] + (1.0 - retain) * update
        memories.append(jnp.where(c * BLK < length, blended, memories[c]))
    grad_memory = grad_final_ref[...].astype(F32)
    dws = jnp.zeros(ws.shape, F32)
    dwu = jnp.zeros(wu.shape, F32)
    dgate = jnp.zeros(retain.shape, F32)
    for c in reversed(range(NB)):
        lo = c * BLK
        active = lo < length
        memory = memories[c]
        memory_low = memory.astype(BF16)
        state = dot_nn(memory_low, ws).astype(BF16)
        sq, sk, sv = state[:, :HD], state[:, HD : 2 * HD], state[:, 2 * HD :]
        skt = sk.T
        state_out = state_out_ref[lo : lo + S]
        update = dot_nn(state_out, wu)
        grad_blend = jnp.where(active, grad_memory, 0.0)
        grad_update = ((1.0 - retain) * grad_blend).astype(BF16)
        dgate = dgate + jnp.sum(grad_blend * (memory - update), axis=0, keepdims=True)
        dwu = dwu + dot_nn(state_out.T, grad_update)
        grad_state_out = dot_nt(grad_update, wu).astype(BF16)
        grad_memory = jnp.where(active, retain * grad_memory, grad_memory)
        deltas = jnp.sum((grad_state_out.astype(F32) * state_out.astype(F32)).T, axis=0, keepdims=True)
        dsk = jnp.zeros((S, HD), F32)
        dsv = jnp.zeros((S, HD), F32)
        dsq = []
        for u in range(2):
            part = slice(u * TILE, (u + 1) * TILE)
            q = sq[part]
            go = grad_state_out[part]
            logs = state_log_ref[0, :, lo + u * TILE : lo + (u + 1) * TILE]
            delta = deltas[:, part]
            dq = jnp.zeros((HD, TILE), F32)
            for j in range(2):
                rows = slice(lo + j * TILE, lo + (j + 1) * TILE)
                s = dot_nt(k_ref[0, rows], q)
                if c == NB - 1:
                    s = jnp.where(key + (lo + j * TILE) < length, s, NEGATIVE)
                p = jnp.exp2(s * TO_POWER - logs)
                ds = (p * (dot_nt(v_ref[0, rows], go) - delta)).astype(BF16)
                dv_ref[rows] += dot_nn(p.astype(BF16), go)
                dk_ref[rows] += dot_nn(ds, q)
                dq = dq + dot_nn(kt_ref[:, rows], ds)
            p = jnp.exp2(dot_nt(sk, q) * TO_POWER - logs)
            ds = (p * (dot_nt(sv, go) - delta)).astype(BF16)
            dsv = dsv + dot_nn(p.astype(BF16), go)
            dsk = dsk + dot_nn(ds, q)
            dq = dq + dot_nn(skt, ds)
            dsq.append(dq.T)
        for t in range(2 * c, 2 * c + 2):
            here = slice(t * TILE, (t + 1) * TILE)
            q = q_ref[0, here]
            go = go_ref[here]
            logs = log_ref[0, :, here]
            delta = jnp.sum((go.astype(F32) * out_ref[here].astype(F32)).T, axis=0, keepdims=True)
            dq = jnp.zeros((HD, TILE), F32)
            for j, behind in token_tiles(t):
                rows = slice(j * TILE, (j + 1) * TILE)
                s = masked_scores(dot_nt(k_ref[0, rows], q), j, behind, length, key, query)
                p = jnp.exp2(s * TO_POWER - logs)
                ds = (p * (dot_nt(v_ref[0, rows], go) - delta)).astype(BF16)
                dv_ref[rows] += dot_nn(p.astype(BF16), go)
                dk_ref[rows] += dot_nn(ds, q)
                dq = dq + dot_nn(kt_ref[:, rows], ds)
            p = jnp.exp2(dot_nt(sk, q) * TO_POWER - logs)
            ds = (p * (dot_nt(sv, go) - delta)).astype(BF16)
            dsv = dsv + dot_nn(p.astype(BF16), go)
            dsk = dsk + dot_nn(ds, q)
            dq = dq + dot_nn(skt, ds)
            dqkv_ref[0, here] = (dq.T * SCALING).astype(BF16)
        grad_state = jnp.concatenate(
            [jnp.concatenate(dsq, axis=0) * SCALING, dsk * SCALING, dsv], axis=1
        ).astype(BF16)
        grad_memory = grad_memory + dot_nt(grad_state, ws)
        dws = dws + dot_nn(memory_low.T, grad_state)
    dqkv_ref[1] = (dk_ref[...] * SCALING).astype(BF16)
    dqkv_ref[2] = dv_ref[...].astype(BF16)
    dws_ref[0] = dws
    dwu_ref[0] = dwu
    dgate_ref[0] = dgate * retain * (1.0 - retain)
    dmemory_ref[...] = grad_memory


def attend_back(
    flags,
    projected,
    carried,
    packs,
    initial_at,
    states,
    gate,
    out,
    state_out,
    logs,
    state_logs,
    go,
    grad_final,
):
    rows = projected.shape[1]
    heads = states.shape[0]
    per_head = lambda a, b: pl.BlockSpec((1, a, b), lambda h: (h, 0, 0))
    return pl.pallas_call(
        attend_back_kernel,
        grid=(heads,),
        in_specs=[
            pl.BlockSpec(memory_space=pltpu.SMEM),
            pl.BlockSpec((1, rows, HD), lambda h: (0, 0, h)),
            pl.BlockSpec((1, rows, HD), lambda h: (1, 0, h)),
            pl.BlockSpec((1, rows, HD), lambda h: (2, 0, h)),
            head_block(S),
            initial_block(packs, initial_at),
            per_head(HD, 3 * HD),
            pl.BlockSpec((1, HD, HD), lambda h: (h, 0, 3)),
            per_head(1, HD),
            head_block(rows),
            head_block(NB * S),
            per_head(1, rows),
            per_head(1, NB * S),
            head_block(rows),
            head_block(S),
        ],
        out_specs=[
            pl.BlockSpec((3, rows, HD), lambda h: (0, 0, h)),
            per_head(HD, 3 * HD),
            per_head(HD, HD),
            per_head(1, HD),
            head_block(S),
        ],
        out_shape=[
            jax.ShapeDtypeStruct((3, rows, heads * HD), BF16),
            jax.ShapeDtypeStruct((heads, HD, 3 * HD), F32),
            jax.ShapeDtypeStruct((heads, HD, HD), F32),
            jax.ShapeDtypeStruct((heads, 1, HD), F32),
            jax.ShapeDtypeStruct((S, heads * HD), F32),
        ],
        scratch_shapes=[
            pltpu.VMEM((HD, rows), BF16),
            pltpu.VMEM((rows, HD), F32),
            pltpu.VMEM((rows, HD), F32),
        ],
        compiler_params=call_params(),
        cost_estimate=cost(
            heads * NB * BLK * HD * 5 * (1152 + 1024),
            heads * HD * (rows * 20 + S * 16),
            heads * NB * BLK * 2176,
        ),
        name="attend_back",
    )(
        flags,
        projected,
        projected,
        projected,
        carried,
        packs,
        states,
        states,
        gate,
        out,
        state_out,
        logs,
        state_logs,
        go,
        grad_final,
    )


def middle_kernel(x_ref, own_ref, sib_ref, wo_own_ref, wo_sib_ref, gain_ref, mid_ref, n_ref, nt_ref):
    middle = x_ref[...].astype(F32) + dot_nt(own_ref[...], wo_own_ref[...])
    middle = middle + dot_nt(sib_ref[...], wo_sib_ref[...])
    scale = lax.rsqrt(jnp.mean(middle * middle, axis=-1, keepdims=True) + EPSILON)
    normed = (middle * scale * gain_ref[...]).astype(BF16)
    mid_ref[...] = middle
    n_ref[...] = normed
    nt_ref[...] = normed.T


def form_middle(x, own, sib, wo_own, wo_sib, gain):
    rows, width = x.shape
    half = own.shape[1]
    row_block = lambda cols: pl.BlockSpec((TILE, cols), lambda r: (r, 0))
    return pl.pallas_call(
        middle_kernel,
        grid=(rows // TILE,),
        in_specs=[
            row_block(width),
            row_block(half),
            row_block(half),
            whole(wo_own.shape),
            whole(wo_sib.shape),
            whole(gain.shape),
        ],
        out_specs=[
            row_block(width),
            row_block(width),
            pl.BlockSpec((width, TILE), lambda r: (0, r)),
        ],
        out_shape=[
            jax.ShapeDtypeStruct((rows, width), F32),
            jax.ShapeDtypeStruct((rows, width), BF16),
            jax.ShapeDtypeStruct((width, rows), BF16),
        ],
        compiler_params=call_params(),
        cost_estimate=cost(2 * rows * width * half, 12 * rows * width),
        name="form_middle",
    )(x, own, sib, wo_own, wo_sib, gain)


ROOT = math.sqrt(2.0 / math.pi)
CUBIC = 0.044715


def feed_kernel(
    place,
    core_ref,
    n_ref,
    nt_ref,
    g_ref,
    gt_ref,
    up_ref,
    dn_ref,
    *refs,
):
    last = len(refs) > 10
    if last:
        ff_in, gn_in, ff_own, ff_give, gn_out, dw_ref = refs[:6]
    else:
        ff_out, gn_out, dw_ref = refs[:3]
    w_full, ff_acc, gn_acc, hid_ref, grad_ref = refs[-5:]
    step = pl.program_id(0)
    rows = n_ref.shape[0]
    depth = dw_ref.shape[2]

    @pl.when(step == 0)
    def _():
        if last:
            ff_acc[...] = ff_in[...].astype(F32)
            gn_acc[...] = gn_in[...].astype(F32)
        else:
            ff_acc[...] = jnp.zeros_like(ff_acc)
            gn_acc[...] = jnp.zeros_like(gn_acc)

    for i, ref in enumerate((up_ref, dn_ref)):
        w_full[i] = jnp.concatenate([ref[p] for p in place], axis=0)
    up = w_full[0]
    dn = w_full[1]

    def rows_step(r, carry):
        here = pl.ds(pl.multiple_of(r * TILE, TILE), TILE)
        pre = dot_nn(n_ref[here, :], up)
        square = pre * pre
        bend = jnp.tanh(ROOT * pre * (1.0 + CUBIC * square))
        half = 0.5 * (1.0 + bend)
        hid = (pre * half).astype(BF16)
        slope = half + (0.5 * ROOT) * pre * (1.0 - bend * bend) * (1.0 + 3.0 * CUBIC * square)
        grad = (dot_nn(g_ref[here, :], dn) * slope).astype(BF16)
        hid_ref[here, :] = hid
        grad_ref[here, :] = grad
        ff_acc[here, :] += dot_nt(hid, dn)
        gn_acc[here, :] += dot_nt(grad, up)
        return carry

    lax.fori_loop(0, rows // TILE, rows_step, 0)
    for i, (left, right) in enumerate(((nt_ref, grad_ref), (gt_ref, hid_ref))):
        product = dot_nn(left[...], right[...]).astype(BF16)
        for block, p in enumerate(place):
            dw_ref[p, i] = product[block * depth : (block + 1) * depth]

    @pl.when(step == pl.num_programs(0) - 1)
    def _():
        if last:
            half = ff_own.shape[0]
            core = core_ref[0]
            ff_own[...] = ff_acc[pl.ds(pl.multiple_of(core * half, half), half), :].astype(BF16)
            ff_give[...] = ff_acc[
                pl.ds(pl.multiple_of((1 - core) * half, half), half), :
            ].astype(BF16)
        else:
            ff_out[...] = ff_acc[...].astype(BF16)
        gn_out[...] = gn_acc[...].astype(BF16)


def feed(place, core, normed, normed_t, grad, grad_t, weights, units, sums=None):
    rows, width = normed.shape
    pieces, depth = weights.shape[:2]
    chunk = next(size for size in (512, 384, 256, 128, units) if units % size == 0)
    steps = units // chunk
    piece_block = lambda first: pl.BlockSpec((pieces, depth, chunk), lambda j: (0, 0, first + j))
    grad_block = pl.BlockSpec((pieces, 2, depth, chunk), lambda j: (0, 0, 0, j))
    full = jax.ShapeDtypeStruct((rows, width), BF16)
    half = jax.ShapeDtypeStruct((rows // 2, width), BF16)
    sums = () if sums is None else tuple(sums)
    outs = [half, half, full] if sums else [full, full]
    return pl.pallas_call(
        functools.partial(feed_kernel, place),
        grid=(steps,),
        in_specs=[
            pl.BlockSpec(memory_space=pltpu.SMEM),
            whole(normed.shape),
            whole(normed_t.shape),
            whole(grad.shape),
            whole(grad_t.shape),
            piece_block(0),
            piece_block(steps),
        ]
        + [whole(v.shape) for v in sums],
        out_specs=[whole(v.shape) for v in outs] + [grad_block],
        out_shape=outs + [jax.ShapeDtypeStruct((pieces, 2, depth, units), BF16)],
        scratch_shapes=[
            pltpu.VMEM((2, width, chunk), BF16),
            pltpu.VMEM((rows, width), F32),
            pltpu.VMEM((rows, width), F32),
            pltpu.VMEM((rows, chunk), BF16),
            pltpu.VMEM((rows, chunk), BF16),
        ],
        compiler_params=call_params(),
        cost_estimate=cost(
            6 * rows * width * units, 14 * rows * width + 8 * width * units, rows * units
        ),
        name="feed",
    )(core, normed, normed_t, grad, grad_t, weights, weights, *sums)


def norm_back(values, gain, grad):
    scale = lax.rsqrt(jnp.mean(values * values, axis=-1, keepdims=True) + EPSILON)
    weighted = grad * gain
    mean = jnp.mean(values * weighted, axis=-1, keepdims=True)
    out = scale * weighted - values * (scale * scale * scale * mean)
    return out, jnp.sum(grad * values * scale, axis=0, keepdims=True)


def middle_back_kernel(
    place, g_ref, mid_ref, own_ref, sib_ref, gain_ref, wo_ref, att_ref, gm_ref, ga_ref, dwo_ref, dgain_ref, acc
):
    step = pl.program_id(0)
    gy = own_ref[...].astype(F32) + sib_ref[...].astype(F32)
    back, dgain = norm_back(mid_ref[...], gain_ref[...], gy)
    grad_middle = g_ref[...].astype(F32) + back
    branch = grad_middle.astype(BF16)
    gm_ref[...] = grad_middle
    ga_ref[...] = dot_nn(branch, wo_ref[...]).astype(BF16)

    @pl.when(step == 0)
    def _():
        acc[...] = jnp.zeros_like(acc)
        dgain_ref[...] = jnp.zeros_like(dgain_ref)

    acc[...] += dot_nn(branch.T, att_ref[...])
    dgain_ref[...] += dgain

    @pl.when(step == pl.num_programs(0) - 1)
    def _():
        piece = dwo_ref.shape[1]
        for chip, p in enumerate(place):
            dwo_ref[p] = acc[chip * piece : (chip + 1) * piece, :].astype(BF16)


def middle_back(place, g, middle, own, sib, gain, wo, att):
    rows, width = g.shape
    half = att.shape[1]
    row_block = lambda cols: pl.BlockSpec((TILE, cols), lambda r: (r, 0))
    pieces = (len(place), width // len(place), half)
    return pl.pallas_call(
        functools.partial(middle_back_kernel, place),
        grid=(rows // TILE,),
        in_specs=[
            row_block(width),
            row_block(width),
            row_block(width),
            row_block(width),
            whole(gain.shape),
            whole(wo.shape),
            row_block(half),
        ],
        out_specs=[row_block(width), row_block(half), whole(pieces), whole((1, width))],
        out_shape=[
            jax.ShapeDtypeStruct((rows, width), F32),
            jax.ShapeDtypeStruct((rows, half), BF16),
            jax.ShapeDtypeStruct(pieces, BF16),
            jax.ShapeDtypeStruct((1, width), F32),
        ],
        scratch_shapes=[pltpu.VMEM((width, half), F32)],
        compiler_params=call_params(),
        cost_estimate=cost(2 * rows * width * half, 16 * rows * width),
        name="middle_back",
    )(g, middle, own, sib, gain, wo, att)


def project_back_kernel(place, core_ref, nt_ref, dqkv_ref, w_ref, dw_ref, own_ref, give_ref, acc):
    step = pl.program_id(0)
    part = dqkv_ref[0]
    weight = w_ref[...].reshape(nt_ref.shape[0], part.shape[1])
    product = dot_nn(nt_ref[...], part).astype(BF16)
    depth = dw_ref.shape[2]
    for chip, p in enumerate(place):
        for t in range(2):
            at = (2 * chip + t) * depth
            dw_ref[p, t] = product[at : at + depth]

    @pl.when(step == 0)
    def _():
        acc[...] = dot_nt(part, weight)

    @pl.when(step > 0)
    def _():
        acc[...] += dot_nt(part, weight)

    @pl.when(step == pl.num_programs(0) - 1)
    def _():
        half = own_ref.shape[0]
        core = core_ref[0]
        own_ref[...] = acc[pl.ds(pl.multiple_of(core * half, half), half), :].astype(BF16)
        give_ref[...] = acc[pl.ds(pl.multiple_of((1 - core) * half, half), half), :].astype(BF16)


def project_back(place, core, normed_t, dqkv, packs, depth):
    width, rows = normed_t.shape
    slices, _, cols = packs.shape
    chips = slices // 2
    weight_block = pl.BlockSpec((slices, depth, cols), lambda i: (0, i, 0))
    grad_block = pl.BlockSpec((chips, 2, depth, cols), lambda i: (0, 0, i, 0))
    return pl.pallas_call(
        functools.partial(project_back_kernel, place),
        grid=(3,),
        in_specs=[
            pl.BlockSpec(memory_space=pltpu.SMEM),
            whole(normed_t.shape),
            pl.BlockSpec((1, rows, cols), lambda i: (i, 0, 0)),
            weight_block,
        ],
        out_specs=[grad_block, whole((rows // 2, width)), whole((rows // 2, width))],
        out_shape=[
            jax.ShapeDtypeStruct((chips, 2, 3 * depth, cols), BF16),
            jax.ShapeDtypeStruct((rows // 2, width), BF16),
            jax.ShapeDtypeStruct((rows // 2, width), BF16),
        ],
        scratch_shapes=[pltpu.VMEM((rows, width), F32)],
        compiler_params=call_params(),
        cost_estimate=cost(2 * rows * width * 3 * cols, 8 * rows * width),
        name="project_back",
    )(core, normed_t, dqkv, packs)


def tokens_back_kernel(x_ref, own_ref, sib_ref, gm_ref, gain_ref, out_ref, dgain_ref):
    gy = own_ref[...].astype(F32) + sib_ref[...].astype(F32)
    back, dgain = norm_back(x_ref[...].astype(F32), gain_ref[...], gy)
    out_ref[...] = (gm_ref[...] + back).astype(out_ref.dtype)

    @pl.when(pl.program_id(0) == 0)
    def _():
        dgain_ref[...] = jnp.zeros_like(dgain_ref)

    dgain_ref[...] += dgain


def tokens_back(x, own, sib, gm, gain):
    rows, width = x.shape
    row_block = pl.BlockSpec((TILE, width), lambda r: (r, 0))
    return pl.pallas_call(
        tokens_back_kernel,
        grid=(rows // TILE,),
        in_specs=[row_block, row_block, row_block, row_block, whole(gain.shape)],
        out_specs=[row_block, whole((1, width))],
        out_shape=[
            jax.ShapeDtypeStruct((rows, width), BF16),
            jax.ShapeDtypeStruct((1, width), F32),
        ],
        compiler_params=call_params(),
        cost_estimate=cost(0, 12 * rows * width),
        name="tokens_back",
    )(x, own, sib, gm, gain)


def ring_order(count):
    evens = list(range(0, count, 2))
    odds = list(range(1, count, 2))
    return evens + odds[::-1]


MESH = pl.DeviceIdType.MESH


def entry_kernel(
    order,
    cut,
    tok_ref,
    grad_ref,
    carried_ref,
    final_ref,
    w_ref,
    states_ref,
    updates_ref,
    gate_ref,
    gain_one_ref,
    gain_two_ref,
    initial_ref,
    wo_ref,
    up_ref,
    down_ref,
    restart_ref,
    length_ref,
    x_ref,
    g_ref,
    memory_ref,
    grad_final_ref,
    packs_ref,
    feed_one_ref,
    feed_two_ref,
    flags_ref,
    pack_ref,
    own_one_ref,
    own_two_ref,
    flag_ref,
    *sems,
):
    turn_send, turn_recv, rows_send, rows_recv, sib_send, sib_recv, ring_send, ring_recv = sems
    chips = len(order)
    dp = lax.axis_index("dp")
    y = lax.axis_index("tp")
    k = dp // 2
    c = dp % 2
    stays = c == y
    moves = jnp.logical_not(stays)
    partner = (2 * k + 1 - c, 1 - y)
    sibling = (2 * k + 1 - c, y)
    opposite = (dp, 1 - y)
    place = [order.index(i) for i in range(chips)]

    def chip_after(steps):
        found = jnp.int32(0)
        for i in range(chips):
            onward = order[(place[i] + steps) % chips]
            back = order[(place[i] - steps) % chips]
            found = jnp.where(k == i, jnp.where(c == 0, onward, back), found)
        return found

    following = (2 * chip_after(1) + c, y)
    previous = (2 * chip_after(-1) + c, y)
    barrier = pltpu.get_barrier_semaphore()
    for device in (sibling, opposite, following, previous):
        pl.semaphore_signal(barrier, inc=1, device_id=device, device_id_type=MESH)

    @pl.when(moves)
    def _():
        pl.semaphore_signal(barrier, inc=1, device_id=partner, device_id_type=MESH)

    parts, depth, cols = w_ref.shape
    heads, state_len, state_cols = states_ref.shape
    for i in range(parts):
        pack_ref[i * depth : (i + 1) * depth] = w_ref[i]
    at = parts * depth
    for h in range(heads):
        rows = slice(at + h * state_len, at + (h + 1) * state_len)
        pack_ref[rows, :state_cols] = states_ref[h]
        pack_ref[rows, state_cols:] = updates_ref[h]
    at += heads * state_len
    pack_ref[at : at + initial_ref.shape[0]] = initial_ref[...]
    at += initial_ref.shape[0]
    pack_ref[at:] = jnp.zeros((pack_ref.shape[0] - at, cols), BF16)
    pack_ref[at : at + heads, :state_len] = gate_ref[...]
    pack_ref[at + heads : at + heads + 1, :depth] = gain_one_ref[...]
    pack_ref[at + heads + 1 : at + heads + 2, :depth] = gain_two_ref[...]
    lane = lax.broadcasted_iota(jnp.int32, flag_ref.shape, 1)
    flag_ref[...] = jnp.where(lane == 0, restart_ref[0], length_ref[0])

    def remote(src, dst, send_sem, recv_sem, device):
        return pltpu.make_async_remote_copy(
            src_ref=src,
            dst_ref=dst,
            send_sem=send_sem,
            recv_sem=recv_sem,
            device_id=device,
            device_id_type=MESH,
        )

    own_block = 2 * k + y
    other_block = 2 * k + 1 - y
    turns = [
        (pack_ref, packs_ref.at[2 * k + c]),
        (flag_ref, flags_ref),
        (own_one_ref, feed_one_ref),
        (own_two_ref, feed_two_ref),
        (carried_ref, memory_ref),
        (final_ref, grad_final_ref),
    ]

    def turn(i):
        src, dst = turns[i]
        return remote(src, dst, turn_send.at[i], turn_recv.at[i], partner)

    pieces = rows_send.shape[1]
    size = tok_ref.shape[0] // pieces
    row_pairs = ((tok_ref, x_ref), (grad_ref, g_ref))

    def swap(n, i, half):
        src, dst = row_pairs[n]
        rows = pl.ds(i * size, size)
        return remote(
            src.at[rows], dst.at[half, rows], rows_send.at[n, i], rows_recv.at[n, i], partner
        )

    def share(n, i, source, half):
        rows = pl.ds(i * size, size)
        return remote(
            source.at[rows],
            row_pairs[n][1].at[half, rows],
            sib_send.at[n, i],
            sib_recv.at[n, i],
            sibling,
        )

    def cross(src, block):
        last = len(turns)
        return remote(src, packs_ref.at[block], turn_send.at[last], turn_recv.at[last], opposite)

    def ring(src, block, step, j):
        return remote(
            src, packs_ref.at[block], ring_send.at[step, j], ring_recv.at[step, j], following
        )

    @pl.when(stays)
    def _():
        pl.semaphore_wait(barrier, 4)
        cross(pack_ref, own_block).start()
        ring(pack_ref, own_block, 0, 0).start()
        for n in range(2):
            for i in range(pieces):
                share(n, i, row_pairs[n][0], c).start()

    @pl.when(moves)
    def _():
        pl.semaphore_wait(barrier, 5)
        turn(0).start()
        turn(1).start()

    units = up_ref.shape[1]
    down = down_ref[...].T
    own_one_ref[:, :cut] = up_ref[:, :cut]
    own_one_ref[:, cut : 2 * cut] = down[:, :cut]
    own_one_ref[:, 2 * cut :] = wo_ref[...].T
    own_two_ref[:, : units - cut] = up_ref[:, cut:]
    own_two_ref[:, units - cut :] = down[:, cut:]

    @pl.when(moves)
    def _():
        remote(
            pack_ref, packs_ref.at[own_block], turn_send.at[0], turn_recv.at[0], partner
        ).wait_recv()
        cross(packs_ref.at[own_block], own_block).start()
        ring(packs_ref.at[own_block], own_block, 0, 0).start()
        for i in range(pieces):
            swap(0, i, 1 - c).start()
        for i in range(2, len(turns)):
            turn(i).start()
        for i in range(pieces):
            swap(1, i, 1 - c).start()

    @pl.when(stays)
    def _():
        packs_ref[own_block] = pack_ref[...]
        flags_ref[...] = flag_ref[...]
        feed_one_ref[...] = own_one_ref[...]
        feed_two_ref[...] = own_two_ref[...]
        x_ref[c] = tok_ref[...]
        g_ref[c] = grad_ref[...]
        memory_ref[...] = carried_ref[...]
        grad_final_ref[...] = final_ref[...]

    def forward(n, i):
        @pl.when(moves)
        def _():
            swap(n, i, c).wait_recv()
            share(n, i, row_pairs[n][1].at[c], c).start()

    cross(pack_ref, other_block).wait_recv()
    ring(packs_ref.at[other_block], other_block, 0, 1).start()
    for step in range(1, chips):
        chip = chip_after(-step)
        for j in range(2):
            block = 2 * chip + jnp.where(j == 0, y, 1 - y)
            ring(packs_ref.at[block], block, step - 1, j).wait_recv()
            if step < chips - 1:
                ring(packs_ref.at[block], block, step, j).start()
        if 2 <= step < 2 + pieces:
            forward(0, step - 2)
    for i in range(max(0, chips - 2), pieces):
        forward(0, i)

    @pl.when(moves)
    def _():
        for i in range(1, len(turns)):
            turn(i).wait_recv()

    for i in range(pieces):
        forward(1, i)
    for n in range(2):
        for i in range(pieces):
            share(n, i, row_pairs[n][0], 1 - c).wait_recv()
            share(n, i, row_pairs[n][0], c).wait_send()
    cross(pack_ref, own_block).wait_send()
    for step in range(chips - 1):
        for j in range(2):
            ring(pack_ref, own_block, step, j).wait_send()

    @pl.when(moves)
    def _():
        for i in range(len(turns)):
            turn(i).wait_send()
        for n in range(2):
            for i in range(pieces):
                swap(n, i, 1 - c).wait_send()


def enter(
    order,
    cut,
    tokens,
    grad,
    carried,
    grad_final,
    w_in,
    states,
    updates,
    gate,
    gain_one,
    gain_two,
    initial,
    wo,
    up,
    down,
    restart,
    lengths,
):
    chips = len(order)
    pieces = 4
    depth, cols = w_in.shape[1:]
    units = up.shape[1]
    heads, state_len = gate.shape
    pack = (3 * depth + heads * state_len + initial.shape[0] + 16, cols)
    feed_one = (depth, 2 * cut + cols)
    feed_two = (depth, 2 * (units - cut))
    dma = pltpu.SemaphoreType.DMA
    in_vmem = pl.BlockSpec(memory_space=pltpu.VMEM)
    in_smem = pl.BlockSpec(memory_space=pltpu.SMEM)
    shape = jax.ShapeDtypeStruct
    return pl.pallas_call(
        functools.partial(entry_kernel, tuple(order), cut),
        in_specs=[in_vmem] * 14 + [in_smem] * 2,
        out_specs=[in_vmem] * 8,
        out_shape=[
            shape((2,) + tokens.shape, BF16),
            shape((2,) + tokens.shape, BF16),
            shape(carried.shape, F32),
            shape(grad_final.shape, BF16),
            shape((2 * chips,) + pack, BF16),
            shape(feed_one, BF16),
            shape(feed_two, BF16),
            shape((1, 128), jnp.int32),
        ],
        scratch_shapes=[
            pltpu.VMEM(pack, BF16),
            pltpu.VMEM(feed_one, BF16),
            pltpu.VMEM(feed_two, BF16),
            pltpu.VMEM((1, 128), jnp.int32),
            dma((7,)),
            dma((7,)),
            dma((2, pieces)),
            dma((2, pieces)),
            dma((2, pieces)),
            dma((2, pieces)),
            dma((chips - 1, 2)),
            dma((chips - 1, 2)),
        ],
        compiler_params=call_params(collective_id=0, has_side_effects=True),
        cost_estimate=cost(0, 16 * tokens.size),
        name="enter",
    )(
        tokens,
        grad,
        carried,
        grad_final,
        w_in,
        states,
        updates,
        gate,
        gain_one.reshape(1, -1),
        gain_two.reshape(1, -1),
        initial,
        wo,
        up,
        down,
        restart,
        lengths,
    )


class Paths:
    def __init__(self, chips):
        self.order = ring_order(chips)
        self.place = tuple(self.order.index(k) for k in range(chips))
        index = lambda k, c, y: (2 * k + c) * 2 + y
        every = [(k, c, y) for k in range(chips) for c in range(2) for y in range(2)]
        self.turned = [(index(k, c, y), index(k, y, c)) for k, c, y in every]
        self.across = [(index(k, c, y), index(k, c, 1 - y)) for k, c, y in every]
        self.sibling = [(index(k, c, y), index(k, 1 - c, y)) for k, c, y in every]
        self.rings = [[2 * k + c for k in self.order] for c in range(2)]
        there = [(k, 0) for k in self.order] + [(k, 1) for k in self.order[::-1]]
        self.loops = [[index(k, c, y) for k, y in there] for c in range(2)]
        self.spots = tuple(there.index((b // 2, b % 2)) for b in range(2 * chips))
        self.chips = chips

    def send(self, values, pairs):
        return lax.ppermute(values, ("dp", "tp"), pairs)

    def gather(self, values):
        return lax.all_gather(values, "dp", axis=0, tiled=False, axis_index_groups=self.rings)

    def gather_loop(self, values):
        return lax.all_gather(
            values, ("dp", "tp"), axis=0, tiled=False, axis_index_groups=self.loops
        )

    def reduce_loop(self, values):
        return lax.psum_scatter(
            values,
            ("dp", "tp"),
            scatter_dimension=0,
            tiled=False,
            axis_index_groups=self.loops,
        )

    def reduce(self, values):
        return lax.psum_scatter(
            values, "dp", scatter_dimension=0, tiled=False, axis_index_groups=self.rings
        )


def body(
    chips,
    tokens,
    carried,
    restart,
    lengths,
    gain_attend,
    input_weights,
    state_weights,
    update_weights,
    gate_bias,
    initial_state,
    output_weights,
    gain_feed,
    feed_up,
    feed_down,
    grad_mixed,
    grad_final,
):
    paths = Paths(chips)
    send, place = paths.send, paths.place
    y = lax.axis_index("tp")
    c = lax.axis_index("dp") % 2
    core = c.reshape(1)
    heads, state_len = gate_bias.shape
    depth = input_weights.shape[1]
    cols = heads * HD
    slices = 2 * chips
    gate_len = heads * state_len
    half_rows = tokens.shape[0]
    ringed = jnp.asarray(paths.order, jnp.int32)

    units = feed_up.shape[1]
    cut = units // 8 * 5
    entered = enter(
        paths.order,
        cut,
        tokens,
        grad_mixed,
        carried[0],
        grad_final[0],
        input_weights,
        state_weights,
        update_weights,
        gate_bias,
        gain_attend,
        gain_feed,
        initial_state,
        output_weights,
        feed_up,
        feed_down,
        restart,
        lengths,
    )
    x, g, carried_own, grad_final_own, packs, first_feed, second_feed, flags = entered
    x = x.reshape(2 * half_rows, -1)
    g = g.reshape(2 * half_rows, -1)
    first_feed = paths.gather_loop(first_feed)
    second_feed = paths.gather_loop(second_feed)
    restarted = flags[0, 0] > 0
    states_at = 3 * depth
    initial_at = states_at + gate_len
    tail_at = initial_at + initial_state.shape[0]
    small = packs[:, tail_at : tail_at + heads + 2, :depth].astype(F32)
    gain_one = small[:, heads].reshape(1, -1)
    gain_two = small[:, heads + 1].reshape(1, -1)
    gate = jnp.moveaxis(small[:, :heads, :state_len], 1, 0).reshape(heads, 1, HD)
    states = packs[:, states_at:initial_at].reshape(slices, heads, state_len, 4 * HD)
    states = jnp.moveaxis(states, 1, 0).reshape(heads, HD, 4 * HD)
    spots = jnp.asarray(paths.spots, jnp.int32)
    wo_own = jnp.take(first_feed[:, :, 2 * cut :], spots, axis=0).reshape(-1, cols)
    wo_sib = send(wo_own, paths.sibling)
    g_t = g.T

    normed_t, projected = project(x, gain_one, packs, depth)
    attended, state_out, logs, state_logs, memory_end = attend(
        flags, projected, carried_own, packs, initial_at, states, gate
    )
    final_memory = send(memory_end, paths.turned)
    attended_sib = send(attended, paths.sibling)
    middle, normed, normed_mid_t = form_middle(x, attended, attended_sib, wo_own, wo_sib, gain_two)

    sums = feed(paths.spots, core, normed, normed_mid_t, g, g_t, first_feed, cut)
    feed_grads = [sums[-1]]
    ff_own, ff_give, gn, feed_grad = feed(
        paths.spots, core, normed, normed_mid_t, g, g_t, second_feed, units - cut, sums[:-1]
    )
    feed_grads.append(feed_grad)
    feed_shard = jnp.concatenate(
        [send(paths.reduce_loop(grads), paths.turned) for grads in feed_grads], axis=-1
    ).astype(F32)

    ff_sib = send(ff_give, paths.sibling)
    middle_own = lax.dynamic_slice_in_dim(middle, c * half_rows, half_rows)
    mixed_own = (middle_own + ff_own.astype(F32) + ff_sib.astype(F32)).astype(BF16)
    mixed = send(mixed_own, paths.turned)

    grad_middle, grad_attended, dwo, dgain_two = middle_back(
        place, g, middle, gn, send(gn, paths.sibling), gain_two, wo_own, attended
    )

    def to_shard(values):
        keep = lax.dynamic_index_in_dim(values, y, 0, keepdims=False)
        give = lax.dynamic_index_in_dim(values, 1 - y, 0, keepdims=False)
        got = send(give, paths.across)
        return send((keep.astype(F32) + got.astype(F32)).astype(BF16), paths.turned)

    dqkv, dws, dwu, dgate, dmemory = attend_back(
        flags,
        projected,
        carried_own,
        packs,
        initial_at,
        states,
        gate,
        attended,
        state_out,
        logs,
        state_logs,
        grad_attended,
        grad_final_own,
    )
    grad_carried = send(jnp.where(restarted, 0.0, dmemory), paths.turned)
    dinitial = jnp.where(restarted, dmemory, 0.0)
    dw_in, gy_own, gy_give = project_back(place, core, normed_t, dqkv, packs, depth)
    gy_sib = send(gy_give, paths.sibling)
    x_own = lax.dynamic_slice_in_dim(x, c * half_rows, half_rows)
    grad_middle_own = lax.dynamic_slice_in_dim(grad_middle, c * half_rows, half_rows)
    grad_own, dgain_one = tokens_back(x_own, gy_own, gy_sib, grad_middle_own, gain_one)
    dgain_one = dgain_one + send(dgain_one, paths.sibling)
    grad_tokens = send(grad_own, paths.turned).astype(F32)

    dstates = jnp.concatenate([dws, dwu], axis=-1).reshape(heads, slices, state_len, 4 * HD)
    dstates = jnp.moveaxis(dstates, 1, 0).reshape(slices, gate_len, cols)
    dgates = jnp.moveaxis(dgate.reshape(heads, slices, state_len), 1, 0).reshape(slices, gate_len)
    dtail = jnp.concatenate(
        [dgates, dgain_one.reshape(slices, depth), dgain_two.reshape(slices, depth)], axis=1
    )
    dtail = jnp.pad(dtail, ((0, 0), (0, 16 * cols - dtail.shape[1]))).reshape(slices, 16, cols)
    small_grads = jnp.concatenate(
        [
            dstates.astype(BF16),
            dinitial.reshape(slices, -1, cols).astype(BF16),
            dtail.astype(BF16),
        ],
        axis=1,
    )
    small_grads = jnp.take(small_grads.reshape(chips, 2, -1, cols), ringed, axis=0)
    grads = jnp.concatenate([dw_in, dwo.reshape(chips, 2, depth, cols), small_grads], axis=2)
    shard = to_shard(paths.reduce(grads)).astype(F32)
    at = 3 * depth
    out_input = shard[:at].reshape(3, depth, cols)
    out_output = shard[at : at + depth].T
    at += depth
    out_states = shard[at : at + gate_len].reshape(heads, state_len, 4 * HD)
    at += gate_len
    out_initial = shard[at : at + initial_state.shape[0]]
    at += initial_state.shape[0]
    out_tail = shard[at]
    return (
        mixed,
        final_memory[None],
        grad_tokens,
        grad_carried[None],
        out_tail[gate_len : gate_len + depth],
        out_input,
        out_states[..., : 3 * HD],
        out_states[..., 3 * HD :],
        out_tail[:gate_len].reshape(heads, state_len),
        out_initial,
        out_output,
        out_tail[gate_len + depth : gate_len + 2 * depth],
        feed_shard[0],
        feed_shard[1].T,
    )


def solution(mesh):
    ranks, groups = mesh.shape["dp"], mesh.shape["tp"]
    chosen = functools.partial(body, ranks // 2) if groups == 2 else general_body
    placed = (
        P(("dp", "tp"), None),
        P("dp", None, "tp"),
        P("dp"),
        P("dp"),
        P("dp"),
        P(None, "dp", "tp"),
        P("tp", "dp", None),
        P("tp", "dp", None),
        P("tp", "dp"),
        P("dp", "tp"),
        P("tp", "dp"),
        P("dp"),
        P("dp", "tp"),
        P("tp", "dp"),
        P(("dp", "tp"), None),
        P("dp", None, "tp"),
    )
    return jax.shard_map(
        chosen,
        mesh=mesh,
        in_specs=placed,
        out_specs=(
            P(("dp", "tp"), None),
            P("dp", None, "tp"),
            P(("dp", "tp"), None),
            P("dp", None, "tp"),
            P("dp"),
            P(None, "dp", "tp"),
            P("tp", "dp", None),
            P("tp", "dp", None),
            P("tp", "dp"),
            P("dp", "tp"),
            P("tp", "dp"),
            P("dp"),
            P("dp", "tp"),
            P("tp", "dp"),
        ),
        check_vma=False,
    )
```

```python
import functools
import math

import jax
import jax.numpy as jnp
from jax import lax
from jax.experimental import pallas as pl
from jax.experimental.pallas import tpu as pltpu
from jax.sharding import PartitionSpec as P

S = 512
BLK = 512
LEN = 1536
NB = 3


EPSILON = 1e-06
NEGATIVE = -1e30


def rms_scale(values, gain):
    return values * lax.rsqrt(jnp.mean(values * values, axis=-1, keepdims=True) + EPSILON) * gain


def block_masks(block_id, length, block_len, state_count):
    row_ids = jnp.arange(block_len, dtype=jnp.int32)
    places = block_id * block_len + row_ids
    key_places = jnp.concatenate([places - block_len, places])
    allowed = (
        (key_places[None, :] >= 0)
        & (key_places[None, :] < length)
        & (key_places[None, :] <= places[:, None])
        & (key_places[None, :] > places[:, None] - block_len)
    )
    state_open = jnp.ones((block_len, state_count), dtype=bool)
    allowed = jnp.concatenate([allowed, state_open], axis=1)
    usable = jnp.concatenate([places < length, jnp.ones((state_count,), dtype=bool)])
    return (allowed, usable)


def masked_softmax(scores, allowed):
    scores = jnp.where(allowed, scores, NEGATIVE)
    peak_val = jnp.max(scores, axis=-1, keepdims=True)
    powers = jnp.exp(scores - peak_val)
    totals = jnp.sum(powers, axis=-1, keepdims=True)
    return (powers / totals, peak_val + jnp.log(totals))


def recall_softmax(scores, allowed, log_total):
    return jnp.exp(jnp.where(allowed, scores, NEGATIVE) - log_total)


def state_project(memory, state_weights):
    head_dim = memory.shape[-1]
    projected = jnp.einsum(
        "shd,hde->she",
        memory.astype(jnp.bfloat16),
        state_weights,
        preferred_element_type=jnp.float32,
    ).astype(jnp.bfloat16)
    return (
        projected[..., :head_dim],
        projected[..., head_dim : 2 * head_dim],
        projected[..., 2 * head_dim :],
    )


def block_forward(
    state_weights,
    update_weights,
    retain,
    memory,
    queries,
    keys_now,
    values_now,
    keys_before,
    values_before,
    block_id,
    length,
):
    head_dim = queries.shape[-1]
    block_len = queries.shape[0]
    state_count = memory.shape[0]
    scaling = head_dim ** (-0.5)
    state_q, state_k, state_v = state_project(memory, state_weights)
    allowed, usable = block_masks(block_id, length, block_len, state_count)
    key_set = jnp.concatenate([keys_before, keys_now, state_k], axis=0)
    value_set = jnp.concatenate([values_before, values_now, state_v], axis=0)
    scores = (
        jnp.einsum("ihd,jhd->hij", queries, key_set, preferred_element_type=jnp.float32) * scaling
    )
    shares, log_total = masked_softmax(scores, allowed[None])
    outputs = jnp.einsum(
        "hij,jhd->ihd", shares.astype(jnp.bfloat16), value_set, preferred_element_type=jnp.float32
    ).astype(jnp.bfloat16)
    state_keys = jnp.concatenate([keys_now, state_k], axis=0)
    state_values = jnp.concatenate([values_now, state_v], axis=0)
    state_scores = (
        jnp.einsum("shd,jhd->hsj", state_q, state_keys, preferred_element_type=jnp.float32)
        * scaling
    )
    state_shares, state_log = masked_softmax(state_scores, usable[None, None])
    state_out = jnp.einsum(
        "hsj,jhd->shd",
        state_shares.astype(jnp.bfloat16),
        state_values,
        preferred_element_type=jnp.float32,
    ).astype(jnp.bfloat16)
    update = jnp.einsum(
        "shd,hde->she", state_out, update_weights, preferred_element_type=jnp.float32
    )
    blended = retain * memory + (1.0 - retain) * update
    active = block_id * block_len < length
    memory_next = jnp.where(active, blended, memory)
    return (memory_next, (outputs, state_out, log_total, state_log))


def block_backward(
    state_weights,
    update_weights,
    retain,
    memory,
    queries,
    keys_now,
    values_now,
    keys_before,
    values_before,
    grad_out,
    state_out,
    log_total,
    state_log,
    block_id,
    length,
    grad_next,
):
    head_dim = queries.shape[-1]
    block_len = queries.shape[0]
    state_count = memory.shape[0]
    scaling = head_dim ** (-0.5)
    span_end = 2 * block_len
    state_q, state_k, state_v = state_project(memory, state_weights)
    allowed, usable = block_masks(block_id, length, block_len, state_count)
    active = block_id * block_len < length
    update = jnp.einsum(
        "shd,hde->she", state_out, update_weights, preferred_element_type=jnp.float32
    )
    grad_blend = jnp.where(active, grad_next, 0.0)
    grad_memory = jnp.where(active, retain * grad_next, grad_next)
    grad_update = ((1.0 - retain) * grad_blend).astype(jnp.bfloat16)
    grad_gate = jnp.sum(grad_blend * (memory - update), axis=0) * retain * (1.0 - retain)
    grad_update_w = jnp.einsum(
        "shd,she->hde", state_out, grad_update, preferred_element_type=jnp.float32
    )
    grad_state_out = jnp.einsum(
        "she,hde->shd", grad_update, update_weights, preferred_element_type=jnp.float32
    ).astype(jnp.bfloat16)
    state_keys = jnp.concatenate([keys_now, state_k], axis=0)
    state_values = jnp.concatenate([values_now, state_v], axis=0)
    state_scores = (
        jnp.einsum("shd,jhd->hsj", state_q, state_keys, preferred_element_type=jnp.float32)
        * scaling
    )
    state_shares = recall_softmax(state_scores, usable[None, None], state_log)
    grad_state_shares = jnp.einsum(
        "shd,jhd->hsj", grad_state_out, state_values, preferred_element_type=jnp.float32
    )
    grad_state_scores = (
        state_shares
        * (grad_state_shares - jnp.sum(state_shares * grad_state_shares, axis=-1, keepdims=True))
    ).astype(jnp.bfloat16)
    grad_state_values = jnp.einsum(
        "hsj,shd->jhd",
        state_shares.astype(jnp.bfloat16),
        grad_state_out,
        preferred_element_type=jnp.float32,
    )
    grad_state_q = (
        jnp.einsum(
            "hsj,jhd->shd", grad_state_scores, state_keys, preferred_element_type=jnp.float32
        )
        * scaling
    )
    grad_state_keys = (
        jnp.einsum("hsj,shd->jhd", grad_state_scores, state_q, preferred_element_type=jnp.float32)
        * scaling
    )
    key_set = jnp.concatenate([keys_before, keys_now, state_k], axis=0)
    value_set = jnp.concatenate([values_before, values_now, state_v], axis=0)
    scores = (
        jnp.einsum("ihd,jhd->hij", queries, key_set, preferred_element_type=jnp.float32) * scaling
    )
    shares = recall_softmax(scores, allowed[None], log_total)
    grad_shares = jnp.einsum(
        "ihd,jhd->hij", grad_out, value_set, preferred_element_type=jnp.float32
    )
    grad_scores = (
        shares * (grad_shares - jnp.sum(shares * grad_shares, axis=-1, keepdims=True))
    ).astype(jnp.bfloat16)
    grad_values = jnp.einsum(
        "hij,ihd->jhd", shares.astype(jnp.bfloat16), grad_out, preferred_element_type=jnp.float32
    )
    grad_queries = (
        jnp.einsum("hij,jhd->ihd", grad_scores, key_set, preferred_element_type=jnp.float32)
        * scaling
    )
    grad_keys = (
        jnp.einsum("hij,ihd->jhd", grad_scores, queries, preferred_element_type=jnp.float32)
        * scaling
    )
    grad_keys_now = grad_keys[block_len:span_end] + grad_state_keys[:block_len]
    grad_values_now = grad_values[block_len:span_end] + grad_state_values[:block_len]
    grad_state_k = grad_keys[span_end:] + grad_state_keys[block_len:]
    grad_state_v = grad_values[span_end:] + grad_state_values[block_len:]
    grad_proj = jnp.concatenate([grad_state_q, grad_state_k, grad_state_v], axis=-1).astype(
        jnp.bfloat16
    )
    grad_memory = grad_memory + jnp.einsum(
        "she,hde->shd", grad_proj, state_weights, preferred_element_type=jnp.float32
    )
    grad_state_w = jnp.einsum(
        "shd,she->hde", memory.astype(jnp.bfloat16), grad_proj, preferred_element_type=jnp.float32
    )
    return (
        grad_memory,
        grad_queries,
        grad_keys_now,
        grad_values_now,
        grad_keys[:block_len],
        grad_values[:block_len],
        grad_state_w,
        grad_update_w,
        grad_gate,
    )


def general_body(
    tokens,
    carried,
    restart,
    lengths,
    gain_attend,
    input_weights,
    state_weights,
    update_weights,
    gate_bias,
    initial_state,
    output_weights,
    gain_feed,
    feed_up,
    feed_down,
    grad_mixed,
    grad_final,
):
    seq_count = lengths.shape[0]
    heads_here = gate_bias.shape[0]
    head_dim = update_weights.shape[-1]
    width_here = heads_here * head_dim
    group_rows = seq_count * LEN
    gathered = (
        lax.all_gather(gain_attend, "dp", axis=0, tiled=True),
        lax.all_gather(gain_feed, "dp", axis=0, tiled=True),
        lax.all_gather(input_weights, "dp", axis=1, tiled=True),
        lax.all_gather(output_weights, "dp", axis=1, tiled=True),
        lax.all_gather(state_weights, "dp", axis=1, tiled=True),
        lax.all_gather(update_weights, "dp", axis=1, tiled=True),
        lax.all_gather(gate_bias, "dp", axis=1, tiled=True),
        lax.all_gather(initial_state, "dp", axis=0, tiled=True),
        lax.all_gather(feed_up, "dp", axis=0, tiled=True),
        lax.all_gather(feed_down, "dp", axis=1, tiled=True),
    )
    (
        gain_attend_all,
        gain_feed_all,
        input_all,
        output_all,
        state_all,
        update_all,
        gate_all,
        initial_all,
        up_all,
        down_all,
    ) = gathered
    tokens_wide = tokens.astype(jnp.float32)
    gain_one = gain_attend_all.astype(jnp.float32)
    gain_two = gain_feed_all.astype(jnp.float32)
    normed = rms_scale(tokens_wide, gain_one).astype(jnp.bfloat16)
    normed_all = lax.all_gather(normed, "tp", axis=0, tiled=True)
    projected = jnp.einsum(
        "rd,kdc->krc", normed_all, input_all, preferred_element_type=jnp.float32
    ).astype(jnp.bfloat16)
    blocked = jnp.moveaxis(projected.reshape(3, seq_count, NB, BLK, heads_here, head_dim), 2, 1)
    earlier = jnp.concatenate([jnp.zeros_like(blocked[:, :1]), blocked[:, :-1]], axis=1)
    retain = jax.nn.sigmoid(gate_all.astype(jnp.float32))
    memory_start = jnp.where(
        restart[:, None, None] > 0, initial_all.astype(jnp.float32)[None], carried
    ).reshape(seq_count, S, heads_here, head_dim)
    forward_block = jax.vmap(block_forward, in_axes=(None, None, None, 0, 0, 0, 0, 0, 0, None, 0))
    block_ids = jnp.arange(NB, dtype=jnp.int32)

    def forward_step(memory, entries):
        queries, keys_now, values_now, keys_before, values_before, block_id = entries
        memory_next, saved = forward_block(
            state_all,
            update_all,
            retain,
            memory,
            queries,
            keys_now,
            values_now,
            keys_before,
            values_before,
            block_id,
            lengths,
        )
        return (memory_next, (memory, saved))

    memory_end, (memories, saved_all) = lax.scan(
        forward_step,
        memory_start,
        (blocked[0], blocked[1], blocked[2], earlier[1], earlier[2], block_ids),
    )
    outputs, state_outs, log_totals, state_logs = saved_all
    attended = jnp.moveaxis(outputs, 0, 1).reshape(group_rows, width_here)
    middle = tokens_wide + lax.psum_scatter(
        jnp.dot(attended, output_all, preferred_element_type=jnp.float32),
        "tp",
        scatter_dimension=0,
        tiled=True,
    )
    normed_mid = rms_scale(middle, gain_two).astype(jnp.bfloat16)
    mid_all = lax.all_gather(normed_mid, "tp", axis=0, tiled=True)
    hidden_pre = jnp.dot(mid_all, up_all, preferred_element_type=jnp.float32)
    hidden = jax.nn.gelu(hidden_pre).astype(jnp.bfloat16)
    mixed = middle + lax.psum_scatter(
        jnp.dot(hidden, down_all, preferred_element_type=jnp.float32),
        "tp",
        scatter_dimension=0,
        tiled=True,
    )
    grad_rows = lax.all_gather(grad_mixed, "tp", axis=0, tiled=True)
    grad_hidden = jnp.einsum("rd,fd->rf", grad_rows, down_all, preferred_element_type=jnp.float32)
    grad_pre = jax.vjp(jax.nn.gelu, hidden_pre)[1](grad_hidden)[0].astype(jnp.bfloat16)
    grad_down = jnp.einsum("rf,rd->fd", hidden, grad_rows, preferred_element_type=jnp.float32)
    grad_up = jnp.einsum("rd,rf->df", mid_all, grad_pre, preferred_element_type=jnp.float32)
    grad_mid_normed = lax.psum_scatter(
        jnp.einsum("rf,df->rd", grad_pre, up_all, preferred_element_type=jnp.float32),
        "tp",
        scatter_dimension=0,
        tiled=True,
    )
    grad_middle_part, grad_gain_two = jax.vjp(rms_scale, middle, gain_two)[1](grad_mid_normed)
    grad_middle = grad_mixed.astype(jnp.float32) + grad_middle_part
    grad_branch = lax.all_gather(grad_middle.astype(jnp.bfloat16), "tp", axis=0, tiled=True)
    grad_output = jnp.einsum("rc,rd->cd", attended, grad_branch, preferred_element_type=jnp.float32)
    grad_attended = jnp.einsum(
        "rd,cd->rc", grad_branch, output_all, preferred_element_type=jnp.float32
    ).astype(jnp.bfloat16)
    grad_blocks = jnp.moveaxis(
        grad_attended.reshape(seq_count, NB, BLK, heads_here, head_dim), 1, 0
    )
    backward_block = jax.vmap(
        block_backward, in_axes=(None, None, None, 0, 0, 0, 0, 0, 0, 0, 0, 0, 0, None, 0, 0)
    )

    def backward_step(carried_in, entries):
        grad_memory, keys_later, values_later, sum_state, sum_update, sum_gate = carried_in
        (
            memory,
            queries,
            keys_now,
            values_now,
            keys_before,
            values_before,
            grad_out,
            state_out,
            log_total,
            state_log,
            block_id,
        ) = entries
        results = backward_block(
            state_all,
            update_all,
            retain,
            memory,
            queries,
            keys_now,
            values_now,
            keys_before,
            values_before,
            grad_out,
            state_out,
            log_total,
            state_log,
            block_id,
            lengths,
            grad_memory,
        )
        (
            grad_prior,
            grad_queries,
            grad_keys,
            grad_values,
            grad_keys_before,
            grad_values_before,
            part_state,
            part_update,
            part_gate,
        ) = results
        carried_out = (
            grad_prior,
            grad_keys_before,
            grad_values_before,
            sum_state + jnp.sum(part_state, axis=0),
            sum_update + jnp.sum(part_update, axis=0),
            sum_gate + jnp.sum(part_gate, axis=0),
        )
        return (carried_out, (grad_queries, grad_keys + keys_later, grad_values + values_later))

    zero_block = jnp.zeros((seq_count, BLK, heads_here, head_dim), jnp.float32)
    start_carry = (
        grad_final.astype(jnp.float32).reshape(seq_count, S, heads_here, head_dim),
        zero_block,
        zero_block,
        jnp.zeros(state_all.shape, jnp.float32),
        jnp.zeros(update_all.shape, jnp.float32),
        jnp.zeros(retain.shape, jnp.float32),
    )
    final_carry, grad_parts = lax.scan(
        backward_step,
        start_carry,
        (
            memories,
            blocked[0],
            blocked[1],
            blocked[2],
            earlier[1],
            earlier[2],
            grad_blocks,
            state_outs,
            log_totals,
            state_logs,
            block_ids,
        ),
        reverse=True,
    )
    grad_memory_start, unused_keys, unused_values, grad_state_w, grad_update_w, grad_gate_w = (
        final_carry
    )
    grad_qkv = jnp.stack(
        [jnp.moveaxis(member, 0, 1).reshape(group_rows, width_here) for member in grad_parts]
    ).astype(jnp.bfloat16)
    grad_memory_start = grad_memory_start.reshape(seq_count, S, width_here)
    restarted = restart[:, None, None] > 0
    grad_carried = jnp.where(restarted, 0.0, grad_memory_start)
    grad_initial = jnp.sum(jnp.where(restarted, grad_memory_start, 0.0), axis=0)
    grad_input = jnp.einsum("rd,krc->kdc", normed_all, grad_qkv, preferred_element_type=jnp.float32)
    grad_normed = lax.psum_scatter(
        jnp.einsum("krc,kdc->rd", grad_qkv, input_all, preferred_element_type=jnp.float32),
        "tp",
        scatter_dimension=0,
        tiled=True,
    )
    grad_tokens_part, grad_gain_one = jax.vjp(rms_scale, tokens_wide, gain_one)[1](grad_normed)
    grad_tokens = grad_middle + grad_tokens_part
    gain_one_sum, gain_two_sum = lax.psum((grad_gain_one, grad_gain_two), "tp")
    summed = (
        lax.psum_scatter(gain_one_sum, "dp", scatter_dimension=0, tiled=True),
        lax.psum_scatter(gain_two_sum, "dp", scatter_dimension=0, tiled=True),
        lax.psum_scatter(grad_input, "dp", scatter_dimension=1, tiled=True),
        lax.psum_scatter(grad_output, "dp", scatter_dimension=1, tiled=True),
        lax.psum_scatter(grad_state_w, "dp", scatter_dimension=1, tiled=True),
        lax.psum_scatter(grad_update_w, "dp", scatter_dimension=1, tiled=True),
        lax.psum_scatter(grad_gate_w, "dp", scatter_dimension=1, tiled=True),
        lax.psum_scatter(grad_initial, "dp", scatter_dimension=0, tiled=True),
        lax.psum_scatter(grad_up, "dp", scatter_dimension=0, tiled=True),
        lax.psum_scatter(grad_down, "dp", scatter_dimension=1, tiled=True),
    )
    (
        out_gain_one,
        out_gain_two,
        out_input,
        out_output,
        out_state,
        out_update,
        out_gate,
        out_initial,
        out_up,
        out_down,
    ) = summed
    return (
        mixed.astype(jnp.bfloat16),
        memory_end.reshape(seq_count, S, width_here),
        grad_tokens,
        grad_carried,
        out_gain_one,
        out_input,
        out_state,
        out_update,
        out_gate,
        out_initial,
        out_output,
        out_gain_two,
        out_up,
        out_down,
    )


BF16 = jnp.bfloat16
F32 = jnp.float32
HD = 128
TILE = 256
LOG2E = math.log2(math.e)
SCALING = HD ** (-0.5)
TO_POWER = SCALING * LOG2E
VMEM_BYTES = 60 * 1024 * 1024


def dot_nn(left, right):
    return jnp.dot(left, right, preferred_element_type=F32)


def dot_nt(left, right):
    return lax.dot_general(left, right, (((1,), (1,)), ((), ())), preferred_element_type=F32)


def call_params(**more):
    return pltpu.CompilerParams(vmem_limit_bytes=VMEM_BYTES, **more)


def cost(macs, moved, powers=0):
    return pl.CostEstimate(flops=2 * macs, bytes_accessed=moved, transcendentals=powers)


def whole(shape):
    return pl.BlockSpec(shape, lambda *_: (0,) * len(shape), pipeline_mode=pl.Buffered(1))


def project_kernel(x_ref, gain_ref, w_ref, normed_t_ref, out_ref, w_full):
    depth = w_ref.shape[1] // 3

    @pl.when(pl.program_id(0) == 0)
    def _():
        for i in range(3):
            part = w_ref[:, i * depth : (i + 1) * depth]
            w_full[i] = part.reshape(w_full.shape[1:])

    x = x_ref[...].astype(F32)
    scale = lax.rsqrt(jnp.mean(x * x, axis=-1, keepdims=True) + EPSILON)
    normed = (x * scale * gain_ref[...]).astype(BF16)
    normed_t_ref[...] = normed.T
    for i in range(3):
        out_ref[i] = dot_nn(normed, w_full[i]).astype(BF16)


def project(x, gain, packs, depth):
    rows, width = x.shape
    cols = packs.shape[2]
    return pl.pallas_call(
        project_kernel,
        grid=(rows // TILE,),
        in_specs=[
            pl.BlockSpec((TILE, width), lambda r: (r, 0)),
            whole((1, width)),
            whole((packs.shape[0], 3 * depth, cols)),
        ],
        out_specs=[
            pl.BlockSpec((width, TILE), lambda r: (0, r)),
            pl.BlockSpec((3, TILE, cols), lambda r: (0, r, 0)),
        ],
        out_shape=[
            jax.ShapeDtypeStruct((width, rows), BF16),
            jax.ShapeDtypeStruct((3, rows, cols), BF16),
        ],
        scratch_shapes=[pltpu.VMEM((3, width, cols), BF16)],
        compiler_params=call_params(),
        cost_estimate=cost(rows * width * 3 * cols, 6 * rows * width),
        name="project",
    )(x, gain, packs)


def tile_masks():
    key = lax.broadcasted_iota(jnp.int32, (TILE, TILE), 0)
    query = lax.broadcasted_iota(jnp.int32, (TILE, TILE), 1)
    return key, query


def token_tiles(t):
    return [(j, t - j) for j in range(max(0, t - 2), t + 1)]


def masked_scores(scores, tile, behind, length, key, query):
    if behind == 0:
        scores = jnp.where(key <= query, scores, NEGATIVE)
    elif behind == 2:
        scores = jnp.where(key > query, scores, NEGATIVE)
    if tile >= 2 * (NB - 1):
        scores = jnp.where(key + tile * TILE < length, scores, NEGATIVE)
    return scores


def softmax_columns(tiles):
    peak = functools.reduce(jnp.maximum, [jnp.max(s, axis=0, keepdims=True) for s in tiles])
    peak = peak * TO_POWER
    powers = [jnp.exp2(s * TO_POWER - peak) for s in tiles]
    total = functools.reduce(jnp.add, [jnp.sum(p, axis=0, keepdims=True) for p in powers])
    return [p.astype(BF16) for p in powers], total, peak + jnp.log2(total)


def first_memory(flags_ref, carried_ref, initial_ref):
    initial = initial_ref[...].reshape(carried_ref.shape).astype(F32)
    return jnp.where(flags_ref[0, 0] > 0, initial, carried_ref[...])


def attend_kernel(
    flags_ref,
    q_ref,
    k_ref,
    v_ref,
    carried_ref,
    initial_ref,
    ws_ref,
    wu_ref,
    gate_ref,
    out_ref,
    state_out_ref,
    log_ref,
    state_log_ref,
    final_ref,
    vt_ref,
):
    length = flags_ref[0, 1]
    key, query = tile_masks()
    retain = jax.nn.sigmoid(gate_ref[0])
    memory = first_memory(flags_ref, carried_ref, initial_ref)
    vt_ref[...] = v_ref[0].T
    for c in range(NB):
        lo = c * BLK
        state = dot_nn(memory.astype(BF16), ws_ref[0]).astype(BF16)
        sq, sk, sv = state[:, :HD], state[:, HD : 2 * HD], state[:, 2 * HD :]
        svt = sv.T
        for t in range(2 * c, 2 * c + 2):
            rows = slice(t * TILE, (t + 1) * TILE)
            q = q_ref[0, rows]
            spans = token_tiles(t)
            tiles = [
                masked_scores(
                    dot_nt(k_ref[0, j * TILE : (j + 1) * TILE], q), j, behind, length, key, query
                )
                for j, behind in spans
            ]
            tiles.append(dot_nt(sk, q))
            powers, total, logs = softmax_columns(tiles)
            first = spans[0][0] * TILE
            out = dot_nn(vt_ref[:, first : (t + 1) * TILE], jnp.concatenate(powers[:-1], axis=0))
            out = out + dot_nn(svt, powers[-1])
            out_ref[rows] = (out / total).T.astype(BF16)
            log_ref[0, :, rows] = logs
        for u in range(2):
            part = slice(u * TILE, (u + 1) * TILE)
            q = sq[part]
            tiles = []
            for j in range(2):
                s = dot_nt(k_ref[0, lo + j * TILE : lo + (j + 1) * TILE], q)
                if c == NB - 1:
                    s = jnp.where(key + (lo + j * TILE) < length, s, NEGATIVE)
                tiles.append(s)
            tiles.append(dot_nt(sk, q))
            powers, total, logs = softmax_columns(tiles)
            out = dot_nn(vt_ref[:, lo : lo + BLK], jnp.concatenate(powers[:-1], axis=0))
            out = out + dot_nn(svt, powers[-1])
            rows = slice(lo + u * TILE, lo + (u + 1) * TILE)
            state_out_ref[rows] = (out / total).T.astype(BF16)
            state_log_ref[0, :, rows] = logs
        update = dot_nn(state_out_ref[lo : lo + BLK], wu_ref[0])
        blended = retain * memory + (1.0 - retain) * update
        memory = jnp.where(lo < length, blended, memory)
    final_ref[...] = memory


def head_block(rows):
    return pl.BlockSpec((rows, HD), lambda h: (0, h))


def initial_block(packs, at, first=0):
    length = S // packs.shape[0]
    return pl.BlockSpec((packs.shape[0], length, HD), lambda h: (0, at // length, first + h))


def attend(flags, projected, carried, packs, initial_at, states, gate):
    rows = projected.shape[1]
    heads = states.shape[0]
    return pl.pallas_call(
        attend_kernel,
        grid=(heads,),
        in_specs=[
            pl.BlockSpec(memory_space=pltpu.SMEM),
            pl.BlockSpec((1, rows, HD), lambda h: (0, 0, h)),
            pl.BlockSpec((1, rows, HD), lambda h: (1, 0, h)),
            pl.BlockSpec((1, rows, HD), lambda h: (2, 0, h)),
            head_block(S),
            initial_block(packs, initial_at),
            pl.BlockSpec((1, HD, 3 * HD), lambda h: (h, 0, 0)),
            pl.BlockSpec((1, HD, HD), lambda h: (h, 0, 3)),
            pl.BlockSpec((1, 1, HD), lambda h: (h, 0, 0)),
        ],
        out_specs=[
            head_block(rows),
            head_block(NB * S),
            pl.BlockSpec((1, 1, rows), lambda h: (h, 0, 0)),
            pl.BlockSpec((1, 1, NB * S), lambda h: (h, 0, 0)),
            head_block(S),
        ],
        out_shape=[
            jax.ShapeDtypeStruct((rows, heads * HD), BF16),
            jax.ShapeDtypeStruct((NB * S, heads * HD), BF16),
            jax.ShapeDtypeStruct((heads, 1, rows), F32),
            jax.ShapeDtypeStruct((heads, 1, NB * S), F32),
            jax.ShapeDtypeStruct((S, heads * HD), F32),
        ],
        scratch_shapes=[pltpu.VMEM((HD, rows), BF16)],
        compiler_params=call_params(),
        cost_estimate=cost(
            heads * NB * BLK * HD * 2 * (1152 + 1024),
            heads * HD * (rows * 10 + S * 8),
            heads * NB * BLK * 2176,
        ),
        name="attend",
    )(flags, projected, projected, projected, carried, packs, states, states, gate)


def attend_back_kernel(
    spots,
    flags_ref,
    q_ref,
    k_ref,
    v_ref,
    carried_ref,
    initial_ref,
    ws_ref,
    wu_ref,
    gate_ref,
    out_ref,
    state_out_ref,
    log_ref,
    state_log_ref,
    go_ref,
    grad_final_ref,
    nt_ref,
    w_ref,
    *refs,
):
    kt_ref, dk_ref, dv_ref, dqkv_ref, acc_ref = refs[-5:]
    last = len(refs) > 12
    if last:
        core_ref, x_ref, sum_ref = refs[:3]
        dws_ref, dwu_ref, dgate_ref, dmemory_ref, dw_ref, own_ref, give_ref, dgain_ref = refs[3:-5]
    else:
        dwo_ref, dws_ref, dwu_ref, dgate_ref, dmemory_ref, dw_ref, out_gy_ref = refs[:-5]
    step = pl.program_id(0)

    @pl.when(step == 0)
    def _():
        acc_ref[...] = sum_ref[...].astype(F32) if last else jnp.zeros_like(acc_ref)

    length = flags_ref[0, 1]
    key, query = tile_masks()
    retain = jax.nn.sigmoid(gate_ref[0])
    ws = ws_ref[0]
    wu = wu_ref[0]
    kt_ref[...] = k_ref[0].T
    dk_ref[...] = jnp.zeros_like(dk_ref)
    dv_ref[...] = jnp.zeros_like(dv_ref)
    memories = [first_memory(flags_ref, carried_ref, initial_ref)]
    for c in range(NB - 1):
        update = dot_nn(state_out_ref[c * S : (c + 1) * S], wu)
        blended = retain * memories[c] + (1.0 - retain) * update
        memories.append(jnp.where(c * BLK < length, blended, memories[c]))
    grad_memory = grad_final_ref[...].astype(F32)
    dws = jnp.zeros(ws.shape, F32)
    dwu = jnp.zeros(wu.shape, F32)
    dgate = jnp.zeros(retain.shape, F32)
    for c in reversed(range(NB)):
        lo = c * BLK
        active = lo < length
        memory = memories[c]
        memory_low = memory.astype(BF16)
        state = dot_nn(memory_low, ws).astype(BF16)
        sq, sk, sv = state[:, :HD], state[:, HD : 2 * HD], state[:, 2 * HD :]
        skt = sk.T
        state_out = state_out_ref[lo : lo + S]
        update = dot_nn(state_out, wu)
        grad_blend = jnp.where(active, grad_memory, 0.0)
        grad_update = ((1.0 - retain) * grad_blend).astype(BF16)
        dgate = dgate + jnp.sum(grad_blend * (memory - update), axis=0, keepdims=True)
        dwu = dwu + dot_nn(state_out.T, grad_update)
        grad_state_out = dot_nt(grad_update, wu).astype(BF16)
        grad_memory = jnp.where(active, retain * grad_memory, grad_memory)
        deltas = jnp.sum((grad_state_out.astype(F32) * state_out.astype(F32)).T, axis=0, keepdims=True)
        dsk = jnp.zeros((S, HD), F32)
        dsv = jnp.zeros((S, HD), F32)
        dsq = []
        for u in range(2):
            part = slice(u * TILE, (u + 1) * TILE)
            q = sq[part]
            go = grad_state_out[part]
            logs = state_log_ref[0, :, lo + u * TILE : lo + (u + 1) * TILE]
            delta = deltas[:, part]
            dq = jnp.zeros((HD, TILE), F32)
            for j in range(2):
                rows = slice(lo + j * TILE, lo + (j + 1) * TILE)
                s = dot_nt(k_ref[0, rows], q)
                if c == NB - 1:
                    s = jnp.where(key + (lo + j * TILE) < length, s, NEGATIVE)
                p = jnp.exp2(s * TO_POWER - logs)
                ds = (p * (dot_nt(v_ref[0, rows], go) - delta)).astype(BF16)
                dv_ref[rows] += dot_nn(p.astype(BF16), go)
                dk_ref[rows] += dot_nn(ds, q)
                dq = dq + dot_nn(kt_ref[:, rows], ds)
            p = jnp.exp2(dot_nt(sk, q) * TO_POWER - logs)
            ds = (p * (dot_nt(sv, go) - delta)).astype(BF16)
            dsv = dsv + dot_nn(p.astype(BF16), go)
            dsk = dsk + dot_nn(ds, q)
            dq = dq + dot_nn(skt, ds)
            dsq.append(dq.T)
        for t in range(2 * c, 2 * c + 2):
            here = slice(t * TILE, (t + 1) * TILE)
            q = q_ref[0, here]
            go = go_ref[here]
            logs = log_ref[0, :, here]
            delta = jnp.sum((go.astype(F32) * out_ref[here].astype(F32)).T, axis=0, keepdims=True)
            dq = jnp.zeros((HD, TILE), F32)
            for j, behind in token_tiles(t):
                rows = slice(j * TILE, (j + 1) * TILE)
                s = masked_scores(dot_nt(k_ref[0, rows], q), j, behind, length, key, query)
                p = jnp.exp2(s * TO_POWER - logs)
                ds = (p * (dot_nt(v_ref[0, rows], go) - delta)).astype(BF16)
                dv_ref[rows] += dot_nn(p.astype(BF16), go)
                dk_ref[rows] += dot_nn(ds, q)
                dq = dq + dot_nn(kt_ref[:, rows], ds)
            p = jnp.exp2(dot_nt(sk, q) * TO_POWER - logs)
            ds = (p * (dot_nt(sv, go) - delta)).astype(BF16)
            dsv = dsv + dot_nn(p.astype(BF16), go)
            dsk = dsk + dot_nn(ds, q)
            dq = dq + dot_nn(skt, ds)
            dqkv_ref[here, :HD] = (dq.T * SCALING).astype(BF16)
        grad_state = jnp.concatenate(
            [jnp.concatenate(dsq, axis=0) * SCALING, dsk * SCALING, dsv], axis=1
        ).astype(BF16)
        grad_memory = grad_memory + dot_nt(grad_state, ws)
        dws = dws + dot_nn(memory_low.T, grad_state)
    dqkv_ref[:, HD : 2 * HD] = (dk_ref[...] * SCALING).astype(BF16)
    dqkv_ref[:, 2 * HD :] = dv_ref[...].astype(BF16)
    dws_ref[0] = dws
    dwu_ref[0] = dwu
    dgate_ref[0] = dgate * retain * (1.0 - retain)
    dmemory_ref[...] = grad_memory
    depth = w_ref.shape[1] // 3
    wide = dqkv_ref[...]
    weights = jnp.concatenate(
        [w_ref[:, i * depth : (i + 1) * depth].reshape(nt_ref.shape[0], HD) for i in range(3)],
        axis=1,
    )
    acc_ref[...] += dot_nt(wide, weights)
    product = dot_nn(nt_ref[...], wide).astype(BF16)
    low = depth // 2
    for i in range(3):
        for block in range(w_ref.shape[0]):
            at = (spots[block // 2], block % 2, slice(i * low, (i + 1) * low))
            piece = product[block * depth : (block + 1) * depth, i * HD : (i + 1) * HD]
            dw_ref[at + (slice(0, HD),)] = piece[:low]
            dw_ref[at + (slice(HD, 2 * HD),)] = piece[low:]
    if not last:
        dw_ref[:, :, 3 * low :] = dwo_ref[...]

    @pl.when(step == pl.num_programs(0) - 1)
    def _():
        if not last:
            out_gy_ref[...] = acc_ref[...].astype(BF16)
            return
        half = own_ref.shape[0]
        core = core_ref[0]
        own = pl.ds(pl.multiple_of(core * half, half), half)
        give = pl.ds(pl.multiple_of((1 - core) * half, half), half)
        own_ref[...] = acc_ref[own, :].astype(BF16)
        give_ref[...] = acc_ref[give, :].astype(BF16)
        dgain = jnp.zeros_like(dgain_ref)
        for r in range(acc_ref.shape[0] // TILE):
            rows = slice(r * TILE, (r + 1) * TILE)
            x = x_ref[rows].astype(F32)
            scale = lax.rsqrt(jnp.mean(x * x, axis=-1, keepdims=True) + EPSILON)
            dgain = dgain + jnp.sum(acc_ref[rows] * x * scale, axis=0, keepdims=True)
        dgain_ref[...] = dgain


def attend_back(
    first,
    heads,
    spots,
    flags,
    projected,
    carried,
    packs,
    initial_at,
    states,
    gate,
    out,
    state_out,
    logs,
    state_logs,
    go,
    grad_final,
    normed_t,
    depth,
    dwo=None,
    more=(),
):
    rows = projected.shape[1]
    width = normed_t.shape[0]
    slices = packs.shape[0]
    chips = slices // 2
    per_head = lambda a, b: pl.BlockSpec((1, a, b), lambda h: (first + h, 0, 0))
    new_head = lambda a, b: pl.BlockSpec((1, a, b), lambda h: (h, 0, 0))
    in_head = lambda rows: pl.BlockSpec((rows, HD), lambda h: (0, first + h))
    part = lambda i: pl.BlockSpec((1, rows, HD), lambda h: (i, 0, first + h))
    lanes = 2 * HD
    piece = lambda rows: pl.BlockSpec((chips, 2, rows, lanes), lambda h: (0, 0, 0, h))
    shape = jax.ShapeDtypeStruct
    low = 3 * (depth // 2)
    if more:
        extra = [pl.BlockSpec(memory_space=pltpu.SMEM)] + [whole((rows, width))] * 2
        operands = more
        outs = [shape((rows // 2, width), BF16)] * 2 + [shape((1, width), F32)]
    else:
        extra = [piece(dwo.shape[2])]
        operands = (dwo,)
        low += dwo.shape[2]
        outs = [shape((rows, width), BF16)]
    return pl.pallas_call(
        functools.partial(attend_back_kernel, spots),
        grid=(heads,),
        in_specs=[
            pl.BlockSpec(memory_space=pltpu.SMEM),
            part(0),
            part(1),
            part(2),
            in_head(S),
            initial_block(packs, initial_at, first),
            per_head(HD, 3 * HD),
            pl.BlockSpec((1, HD, HD), lambda h: (first + h, 0, 3)),
            per_head(1, HD),
            in_head(rows),
            in_head(NB * S),
            per_head(1, rows),
            per_head(1, NB * S),
            in_head(rows),
            in_head(S),
            whole(normed_t.shape),
            pl.BlockSpec((slices, 3 * depth, HD), lambda h: (0, 0, first + h)),
        ]
        + extra,
        out_specs=[
            new_head(HD, 3 * HD),
            new_head(HD, HD),
            new_head(1, HD),
            head_block(S),
            piece(low),
        ]
        + [whole(v.shape) for v in outs],
        out_shape=[
            shape((heads, HD, 3 * HD), F32),
            shape((heads, HD, HD), F32),
            shape((heads, 1, HD), F32),
            shape((S, heads * HD), F32),
            shape((chips, 2, low, heads * lanes), BF16),
        ]
        + outs,
        scratch_shapes=[
            pltpu.VMEM((HD, rows), BF16),
            pltpu.VMEM((rows, HD), F32),
            pltpu.VMEM((rows, HD), F32),
            pltpu.VMEM((rows, 3 * HD), BF16),
            pltpu.VMEM((rows, width), F32),
        ],
        compiler_params=call_params(),
        cost_estimate=cost(
            heads * NB * BLK * HD * (5 * (1152 + 1024) + 6 * width),
            heads * HD * (rows * 20 + S * 16) + 8 * rows * width,
            heads * NB * BLK * 2176,
        ),
        name="attend_back",
    )(
        flags,
        projected,
        projected,
        projected,
        carried,
        packs,
        states,
        states,
        gate,
        out,
        state_out,
        logs,
        state_logs,
        go,
        grad_final,
        normed_t,
        packs,
        *operands,
    )


def middle_kernel(
    core_ref,
    x_ref,
    own_ref,
    sib_ref,
    wo_own_ref,
    wo_sib_ref,
    gain_ref,
    g_own_ref,
    g_sib_ref,
    mid_ref,
    n_ref,
    nt_ref,
    g_ref,
    gt_ref,
):
    mine = pl.program_id(0) * 2 // pl.num_programs(0) == core_ref[0]
    g = jnp.where(mine, g_own_ref[...], g_sib_ref[...])
    g_ref[...] = g
    gt_ref[...] = g.T
    middle = x_ref[...].astype(F32) + dot_nt(own_ref[...], wo_own_ref[...])
    middle = middle + dot_nt(sib_ref[...], wo_sib_ref[...])
    scale = lax.rsqrt(jnp.mean(middle * middle, axis=-1, keepdims=True) + EPSILON)
    normed = (middle * scale * gain_ref[...]).astype(BF16)
    mid_ref[...] = middle
    n_ref[...] = normed
    nt_ref[...] = normed.T


def form_middle(core, x, own, sib, wo_own, wo_sib, gain, g_own, g_sib):
    rows, width = x.shape
    half = own.shape[1]
    row_block = lambda cols: pl.BlockSpec((TILE, cols), lambda r: (r, 0))
    col_block = pl.BlockSpec((width, TILE), lambda r: (0, r))
    half_tiles = rows // TILE // 2
    half_block = pl.BlockSpec((TILE, width), lambda r: (r % half_tiles, 0))
    return pl.pallas_call(
        middle_kernel,
        grid=(rows // TILE,),
        in_specs=[
            pl.BlockSpec(memory_space=pltpu.SMEM),
            row_block(width),
            row_block(half),
            row_block(half),
            whole(wo_own.shape),
            whole(wo_sib.shape),
            whole(gain.shape),
            half_block,
            half_block,
        ],
        out_specs=[row_block(width), row_block(width), col_block, row_block(width), col_block],
        out_shape=[
            jax.ShapeDtypeStruct((rows, width), F32),
            jax.ShapeDtypeStruct((rows, width), BF16),
            jax.ShapeDtypeStruct((width, rows), BF16),
            jax.ShapeDtypeStruct((rows, width), BF16),
            jax.ShapeDtypeStruct((width, rows), BF16),
        ],
        compiler_params=call_params(),
        cost_estimate=cost(2 * rows * width * half, 12 * rows * width),
        name="form_middle",
    )(core, x, own, sib, wo_own, wo_sib, gain, g_own, g_sib)


ROOT = math.sqrt(2.0 / math.pi)
CUBIC = 0.044715


def feed_kernel(
    place, spots, core_ref, n_ref, nt_ref, g_ref, gt_ref, up_ref, dn_ref, *refs
):
    last = len(refs) > 6
    if last:
        ff_in, gn_in, ff_out, gn_out, dw_ref = refs[:5]
    else:
        ff_out, gn_out, dw_ref = refs[:3]
    w_full, hid_ref, grad_ref = refs[-3:]
    step = pl.program_id(0)
    depth = dw_ref.shape[3]

    @pl.when(step == 0)
    def _():
        for i, ref in enumerate((up_ref, dn_ref)):
            for block, p in enumerate(spots):
                w_full[i, block * depth : (block + 1) * depth] = ref[p]

    up = w_full[0]
    dn = w_full[1]
    here = pl.ds(pl.multiple_of(step * n_ref.shape[0], TILE), n_ref.shape[0])
    pre = dot_nn(n_ref[...], up)
    square = pre * pre
    bend = jnp.tanh(ROOT * pre * (1.0 + CUBIC * square))
    half = 0.5 * (1.0 + bend)
    hid = (pre * half).astype(BF16)
    slope = half + (0.5 * ROOT) * pre * (1.0 - bend * bend) * (1.0 + 3.0 * CUBIC * square)
    grad = (dot_nn(g_ref[...], dn) * slope).astype(BF16)
    hid_ref[here, :] = hid
    grad_ref[here, :] = grad
    ff = dot_nt(hid, dn)
    gn = dot_nt(grad, up)
    if last:
        ff = ff + ff_in[...].astype(F32)
        gn = gn + gn_in[...].astype(F32)
    ff_out[...] = ff.astype(BF16)
    gn_out[...] = gn.astype(BF16)

    @pl.when(step == pl.num_programs(0) - 1)
    def _():
        for i, (left, right) in enumerate(((nt_ref, grad_ref), (gt_ref, hid_ref))):
            for at in range(0, left.shape[0], TILE):
                product = dot_nn(left[at : at + TILE], right[...]).astype(BF16)
                for t in range(TILE // depth):
                    block = at // depth + t
                    piece = product[t * depth : (t + 1) * depth]
                    dw_ref[place[block // 2], block % 2, i] = piece


def feed(place, spots, core, normed, normed_t, grad, grad_t, weights, units, sums=()):
    rows, width = normed.shape
    pieces, depth = weights.shape[:2]
    row_block = pl.BlockSpec((TILE, width), lambda r: (r, 0))
    piece_block = lambda at: pl.BlockSpec(
        (pieces, depth, units), lambda r: (0, 0, at), pipeline_mode=pl.Buffered(1)
    )
    grad_shape = jax.ShapeDtypeStruct((pieces // 2, 2, 2, depth, units), BF16)
    full = jax.ShapeDtypeStruct((rows, width), BF16)
    return pl.pallas_call(
        functools.partial(feed_kernel, place, spots),
        grid=(rows // TILE,),
        in_specs=[
            pl.BlockSpec(memory_space=pltpu.SMEM),
            row_block,
            whole(normed_t.shape),
            row_block,
            whole(grad_t.shape),
            piece_block(0),
            piece_block(1),
        ]
        + [row_block for _ in sums],
        out_specs=[row_block, row_block, whole(grad_shape.shape)],
        out_shape=[full, full, grad_shape],
        scratch_shapes=[
            pltpu.VMEM((2, width, units), BF16),
            pltpu.VMEM((rows, units), BF16),
            pltpu.VMEM((rows, units), BF16),
        ],
        compiler_params=call_params(),
        cost_estimate=cost(
            6 * rows * width * units, 14 * rows * width + 8 * width * units, rows * units
        ),
        name="feed",
    )(core, normed, normed_t, grad, grad_t, weights, weights, *sums)


def norm_back(values, gain, grad):
    scale = lax.rsqrt(jnp.mean(values * values, axis=-1, keepdims=True) + EPSILON)
    weighted = grad * gain
    mean = jnp.mean(values * weighted, axis=-1, keepdims=True)
    out = scale * weighted - values * (scale * scale * scale * mean)
    return out, jnp.sum(grad * values * scale, axis=0, keepdims=True)


def middle_back_kernel(
    place, g_ref, mid_ref, own_ref, sib_ref, gain_ref, wo_ref, att_ref, gm_ref, ga_ref, dwo_ref, dgain_ref, acc
):
    step = pl.program_id(0)
    gy = own_ref[...].astype(F32) + sib_ref[...].astype(F32)
    back, dgain = norm_back(mid_ref[...], gain_ref[...], gy)
    grad_middle = g_ref[...].astype(F32) + back
    branch = grad_middle.astype(BF16)
    gm_ref[...] = branch
    ga_ref[...] = dot_nn(branch, wo_ref[...]).astype(BF16)

    @pl.when(step == 0)
    def _():
        acc[...] = jnp.zeros_like(acc)
        dgain_ref[...] = jnp.zeros_like(dgain_ref)

    acc[...] += dot_nn(branch.T, att_ref[...])
    dgain_ref[...] += dgain

    @pl.when(step == pl.num_programs(0) - 1)
    def _():
        piece = dwo_ref.shape[1]
        for chip, p in enumerate(place):
            dwo_ref[p] = acc[chip * piece : (chip + 1) * piece, :].astype(BF16)


def middle_back(place, g, middle, own, sib, gain, wo, att):
    rows, width = g.shape
    half = att.shape[1]
    row_block = lambda cols: pl.BlockSpec((TILE, cols), lambda r: (r, 0))
    pieces = (len(place), width // len(place), half)
    return pl.pallas_call(
        functools.partial(middle_back_kernel, place),
        grid=(rows // TILE,),
        in_specs=[
            row_block(width),
            row_block(width),
            row_block(width),
            row_block(width),
            whole(gain.shape),
            whole(wo.shape),
            row_block(half),
        ],
        out_specs=[row_block(width), row_block(half), whole(pieces), whole((1, width))],
        out_shape=[
            jax.ShapeDtypeStruct((rows, width), BF16),
            jax.ShapeDtypeStruct((rows, half), BF16),
            jax.ShapeDtypeStruct(pieces, BF16),
            jax.ShapeDtypeStruct((1, width), F32),
        ],
        scratch_shapes=[pltpu.VMEM((width, half), F32)],
        compiler_params=call_params(),
        cost_estimate=cost(2 * rows * width * half, 16 * rows * width),
        name="middle_back",
    )(g, middle, own, sib, gain, wo, att)


def ring_order(count):
    evens = list(range(0, count, 2))
    odds = list(range(1, count, 2))
    return evens + odds[::-1]


MESH = pl.DeviceIdType.MESH


def entry_kernel(
    order,
    cut,
    tok_ref,
    w_ref,
    states_ref,
    updates_ref,
    gate_ref,
    gain_one_ref,
    gain_two_ref,
    initial_ref,
    wo_ref,
    up_ref,
    down_ref,
    restart_ref,
    length_ref,
    x_ref,
    packs_ref,
    feed_one_ref,
    feed_two_ref,
    flags_ref,
    pack_ref,
    own_one_ref,
    own_two_ref,
    flag_ref,
    *sems,
):
    turn_send, turn_recv, rows_send, rows_recv, sib_send, sib_recv, ring_send, ring_recv = sems
    chips = len(order)
    dp = lax.axis_index("dp")
    y = lax.axis_index("tp")
    k = dp // 2
    c = dp % 2
    stays = c == y
    moves = jnp.logical_not(stays)
    partner = (2 * k + 1 - c, 1 - y)
    sibling = (2 * k + 1 - c, y)
    opposite = (dp, 1 - y)
    place = [order.index(i) for i in range(chips)]

    def chip_after(steps):
        found = jnp.int32(0)
        for i in range(chips):
            onward = order[(place[i] + steps) % chips]
            back = order[(place[i] - steps) % chips]
            found = jnp.where(k == i, jnp.where(c == 0, onward, back), found)
        return found

    following = (2 * chip_after(1) + c, y)
    previous = (2 * chip_after(-1) + c, y)
    barrier = pltpu.get_barrier_semaphore()
    for device in (sibling, opposite, following, previous):
        pl.semaphore_signal(barrier, inc=1, device_id=device, device_id_type=MESH)

    @pl.when(moves)
    def _():
        pl.semaphore_signal(barrier, inc=1, device_id=partner, device_id_type=MESH)

    parts, depth, cols = w_ref.shape
    heads, state_len, state_cols = states_ref.shape
    for i in range(parts):
        pack_ref[i * depth : (i + 1) * depth] = w_ref[i]
    at = parts * depth
    for h in range(heads):
        rows = slice(at + h * state_len, at + (h + 1) * state_len)
        pack_ref[rows, :state_cols] = states_ref[h]
        pack_ref[rows, state_cols:] = updates_ref[h]
    at += heads * state_len
    pack_ref[at : at + initial_ref.shape[0]] = initial_ref[...]
    at += initial_ref.shape[0]
    pack_ref[at:] = jnp.zeros((pack_ref.shape[0] - at, cols), BF16)
    pack_ref[at : at + heads, :state_len] = gate_ref[...]
    pack_ref[at + heads : at + heads + 1, :depth] = gain_one_ref[...]
    pack_ref[at + heads + 1 : at + heads + 2, :depth] = gain_two_ref[...]
    lane = lax.broadcasted_iota(jnp.int32, flag_ref.shape, 1)
    flag_ref[...] = jnp.where(lane == 0, restart_ref[0], length_ref[0])

    def remote(src, dst, send_sem, recv_sem, device):
        return pltpu.make_async_remote_copy(
            src_ref=src,
            dst_ref=dst,
            send_sem=send_sem,
            recv_sem=recv_sem,
            device_id=device,
            device_id_type=MESH,
        )

    own_block = 2 * k + y
    other_block = 2 * k + 1 - y
    turns = [
        (pack_ref, packs_ref.at[2 * k + c]),
        (flag_ref, flags_ref),
        (own_one_ref, feed_one_ref.at[c]),
        (own_two_ref, feed_two_ref.at[c]),
    ]

    def turn(i):
        src, dst = turns[i]
        return remote(src, dst, turn_send.at[i], turn_recv.at[i], partner)

    pieces = rows_send.shape[0]
    size = tok_ref.shape[0] // pieces

    def swap(i, half):
        rows = pl.ds(i * size, size)
        return remote(
            tok_ref.at[rows], x_ref.at[half, rows], rows_send.at[i], rows_recv.at[i], partner
        )

    def share(i, source, half):
        rows = pl.ds(i * size, size)
        return remote(
            source.at[rows], x_ref.at[half, rows], sib_send.at[i], sib_recv.at[i], sibling
        )

    def cross(src, block):
        last = len(turns)
        return remote(src, packs_ref.at[block], turn_send.at[last], turn_recv.at[last], opposite)

    def cross_feed(n, src, at):
        out = (feed_one_ref, feed_two_ref)[n]
        last = len(turns) + 1 + n
        return remote(src, out.at[at], turn_send.at[last], turn_recv.at[last], opposite)

    def ring(src, block, step, j):
        return remote(
            src, packs_ref.at[block], ring_send.at[step, j], ring_recv.at[step, j], following
        )

    @pl.when(stays)
    def _():
        pl.semaphore_wait(barrier, 4)
        cross(pack_ref, own_block).start()
        ring(pack_ref, own_block, 0, 0).start()
        for i in range(pieces):
            share(i, tok_ref, c).start()

    @pl.when(moves)
    def _():
        pl.semaphore_wait(barrier, 5)
        turn(0).start()
        turn(1).start()

    units = up_ref.shape[1]
    own_one_ref[:, :cut] = up_ref[:, :cut]
    own_one_ref[:, cut : 2 * cut] = down_ref[:, :cut]
    own_one_ref[:, 2 * cut :] = wo_ref[...]
    own_two_ref[:, : units - cut] = up_ref[:, cut:]
    own_two_ref[:, units - cut :] = down_ref[:, cut:]

    @pl.when(moves)
    def _():
        remote(
            pack_ref, packs_ref.at[own_block], turn_send.at[0], turn_recv.at[0], partner
        ).wait_recv()
        cross(packs_ref.at[own_block], own_block).start()
        ring(packs_ref.at[own_block], own_block, 0, 0).start()
        turn(2).start()
        for i in range(pieces):
            swap(i, 1 - c).start()
        for i in range(3, len(turns)):
            turn(i).start()

    @pl.when(stays)
    def _():
        cross_feed(0, own_one_ref, y).start()
        cross_feed(1, own_two_ref, y).start()
        packs_ref[own_block] = pack_ref[...]
        flags_ref[...] = flag_ref[...]
        feed_one_ref[y] = own_one_ref[...]
        feed_two_ref[y] = own_two_ref[...]
        x_ref[c] = tok_ref[...]

    def forward(i):
        @pl.when(moves)
        def _():
            swap(i, c).wait_recv()
            share(i, x_ref.at[c], c).start()

    def forward_feed(n):
        @pl.when(moves)
        def _():
            turn(2 + n).wait_recv()
            cross_feed(n, (feed_one_ref, feed_two_ref)[n].at[y], y).start()

    cross(pack_ref, other_block).wait_recv()
    ring(packs_ref.at[other_block], other_block, 0, 1).start()
    for step in range(1, chips):
        chip = chip_after(-step)
        for j in range(2):
            block = 2 * chip + jnp.where(j == 0, y, 1 - y)
            ring(packs_ref.at[block], block, step - 1, j).wait_recv()
            if step < chips - 1:
                ring(packs_ref.at[block], block, step, j).start()
        if step == 1:
            forward_feed(0)
        if 2 <= step < 2 + pieces:
            forward(step - 2)
    for i in range(max(0, chips - 2), pieces):
        forward(i)
    forward_feed(1)

    @pl.when(moves)
    def _():
        turn(1).wait_recv()

    for i in range(pieces):
        share(i, tok_ref, 1 - c).wait_recv()
        share(i, tok_ref, c).wait_send()
    for n, src in enumerate((own_one_ref, own_two_ref)):
        cross_feed(n, src, 1 - y).wait_recv()
        cross_feed(n, src, y).wait_send()
    cross(pack_ref, own_block).wait_send()
    for step in range(chips - 1):
        for j in range(2):
            ring(pack_ref, own_block, step, j).wait_send()

    @pl.when(moves)
    def _():
        for i in range(len(turns)):
            turn(i).wait_send()
        for i in range(pieces):
            swap(i, 1 - c).wait_send()


def enter(
    order,
    cut,
    tokens,
    w_in,
    states,
    updates,
    gate,
    gain_one,
    gain_two,
    initial,
    wo,
    up,
    down,
    restart,
    lengths,
):
    chips = len(order)
    pieces = 4
    depth, cols = w_in.shape[1:]
    units = up.shape[1]
    heads, state_len = gate.shape
    pack = (3 * depth + heads * state_len + initial.shape[0] + 16, cols)
    feed_one = (depth, 2 * cut + cols)
    feed_two = (depth, 2 * (units - cut))
    dma = pltpu.SemaphoreType.DMA
    in_vmem = pl.BlockSpec(memory_space=pltpu.VMEM)
    in_smem = pl.BlockSpec(memory_space=pltpu.SMEM)
    shape = jax.ShapeDtypeStruct
    return pl.pallas_call(
        functools.partial(entry_kernel, tuple(order), cut),
        in_specs=[in_vmem] * 11 + [in_smem] * 2,
        out_specs=[in_vmem] * 5,
        out_shape=[
            shape((2,) + tokens.shape, BF16),
            shape((2 * chips,) + pack, BF16),
            shape((2,) + feed_one, BF16),
            shape((2,) + feed_two, BF16),
            shape((1, 128), jnp.int32),
        ],
        scratch_shapes=[
            pltpu.VMEM(pack, BF16),
            pltpu.VMEM(feed_one, BF16),
            pltpu.VMEM(feed_two, BF16),
            pltpu.VMEM((1, 128), jnp.int32),
            dma((7,)),
            dma((7,)),
            dma((pieces,)),
            dma((pieces,)),
            dma((pieces,)),
            dma((pieces,)),
            dma((chips - 1, 2)),
            dma((chips - 1, 2)),
        ],
        compiler_params=call_params(collective_id=0, has_side_effects=True),
        cost_estimate=cost(0, 16 * tokens.size),
        name="enter",
    )(
        tokens,
        w_in,
        states,
        updates,
        gate,
        gain_one.reshape(1, -1),
        gain_two.reshape(1, -1),
        initial,
        wo,
        up,
        down,
        restart,
        lengths,
    )


def exit_kernel(
    order,
    dw_ref,
    ready_refs,
    dws_refs,
    dwu_refs,
    dgate_refs,
    dmemory_refs,
    dgain_one_ref,
    dgain_two_ref,
    flags_ref,
    gy_own_ref,
    gy_give_ref,
    gain_ref,
    x_any,
    gm_any,
    gt_ref,
    gc_ref,
    turned_ref,
    ready_turned_refs,
    wide_ref,
    small_ref,
    first_ref,
    ring_ref,
    cross_ref,
    total_ref,
    gy_sib_ref,
    result_ref,
    carried_ref,
    x_ref,
    gm_ref,
    gain_sib_ref,
    ready_cross_refs,
    ready_total_refs,
    ready_sems,
    load_sems,
    gain_sems,
    sib_send,
    sib_recv,
    rows_send,
    rows_recv,
    ring_send,
    ring_recv,
    cross_sems,
    turn_sems,
    carried_sems,
):
    chips = len(order)
    dp = lax.axis_index("dp")
    y = lax.axis_index("tp")
    k = dp // 2
    c = dp % 2
    stays = c == y
    moves = jnp.logical_not(stays)
    partner = (2 * k + 1 - c, 1 - y)
    sibling = (2 * k + 1 - c, y)
    opposite = (dp, 1 - y)
    place = [order.index(i) for i in range(chips)]

    def chip_after(steps):
        found = jnp.int32(0)
        for i in range(chips):
            onward = order[(place[i] + steps) % chips]
            back = order[(place[i] - steps) % chips]
            found = jnp.where(k == i, jnp.where(c == 0, onward, back), found)
        return found

    following = (2 * chip_after(1) + c, y)
    previous = (2 * chip_after(-1) + c, y)
    barrier = pltpu.get_barrier_semaphore()
    for device in (sibling, opposite, following, previous):
        pl.semaphore_signal(barrier, inc=1, device_id=device, device_id_type=MESH)

    @pl.when(moves)
    def _():
        pl.semaphore_signal(barrier, inc=1, device_id=partner, device_id_type=MESH)

    loads = [
        pltpu.make_async_copy(x_any.at[c], x_ref, load_sems.at[0]),
        pltpu.make_async_copy(gm_any.at[c], gm_ref, load_sems.at[1]),
    ]
    for load in loads:
        load.start()

    def remote(src, dst, send_sem, recv_sem, device):
        return pltpu.make_async_remote_copy(
            src_ref=src,
            dst_ref=dst,
            send_sem=send_sem,
            recv_sem=recv_sem,
            device_id=device,
            device_id_type=MESH,
        )

    pieces = sib_send.shape[0]
    size = gy_own_ref.shape[0] // pieces
    in_rows, lanes_in = dw_ref.shape[2:]
    gain_swap = remote(dgain_one_ref, gain_sib_ref, gain_sems.at[0], gain_sems.at[1], sibling)
    carried_turn = remote(carried_ref, gc_ref, carried_sems.at[0], carried_sems.at[1], partner)

    def give(i):
        rows = pl.ds(i * size, size)
        return remote(
            gy_give_ref.at[rows], gy_sib_ref.at[rows], sib_send.at[i], sib_recv.at[i], sibling
        )

    def swap(i):
        rows = pl.ds(i * size, size)
        return remote(
            result_ref.at[rows], gt_ref.at[rows], rows_send.at[i], rows_recv.at[i], partner
        )

    def ring(src, step, j):
        return remote(
            src, ring_ref.at[step, j], ring_send.at[step, j], ring_recv.at[step, j], following
        )

    many = len(ready_refs)

    def ready_cross(n):
        sems = ready_sems.at[n]
        return remote(
            ready_refs[n].at[1 - y], ready_cross_refs[n], sems.at[0], sems.at[1], opposite
        )

    def ready_turn(n):
        sems = ready_sems.at[n]
        return remote(ready_total_refs[n], ready_turned_refs[n], sems.at[2], sems.at[3], partner)

    def ready_arrives(n):
        ready_cross(n).wait_recv()
        total = (ready_refs[n][y].astype(F32) + ready_cross_refs[n][...].astype(F32)).astype(BF16)

        @pl.when(stays)
        def _():
            ready_turned_refs[n][...] = total

        @pl.when(moves)
        def _():
            ready_total_refs[n][...] = total
            ready_turn(n).start()

    @pl.when(stays)
    def _():
        pl.semaphore_wait(barrier, 4)

    @pl.when(moves)
    def _():
        pl.semaphore_wait(barrier, 5)

    gain_swap.start()
    for i in range(pieces):
        give(i).start()
    for n in range(many):
        ready_cross(n).start()

    restarted = flags_ref[0, 0] > 0
    dmemory = jnp.concatenate([ref[...] for ref in dmemory_refs], axis=1)
    initial = jnp.where(restarted, dmemory, 0.0)
    kept = jnp.where(restarted, 0.0, dmemory).astype(BF16)

    part_heads, head_dim, state_cols = dws_refs[0].shape
    heads = part_heads * len(dws_refs)
    state_len = head_dim // (2 * chips)
    init_len = initial.shape[0] // (2 * chips)
    depth = dgain_two_ref.shape[1] // (2 * chips)
    states = heads * state_len
    tail = states + init_len
    wide_ref[:, :, tail:] = jnp.zeros_like(wide_ref[:, :, tail:])
    gain_swap.wait_recv()
    gain = dgain_one_ref[...] + gain_sib_ref[...]
    for block in range(2 * chips):
        at = (block // 2, block % 2)
        lines = slice(block * state_len, (block + 1) * state_len)
        for h in range(heads):
            rows = slice(h * state_len, (h + 1) * state_len)
            n, i = h // part_heads, h % part_heads
            wide_ref[at + (rows, slice(0, state_cols))] = dws_refs[n][i, lines]
            wide_ref[at + (rows, slice(state_cols, None))] = dwu_refs[n][i, lines]
            wide_ref[at + (slice(tail + h, tail + h + 1), slice(0, state_len))] = dgate_refs[n][
                i, :, lines
            ]
        wide_ref[at + (slice(states, tail),)] = initial[block * init_len : (block + 1) * init_len]
        lanes = slice(block * depth, (block + 1) * depth)
        row = tail + heads
        wide_ref[at + (slice(row, row + 1), slice(0, depth))] = gain[:, lanes]
        wide_ref[at + (slice(row + 1, row + 2), slice(0, depth))] = dgain_two_ref[:, lanes]
    small = wide_ref.shape[2]
    for i in range(wide_ref.shape[3] // lanes_in):
        lanes = slice(i * lanes_in, (i + 1) * lanes_in)
        small_ref[:, :, i * small : (i + 1) * small] = wide_ref[:, :, :, lanes].astype(BF16)

    slice_of = [1 - y, y]
    start = chip_after(-1)
    for j in range(2):
        first_ref[j, :in_rows] = dw_ref[start, slice_of[j]]
        first_ref[j, in_rows:] = small_ref[start, slice_of[j]]
        ring(first_ref.at[j], 0, j).start()

    @pl.when(stays)
    def _():
        gc_ref[...] = kept

    @pl.when(moves)
    def _():
        carried_ref[...] = kept
        carried_turn.start()

    for load in loads:
        load.wait()
    gain_one = gain_ref[...]

    def token_rows(i):
        rows = slice(i * size, (i + 1) * size)
        give(i).wait_recv()
        gy = gy_own_ref[rows].astype(F32) + gy_sib_ref[rows].astype(F32)
        back, _ = norm_back(x_ref[rows].astype(F32), gain_one, gy)
        grad = (gm_ref[rows].astype(F32) + back).astype(BF16)

        @pl.when(stays)
        def _():
            gt_ref[rows] = grad

        @pl.when(moves)
        def _():
            result_ref[rows] = grad
            swap(i).start()

    cross = remote(
        ring_ref.at[chips - 2, 0], cross_ref, cross_sems.at[0], cross_sems.at[1], opposite
    )
    token_rows(0)
    tasks = [functools.partial(token_rows, i) for i in range(1, pieces)]
    tasks += [functools.partial(ready_arrives, n) for n in range(many)]
    for step in range(chips - 1):
        chip = chip_after(-step - 2)
        for j in range(2):
            ring(first_ref.at[j], step, j).wait_recv()
            ring_ref[step, j, :in_rows] = (
                ring_ref[step, j, :in_rows].astype(F32) + dw_ref[chip, slice_of[j]].astype(F32)
            ).astype(BF16)
            ring_ref[step, j, in_rows:] = (
                ring_ref[step, j, in_rows:].astype(F32) + small_ref[chip, slice_of[j]].astype(F32)
            ).astype(BF16)
            if step < chips - 2:
                ring(ring_ref.at[step, j], step + 1, j).start()
            elif j == 0:
                cross.start()
        if tasks and step < chips - 2:
            tasks.pop(0)()
    for task in tasks:
        task()
    cross.wait_recv()
    total_ref[...] = (
        ring_ref[chips - 2, 1].astype(F32) + cross_ref[...].astype(F32)
    ).astype(BF16)
    turn = remote(total_ref, turned_ref, turn_sems.at[0], turn_sems.at[1], partner)

    @pl.when(stays)
    def _():
        turned_ref[...] = total_ref[...]

    @pl.when(moves)
    def _():
        turn.start()
        for i in range(pieces):
            swap(i).wait_recv()
        carried_turn.wait_recv()
        for n in range(many):
            ready_turn(n).wait_recv()
        turn.wait_recv()

    gain_swap.wait_send()
    cross.wait_send()
    for i in range(pieces):
        give(i).wait_send()
    for n in range(many):
        ready_cross(n).wait_send()
    for step in range(chips - 1):
        for j in range(2):
            ring(first_ref.at[j], step, j).wait_send()

    @pl.when(moves)
    def _():
        turn.wait_send()
        carried_turn.wait_send()
        for n in range(many):
            ready_turn(n).wait_send()
        for i in range(pieces):
            swap(i).wait_send()


def leave(
    order, dw, ready, dws, dwu, dgate, dmemory, dgain_one, dgain_two, flags, gy_own, gy_give, gain, x, gm
):
    chips = len(order)
    pieces = 4
    many = len(ready)
    parts = len(dws)
    half, width = gy_own.shape
    in_rows, lanes = dw.shape[2:]
    heads, head_dim, state_cols = dws[0].shape
    heads = heads * parts
    cols = heads * head_dim
    small = heads * head_dim // (2 * chips) + S // (2 * chips) + 16
    message = (in_rows + small * (cols // lanes), lanes)
    dma = pltpu.SemaphoreType.DMA
    in_vmem = pl.BlockSpec(memory_space=pltpu.VMEM)
    anywhere = pl.BlockSpec(memory_space=pl.ANY)
    shape = jax.ShapeDtypeStruct
    ready_scratch = tuple(pltpu.VMEM(v.shape[1:], BF16) for v in ready)
    inputs = (dw, *ready, *dws, *dwu, *dgate, *dmemory)

    def kernel(*refs):
        at = 1 + many
        groups = [refs[1:at]] + [refs[at + parts * i : at + parts * (i + 1)] for i in range(4)]
        at = len(inputs) + 11
        rest = refs[len(inputs) : at]
        exit_kernel(tuple(order), refs[0], *groups, *rest, refs[at : at + many], *refs[at + many :])

    outs = pl.pallas_call(
        kernel,
        in_specs=[in_vmem] * (len(inputs) + 2)
        + [pl.BlockSpec(memory_space=pltpu.SMEM)]
        + [in_vmem] * 3
        + [anywhere] * 2,
        out_specs=[in_vmem] * (3 + many),
        out_shape=[shape((half, width), BF16), shape((S, cols), BF16), shape(message, BF16)]
        + [shape(v.shape[1:], BF16) for v in ready],
        scratch_shapes=[
            pltpu.VMEM((chips, 2, small, cols), F32),
            pltpu.VMEM((chips, 2, small * (cols // lanes), lanes), BF16),
            pltpu.VMEM((2,) + message, BF16),
            pltpu.VMEM((chips - 1, 2) + message, BF16),
            pltpu.VMEM(message, BF16),
            pltpu.VMEM(message, BF16),
            pltpu.VMEM((half, width), BF16),
            pltpu.VMEM((half, width), BF16),
            pltpu.VMEM((S, cols), BF16),
            pltpu.VMEM((half, width), BF16),
            pltpu.VMEM((half, width), BF16),
            pltpu.VMEM((1, width), F32),
            ready_scratch,
            ready_scratch,
            dma((many, 4)),
            dma((2,)),
            dma((2,)),
            dma((pieces,)),
            dma((pieces,)),
            dma((pieces,)),
            dma((pieces,)),
            dma((chips - 1, 2)),
            dma((chips - 1, 2)),
            dma((2,)),
            dma((2,)),
            dma((2,)),
        ],
        compiler_params=call_params(collective_id=1, has_side_effects=True),
        cost_estimate=cost(0, 30 * half * width),
        name="leave",
    )(*inputs, dgain_one, dgain_two, flags, gy_own, gy_give, gain, x, gm)
    return outs[0], outs[1], outs[2], outs[3:]


def unpack_kernel(
    gt_ref,
    gc_ref,
    last_ref,
    two_ref,
    first_ref,
    one_ref,
    out_gt_ref,
    out_gc_ref,
    out_in_ref,
    out_wo_ref,
    out_ws_ref,
    out_wu_ref,
    out_gate_ref,
    out_initial_ref,
    out_one_ref,
    out_two_ref,
    out_up_ref,
    out_down_ref,
):
    out_gt_ref[...] = gt_ref[...].astype(F32)
    out_gc_ref[...] = gc_ref[...].astype(F32)
    cut = one_ref.shape[2]
    for i, out in enumerate((out_up_ref, out_down_ref)):
        out[:, :cut] = one_ref[i].astype(F32)
        out[:, cut:] = two_ref[i].astype(F32)
    parts, depth, cols = out_in_ref.shape
    low = depth // 2
    pair = cols // HD // 2
    for n, ref in enumerate((first_ref, last_ref)):
        for i in range(parts):
            for h in range(pair):
                for t in range(2):
                    at = (2 * h + t) * HD
                    lanes = slice((n * pair + h) * HD, (n * pair + h + 1) * HD)
                    piece = ref[i * low : (i + 1) * low, at : at + HD]
                    out_in_ref[i, t * low : (t + 1) * low, lanes] = piece.astype(F32)
    out_wo_ref[...] = first_ref[parts * low :].astype(F32)
    rest = last_ref[parts * low :].astype(F32)
    heads, state_len, state_cols = out_ws_ref.shape
    for h in range(heads):
        rows = slice(h * state_len, (h + 1) * state_len)
        out_ws_ref[h] = rest[rows, :state_cols]
        out_wu_ref[h] = rest[rows, state_cols:]
    at = heads * state_len
    out_initial_ref[...] = rest[at : at + out_initial_ref.shape[0]]
    at += out_initial_ref.shape[0]
    out_gate_ref[...] = rest[at : at + heads, :state_len]
    out_one_ref[...] = rest[at + heads : at + heads + 1, :depth]
    out_two_ref[...] = rest[at + heads + 1 : at + heads + 2, :depth]


def unpack(arrays, shapes):
    gt, gc = arrays[:2]
    shape = lambda dims: jax.ShapeDtypeStruct(dims, F32)
    in_vmem = pl.BlockSpec(memory_space=pltpu.VMEM)
    return pl.pallas_call(
        unpack_kernel,
        in_specs=[in_vmem] * len(arrays),
        out_specs=[in_vmem] * (2 + len(shapes)),
        out_shape=[shape(gt.shape), shape(gc.shape)] + [shape(dims) for dims in shapes],
        compiler_params=call_params(),
        cost_estimate=cost(0, 6 * gt.size),
        name="unpack",
    )(*arrays)


def tie(*values):
    return lax.optimization_barrier(values)


class Paths:
    def __init__(self, chips):
        self.order = ring_order(chips)
        self.place = tuple(self.order.index(k) for k in range(chips))
        index = lambda k, c, y: (2 * k + c) * 2 + y
        every = [(k, c, y) for k in range(chips) for c in range(2) for y in range(2)]
        self.turned = [(index(k, c, y), index(k, y, c)) for k, c, y in every if c != y]
        self.across = [(index(k, c, y), index(k, c, 1 - y)) for k, c, y in every]
        self.sibling = [(index(k, c, y), index(k, 1 - c, y)) for k, c, y in every]
        self.rings = [[2 * k + c for k in self.order] for c in range(2)]
        self.spots = tuple(2 * self.place[b // 2] + b % 2 for b in range(2 * chips))
        self.chips = chips

    def send(self, values, pairs):
        return lax.ppermute(values, ("dp", "tp"), pairs)

    def turn(self, values):
        stays = lax.axis_index("dp") % 2 == lax.axis_index("tp")
        return jnp.where(stays, values, self.send(values, self.turned))

    def gather(self, values):
        return lax.all_gather(values, "dp", axis=0, tiled=False, axis_index_groups=self.rings)

    def reduce(self, values):
        return lax.psum_scatter(
            values, "dp", scatter_dimension=0, tiled=False, axis_index_groups=self.rings
        )


def body(
    chips,
    tokens,
    carried,
    restart,
    lengths,
    gain_attend,
    input_weights,
    state_weights,
    update_weights,
    gate_bias,
    initial_state,
    output_weights,
    gain_feed,
    feed_up,
    feed_down,
    grad_mixed,
    grad_final,
):
    paths = Paths(chips)
    send, place = paths.send, paths.place
    y = lax.axis_index("tp")
    c = lax.axis_index("dp") % 2
    core = jnp.stack([c, y])
    heads, state_len = gate_bias.shape
    depth = input_weights.shape[1]
    cols = heads * HD
    slices = 2 * chips
    gate_len = heads * state_len
    half_rows = tokens.shape[0]

    units = feed_up.shape[1]
    cut = units // 2
    entered = enter(
        paths.order,
        cut,
        tokens,
        input_weights,
        state_weights,
        update_weights,
        gate_bias,
        gain_attend,
        gain_feed,
        initial_state,
        output_weights.T,
        feed_up,
        feed_down.T,
        restart,
        lengths,
    )
    entered, carried = tie(entered, carried)
    x, packs, first_feed, second_feed, flags = entered
    carried_own = paths.turn(carried[0])
    x = x.reshape(2 * half_rows, -1)
    first_feed = paths.gather(first_feed).reshape(slices, depth, -1)
    second_feed = paths.gather(second_feed).reshape(slices, depth, -1)
    states_at = 3 * depth
    initial_at = states_at + gate_len
    tail_at = initial_at + initial_state.shape[0]
    small = packs[:, tail_at : tail_at + heads + 2, :depth].astype(F32)
    gain_one = small[:, heads].reshape(1, -1)
    gain_two = small[:, heads + 1].reshape(1, -1)
    gate = jnp.moveaxis(small[:, :heads, :state_len], 1, 0).reshape(heads, 1, HD)
    states = packs[:, states_at:initial_at].reshape(slices, heads, state_len, 4 * HD)
    states = jnp.moveaxis(states, 1, 0).reshape(heads, HD, 4 * HD)
    spots = jnp.asarray(paths.spots, jnp.int32)
    wo_own = jnp.take(first_feed[:, :, 2 * cut :], spots, axis=0).reshape(-1, cols)
    wo_sib = send(wo_own, paths.sibling)

    normed_t, projected = project(x, gain_one, packs, depth)
    projected, carried_own, grad_mixed, grad_final = tie(
        projected, carried_own, grad_mixed, grad_final
    )
    g_own = paths.turn(grad_mixed)
    grad_final_own = paths.turn(grad_final[0])
    attended, state_out, logs, state_logs, memory_end = attend(
        flags, projected, carried_own, packs, initial_at, states, gate
    )
    attended, g_own, memory_end, grad_final_own = tie(attended, g_own, memory_end, grad_final_own)
    attended_sib = send(attended, paths.sibling)
    g_sib = send(g_own, paths.sibling)
    middle, normed, normed_mid_t, g, g_t = form_middle(
        core, x, attended, attended_sib, wo_own, wo_sib, gain_two, g_own, g_sib
    )
    final_memory = paths.turn(memory_end)

    ff, gn, feed_grad = feed(
        place, paths.spots, core, normed, normed_mid_t, g, g_t, first_feed, cut
    )
    feed_one = paths.reduce(feed_grad)
    ff, gn, feed_grad = feed(
        place,
        paths.spots,
        core,
        normed,
        normed_mid_t,
        g,
        g_t,
        second_feed,
        units - cut,
        (ff, gn),
    )
    feed_two = paths.reduce(feed_grad)
    half_of = lambda values, at: lax.dynamic_slice_in_dim(values, at * half_rows, half_rows)
    gn_sib = send(gn, paths.sibling)
    grad_middle, grad_attended, dwo, dgain_two = middle_back(
        place, g, middle, gn, gn_sib, gain_two, wo_own, attended
    )
    grad_attended, ff, final_memory = tie(grad_attended, ff, final_memory)
    ff_sib = send(half_of(ff, 1 - c), paths.sibling)

    pair = heads // 2

    def back(n, spots, grad, **more):
        return attend_back(
            n * pair,
            pair,
            spots,
            flags,
            projected,
            carried_own,
            packs,
            initial_at,
            states,
            gate,
            attended,
            state_out,
            logs,
            state_logs,
            grad,
            grad_final_own,
            normed_t,
            depth,
            **more,
        )

    left = back(0, place, grad_attended, dwo=dwo.reshape(chips, 2, depth, cols))
    left, ff_sib, grad_attended, feed_one = tie(left, ff_sib, grad_attended, feed_one)
    first_sum = paths.reduce(left[4])
    mixed_own = half_of(middle, c) + half_of(ff, c).astype(F32) + ff_sib.astype(F32)
    feed_keep = lax.dynamic_index_in_dim(feed_one, y, 0, keepdims=False)
    feed_give = lax.dynamic_index_in_dim(feed_one, 1 - y, 0, keepdims=False)
    mixed_own, feed_give, grad_attended = tie(mixed_own.astype(BF16), feed_give, grad_attended)
    feed_got = send(feed_give, paths.across)
    mixed = paths.turn(mixed_own)
    right = back(1, tuple(range(chips)), grad_attended, more=(core, x, left[5]))
    right, mixed, feed_got = tie(right, mixed, feed_got)
    feed_one = paths.turn((feed_keep.astype(F32) + feed_got.astype(F32)).astype(BF16))
    dws, dwu, dgate, dmemory, (_, dw_right) = list(zip(left, right))[:5]
    gy_own, gy_give, dgain_one = right[5:]
    gt, gc, last, ready = leave(
        paths.order,
        dw_right,
        (feed_two, first_sum),
        dws,
        dwu,
        dgate,
        dmemory,
        dgain_one,
        dgain_two,
        flags,
        gy_own,
        gy_give,
        gain_one,
        x.reshape(2, half_rows, -1),
        grad_middle.reshape(2, half_rows, -1),
    )
    (
        grad_tokens,
        grad_carried,
        out_input,
        out_output,
        out_state,
        out_update,
        out_gate,
        out_initial,
        out_one,
        out_two,
        out_up,
        out_down,
    ) = unpack(
        (gt, gc, last, *ready, feed_one),
        (
            input_weights.shape,
            (depth, cols),
            state_weights.shape,
            update_weights.shape,
            gate_bias.shape,
            initial_state.shape,
            (1, depth),
            (1, depth),
            (depth, units),
            (depth, units),
        ),
    )
    return (
        mixed,
        final_memory[None],
        grad_tokens,
        grad_carried[None],
        out_one[0],
        out_input,
        out_state,
        out_update,
        out_gate,
        out_initial,
        out_output.T,
        out_two[0],
        out_up,
        out_down.T,
    )


def solution(mesh):
    ranks, groups = mesh.shape["dp"], mesh.shape["tp"]
    chosen = functools.partial(body, ranks // 2) if groups == 2 else general_body
    placed = (
        P(("dp", "tp"), None),
        P("dp", None, "tp"),
        P("dp"),
        P("dp"),
        P("dp"),
        P(None, "dp", "tp"),
        P("tp", "dp", None),
        P("tp", "dp", None),
        P("tp", "dp"),
        P("dp", "tp"),
        P("tp", "dp"),
        P("dp"),
        P("dp", "tp"),
        P("tp", "dp"),
        P(("dp", "tp"), None),
        P("dp", None, "tp"),
    )
    return jax.shard_map(
        chosen,
        mesh=mesh,
        in_specs=placed,
        out_specs=(
            P(("dp", "tp"), None),
            P("dp", None, "tp"),
            P(("dp", "tp"), None),
            P("dp", None, "tp"),
            P("dp"),
            P(None, "dp", "tp"),
            P("tp", "dp", None),
            P("tp", "dp", None),
            P("tp", "dp"),
            P("dp", "tp"),
            P("tp", "dp"),
            P("dp"),
            P("dp", "tp"),
            P("tp", "dp"),
        ),
        check_vma=False,
    )
```

```python
import functools
import math

import jax
import jax.numpy as jnp
from jax import lax
from jax.experimental import pallas as pl
from jax.experimental.pallas import tpu as pltpu
from jax.sharding import PartitionSpec as P

S = 512
BLK = 512
LEN = 1536
NB = 3


EPSILON = 1e-06
NEGATIVE = -1e30


def rms_scale(values, gain):
    return values * lax.rsqrt(jnp.mean(values * values, axis=-1, keepdims=True) + EPSILON) * gain


def block_masks(block_id, length, block_len, state_count):
    row_ids = jnp.arange(block_len, dtype=jnp.int32)
    places = block_id * block_len + row_ids
    key_places = jnp.concatenate([places - block_len, places])
    allowed = (
        (key_places[None, :] >= 0)
        & (key_places[None, :] < length)
        & (key_places[None, :] <= places[:, None])
        & (key_places[None, :] > places[:, None] - block_len)
    )
    state_open = jnp.ones((block_len, state_count), dtype=bool)
    allowed = jnp.concatenate([allowed, state_open], axis=1)
    usable = jnp.concatenate([places < length, jnp.ones((state_count,), dtype=bool)])
    return (allowed, usable)


def masked_softmax(scores, allowed):
    scores = jnp.where(allowed, scores, NEGATIVE)
    peak_val = jnp.max(scores, axis=-1, keepdims=True)
    powers = jnp.exp(scores - peak_val)
    totals = jnp.sum(powers, axis=-1, keepdims=True)
    return (powers / totals, peak_val + jnp.log(totals))


def recall_softmax(scores, allowed, log_total):
    return jnp.exp(jnp.where(allowed, scores, NEGATIVE) - log_total)


def state_project(memory, state_weights):
    head_dim = memory.shape[-1]
    projected = jnp.einsum(
        "shd,hde->she",
        memory.astype(jnp.bfloat16),
        state_weights,
        preferred_element_type=jnp.float32,
    ).astype(jnp.bfloat16)
    return (
        projected[..., :head_dim],
        projected[..., head_dim : 2 * head_dim],
        projected[..., 2 * head_dim :],
    )


def block_forward(
    state_weights,
    update_weights,
    retain,
    memory,
    queries,
    keys_now,
    values_now,
    keys_before,
    values_before,
    block_id,
    length,
):
    head_dim = queries.shape[-1]
    block_len = queries.shape[0]
    state_count = memory.shape[0]
    scaling = head_dim ** (-0.5)
    state_q, state_k, state_v = state_project(memory, state_weights)
    allowed, usable = block_masks(block_id, length, block_len, state_count)
    key_set = jnp.concatenate([keys_before, keys_now, state_k], axis=0)
    value_set = jnp.concatenate([values_before, values_now, state_v], axis=0)
    scores = (
        jnp.einsum("ihd,jhd->hij", queries, key_set, preferred_element_type=jnp.float32) * scaling
    )
    shares, log_total = masked_softmax(scores, allowed[None])
    outputs = jnp.einsum(
        "hij,jhd->ihd", shares.astype(jnp.bfloat16), value_set, preferred_element_type=jnp.float32
    ).astype(jnp.bfloat16)
    state_keys = jnp.concatenate([keys_now, state_k], axis=0)
    state_values = jnp.concatenate([values_now, state_v], axis=0)
    state_scores = (
        jnp.einsum("shd,jhd->hsj", state_q, state_keys, preferred_element_type=jnp.float32)
        * scaling
    )
    state_shares, state_log = masked_softmax(state_scores, usable[None, None])
    state_out = jnp.einsum(
        "hsj,jhd->shd",
        state_shares.astype(jnp.bfloat16),
        state_values,
        preferred_element_type=jnp.float32,
    ).astype(jnp.bfloat16)
    update = jnp.einsum(
        "shd,hde->she", state_out, update_weights, preferred_element_type=jnp.float32
    )
    blended = retain * memory + (1.0 - retain) * update
    active = block_id * block_len < length
    memory_next = jnp.where(active, blended, memory)
    return (memory_next, (outputs, state_out, log_total, state_log))


def block_backward(
    state_weights,
    update_weights,
    retain,
    memory,
    queries,
    keys_now,
    values_now,
    keys_before,
    values_before,
    grad_out,
    state_out,
    log_total,
    state_log,
    block_id,
    length,
    grad_next,
):
    head_dim = queries.shape[-1]
    block_len = queries.shape[0]
    state_count = memory.shape[0]
    scaling = head_dim ** (-0.5)
    span_end = 2 * block_len
    state_q, state_k, state_v = state_project(memory, state_weights)
    allowed, usable = block_masks(block_id, length, block_len, state_count)
    active = block_id * block_len < length
    update = jnp.einsum(
        "shd,hde->she", state_out, update_weights, preferred_element_type=jnp.float32
    )
    grad_blend = jnp.where(active, grad_next, 0.0)
    grad_memory = jnp.where(active, retain * grad_next, grad_next)
    grad_update = ((1.0 - retain) * grad_blend).astype(jnp.bfloat16)
    grad_gate = jnp.sum(grad_blend * (memory - update), axis=0) * retain * (1.0 - retain)
    grad_update_w = jnp.einsum(
        "shd,she->hde", state_out, grad_update, preferred_element_type=jnp.float32
    )
    grad_state_out = jnp.einsum(
        "she,hde->shd", grad_update, update_weights, preferred_element_type=jnp.float32
    ).astype(jnp.bfloat16)
    state_keys = jnp.concatenate([keys_now, state_k], axis=0)
    state_values = jnp.concatenate([values_now, state_v], axis=0)
    state_scores = (
        jnp.einsum("shd,jhd->hsj", state_q, state_keys, preferred_element_type=jnp.float32)
        * scaling
    )
    state_shares = recall_softmax(state_scores, usable[None, None], state_log)
    grad_state_shares = jnp.einsum(
        "shd,jhd->hsj", grad_state_out, state_values, preferred_element_type=jnp.float32
    )
    grad_state_scores = (
        state_shares
        * (grad_state_shares - jnp.sum(state_shares * grad_state_shares, axis=-1, keepdims=True))
    ).astype(jnp.bfloat16)
    grad_state_values = jnp.einsum(
        "hsj,shd->jhd",
        state_shares.astype(jnp.bfloat16),
        grad_state_out,
        preferred_element_type=jnp.float32,
    )
    grad_state_q = (
        jnp.einsum(
            "hsj,jhd->shd", grad_state_scores, state_keys, preferred_element_type=jnp.float32
        )
        * scaling
    )
    grad_state_keys = (
        jnp.einsum("hsj,shd->jhd", grad_state_scores, state_q, preferred_element_type=jnp.float32)
        * scaling
    )
    key_set = jnp.concatenate([keys_before, keys_now, state_k], axis=0)
    value_set = jnp.concatenate([values_before, values_now, state_v], axis=0)
    scores = (
        jnp.einsum("ihd,jhd->hij", queries, key_set, preferred_element_type=jnp.float32) * scaling
    )
    shares = recall_softmax(scores, allowed[None], log_total)
    grad_shares = jnp.einsum(
        "ihd,jhd->hij", grad_out, value_set, preferred_element_type=jnp.float32
    )
    grad_scores = (
        shares * (grad_shares - jnp.sum(shares * grad_shares, axis=-1, keepdims=True))
    ).astype(jnp.bfloat16)
    grad_values = jnp.einsum(
        "hij,ihd->jhd", shares.astype(jnp.bfloat16), grad_out, preferred_element_type=jnp.float32
    )
    grad_queries = (
        jnp.einsum("hij,jhd->ihd", grad_scores, key_set, preferred_element_type=jnp.float32)
        * scaling
    )
    grad_keys = (
        jnp.einsum("hij,ihd->jhd", grad_scores, queries, preferred_element_type=jnp.float32)
        * scaling
    )
    grad_keys_now = grad_keys[block_len:span_end] + grad_state_keys[:block_len]
    grad_values_now = grad_values[block_len:span_end] + grad_state_values[:block_len]
    grad_state_k = grad_keys[span_end:] + grad_state_keys[block_len:]
    grad_state_v = grad_values[span_end:] + grad_state_values[block_len:]
    grad_proj = jnp.concatenate([grad_state_q, grad_state_k, grad_state_v], axis=-1).astype(
        jnp.bfloat16
    )
    grad_memory = grad_memory + jnp.einsum(
        "she,hde->shd", grad_proj, state_weights, preferred_element_type=jnp.float32
    )
    grad_state_w = jnp.einsum(
        "shd,she->hde", memory.astype(jnp.bfloat16), grad_proj, preferred_element_type=jnp.float32
    )
    return (
        grad_memory,
        grad_queries,
        grad_keys_now,
        grad_values_now,
        grad_keys[:block_len],
        grad_values[:block_len],
        grad_state_w,
        grad_update_w,
        grad_gate,
    )


def general_body(
    tokens,
    carried,
    restart,
    lengths,
    gain_attend,
    input_weights,
    state_weights,
    update_weights,
    gate_bias,
    initial_state,
    output_weights,
    gain_feed,
    feed_up,
    feed_down,
    grad_mixed,
    grad_final,
):
    seq_count = lengths.shape[0]
    heads_here = gate_bias.shape[0]
    head_dim = update_weights.shape[-1]
    width_here = heads_here * head_dim
    group_rows = seq_count * LEN
    gathered = (
        lax.all_gather(gain_attend, "dp", axis=0, tiled=True),
        lax.all_gather(gain_feed, "dp", axis=0, tiled=True),
        lax.all_gather(input_weights, "dp", axis=1, tiled=True),
        lax.all_gather(output_weights, "dp", axis=1, tiled=True),
        lax.all_gather(state_weights, "dp", axis=1, tiled=True),
        lax.all_gather(update_weights, "dp", axis=1, tiled=True),
        lax.all_gather(gate_bias, "dp", axis=1, tiled=True),
        lax.all_gather(initial_state, "dp", axis=0, tiled=True),
        lax.all_gather(feed_up, "dp", axis=0, tiled=True),
        lax.all_gather(feed_down, "dp", axis=1, tiled=True),
    )
    (
        gain_attend_all,
        gain_feed_all,
        input_all,
        output_all,
        state_all,
        update_all,
        gate_all,
        initial_all,
        up_all,
        down_all,
    ) = gathered
    tokens_wide = tokens.astype(jnp.float32)
    gain_one = gain_attend_all.astype(jnp.float32)
    gain_two = gain_feed_all.astype(jnp.float32)
    normed = rms_scale(tokens_wide, gain_one).astype(jnp.bfloat16)
    normed_all = lax.all_gather(normed, "tp", axis=0, tiled=True)
    projected = jnp.einsum(
        "rd,kdc->krc", normed_all, input_all, preferred_element_type=jnp.float32
    ).astype(jnp.bfloat16)
    blocked = jnp.moveaxis(projected.reshape(3, seq_count, NB, BLK, heads_here, head_dim), 2, 1)
    earlier = jnp.concatenate([jnp.zeros_like(blocked[:, :1]), blocked[:, :-1]], axis=1)
    retain = jax.nn.sigmoid(gate_all.astype(jnp.float32))
    memory_start = jnp.where(
        restart[:, None, None] > 0, initial_all.astype(jnp.float32)[None], carried
    ).reshape(seq_count, S, heads_here, head_dim)
    forward_block = jax.vmap(block_forward, in_axes=(None, None, None, 0, 0, 0, 0, 0, 0, None, 0))
    block_ids = jnp.arange(NB, dtype=jnp.int32)

    def forward_step(memory, entries):
        queries, keys_now, values_now, keys_before, values_before, block_id = entries
        memory_next, saved = forward_block(
            state_all,
            update_all,
            retain,
            memory,
            queries,
            keys_now,
            values_now,
            keys_before,
            values_before,
            block_id,
            lengths,
        )
        return (memory_next, (memory, saved))

    memory_end, (memories, saved_all) = lax.scan(
        forward_step,
        memory_start,
        (blocked[0], blocked[1], blocked[2], earlier[1], earlier[2], block_ids),
    )
    outputs, state_outs, log_totals, state_logs = saved_all
    attended = jnp.moveaxis(outputs, 0, 1).reshape(group_rows, width_here)
    middle = tokens_wide + lax.psum_scatter(
        jnp.dot(attended, output_all, preferred_element_type=jnp.float32),
        "tp",
        scatter_dimension=0,
        tiled=True,
    )
    normed_mid = rms_scale(middle, gain_two).astype(jnp.bfloat16)
    mid_all = lax.all_gather(normed_mid, "tp", axis=0, tiled=True)
    hidden_pre = jnp.dot(mid_all, up_all, preferred_element_type=jnp.float32)
    hidden = jax.nn.gelu(hidden_pre).astype(jnp.bfloat16)
    mixed = middle + lax.psum_scatter(
        jnp.dot(hidden, down_all, preferred_element_type=jnp.float32),
        "tp",
        scatter_dimension=0,
        tiled=True,
    )
    grad_rows = lax.all_gather(grad_mixed, "tp", axis=0, tiled=True)
    grad_hidden = jnp.einsum("rd,fd->rf", grad_rows, down_all, preferred_element_type=jnp.float32)
    grad_pre = jax.vjp(jax.nn.gelu, hidden_pre)[1](grad_hidden)[0].astype(jnp.bfloat16)
    grad_down = jnp.einsum("rf,rd->fd", hidden, grad_rows, preferred_element_type=jnp.float32)
    grad_up = jnp.einsum("rd,rf->df", mid_all, grad_pre, preferred_element_type=jnp.float32)
    grad_mid_normed = lax.psum_scatter(
        jnp.einsum("rf,df->rd", grad_pre, up_all, preferred_element_type=jnp.float32),
        "tp",
        scatter_dimension=0,
        tiled=True,
    )
    grad_middle_part, grad_gain_two = jax.vjp(rms_scale, middle, gain_two)[1](grad_mid_normed)
    grad_middle = grad_mixed.astype(jnp.float32) + grad_middle_part
    grad_branch = lax.all_gather(grad_middle.astype(jnp.bfloat16), "tp", axis=0, tiled=True)
    grad_output = jnp.einsum("rc,rd->cd", attended, grad_branch, preferred_element_type=jnp.float32)
    grad_attended = jnp.einsum(
        "rd,cd->rc", grad_branch, output_all, preferred_element_type=jnp.float32
    ).astype(jnp.bfloat16)
    grad_blocks = jnp.moveaxis(
        grad_attended.reshape(seq_count, NB, BLK, heads_here, head_dim), 1, 0
    )
    backward_block = jax.vmap(
        block_backward, in_axes=(None, None, None, 0, 0, 0, 0, 0, 0, 0, 0, 0, 0, None, 0, 0)
    )

    def backward_step(carried_in, entries):
        grad_memory, keys_later, values_later, sum_state, sum_update, sum_gate = carried_in
        (
            memory,
            queries,
            keys_now,
            values_now,
            keys_before,
            values_before,
            grad_out,
            state_out,
            log_total,
            state_log,
            block_id,
        ) = entries
        results = backward_block(
            state_all,
            update_all,
            retain,
            memory,
            queries,
            keys_now,
            values_now,
            keys_before,
            values_before,
            grad_out,
            state_out,
            log_total,
            state_log,
            block_id,
            lengths,
            grad_memory,
        )
        (
            grad_prior,
            grad_queries,
            grad_keys,
            grad_values,
            grad_keys_before,
            grad_values_before,
            part_state,
            part_update,
            part_gate,
        ) = results
        carried_out = (
            grad_prior,
            grad_keys_before,
            grad_values_before,
            sum_state + jnp.sum(part_state, axis=0),
            sum_update + jnp.sum(part_update, axis=0),
            sum_gate + jnp.sum(part_gate, axis=0),
        )
        return (carried_out, (grad_queries, grad_keys + keys_later, grad_values + values_later))

    zero_block = jnp.zeros((seq_count, BLK, heads_here, head_dim), jnp.float32)
    start_carry = (
        grad_final.astype(jnp.float32).reshape(seq_count, S, heads_here, head_dim),
        zero_block,
        zero_block,
        jnp.zeros(state_all.shape, jnp.float32),
        jnp.zeros(update_all.shape, jnp.float32),
        jnp.zeros(retain.shape, jnp.float32),
    )
    final_carry, grad_parts = lax.scan(
        backward_step,
        start_carry,
        (
            memories,
            blocked[0],
            blocked[1],
            blocked[2],
            earlier[1],
            earlier[2],
            grad_blocks,
            state_outs,
            log_totals,
            state_logs,
            block_ids,
        ),
        reverse=True,
    )
    grad_memory_start, unused_keys, unused_values, grad_state_w, grad_update_w, grad_gate_w = (
        final_carry
    )
    grad_qkv = jnp.stack(
        [jnp.moveaxis(member, 0, 1).reshape(group_rows, width_here) for member in grad_parts]
    ).astype(jnp.bfloat16)
    grad_memory_start = grad_memory_start.reshape(seq_count, S, width_here)
    restarted = restart[:, None, None] > 0
    grad_carried = jnp.where(restarted, 0.0, grad_memory_start)
    grad_initial = jnp.sum(jnp.where(restarted, grad_memory_start, 0.0), axis=0)
    grad_input = jnp.einsum("rd,krc->kdc", normed_all, grad_qkv, preferred_element_type=jnp.float32)
    grad_normed = lax.psum_scatter(
        jnp.einsum("krc,kdc->rd", grad_qkv, input_all, preferred_element_type=jnp.float32),
        "tp",
        scatter_dimension=0,
        tiled=True,
    )
    grad_tokens_part, grad_gain_one = jax.vjp(rms_scale, tokens_wide, gain_one)[1](grad_normed)
    grad_tokens = grad_middle + grad_tokens_part
    gain_one_sum, gain_two_sum = lax.psum((grad_gain_one, grad_gain_two), "tp")
    summed = (
        lax.psum_scatter(gain_one_sum, "dp", scatter_dimension=0, tiled=True),
        lax.psum_scatter(gain_two_sum, "dp", scatter_dimension=0, tiled=True),
        lax.psum_scatter(grad_input, "dp", scatter_dimension=1, tiled=True),
        lax.psum_scatter(grad_output, "dp", scatter_dimension=1, tiled=True),
        lax.psum_scatter(grad_state_w, "dp", scatter_dimension=1, tiled=True),
        lax.psum_scatter(grad_update_w, "dp", scatter_dimension=1, tiled=True),
        lax.psum_scatter(grad_gate_w, "dp", scatter_dimension=1, tiled=True),
        lax.psum_scatter(grad_initial, "dp", scatter_dimension=0, tiled=True),
        lax.psum_scatter(grad_up, "dp", scatter_dimension=0, tiled=True),
        lax.psum_scatter(grad_down, "dp", scatter_dimension=1, tiled=True),
    )
    (
        out_gain_one,
        out_gain_two,
        out_input,
        out_output,
        out_state,
        out_update,
        out_gate,
        out_initial,
        out_up,
        out_down,
    ) = summed
    return (
        mixed.astype(jnp.bfloat16),
        memory_end.reshape(seq_count, S, width_here),
        grad_tokens,
        grad_carried,
        out_gain_one,
        out_input,
        out_state,
        out_update,
        out_gate,
        out_initial,
        out_output,
        out_gain_two,
        out_up,
        out_down,
    )


BF16 = jnp.bfloat16
F32 = jnp.float32
HD = 128
TILE = 256
LOG2E = math.log2(math.e)
SCALING = HD ** (-0.5)
TO_POWER = SCALING * LOG2E
VMEM_BYTES = 60 * 1024 * 1024


def dot_nn(left, right):
    return jnp.dot(left, right, preferred_element_type=F32)


def dot_nt(left, right):
    return lax.dot_general(left, right, (((1,), (1,)), ((), ())), preferred_element_type=F32)


def call_params(**more):
    return pltpu.CompilerParams(vmem_limit_bytes=VMEM_BYTES, **more)


def cost(macs, moved, powers=0):
    return pl.CostEstimate(flops=2 * macs, bytes_accessed=moved, transcendentals=powers)


def whole(shape):
    return pl.BlockSpec(shape, lambda *_: (0,) * len(shape), pipeline_mode=pl.Buffered(1))


def project_kernel(x_ref, gain_ref, w_ref, normed_t_ref, out_ref, w_full):
    depth = w_ref.shape[1] // 3

    @pl.when(pl.program_id(0) == 0)
    def _():
        for i in range(3):
            part = w_ref[:, i * depth : (i + 1) * depth]
            w_full[i] = part.reshape(w_full.shape[1:])

    x = x_ref[...].astype(F32)
    scale = lax.rsqrt(jnp.mean(x * x, axis=-1, keepdims=True) + EPSILON)
    normed = (x * scale * gain_ref[...]).astype(BF16)
    normed_t_ref[...] = normed.T
    for i in range(3):
        out_ref[i] = dot_nn(normed, w_full[i]).astype(BF16)


def project(x, gain, packs, depth):
    rows, width = x.shape
    cols = packs.shape[2]
    return pl.pallas_call(
        project_kernel,
        grid=(rows // TILE,),
        in_specs=[
            pl.BlockSpec((TILE, width), lambda r: (r, 0)),
            whole((1, width)),
            whole((packs.shape[0], 3 * depth, cols)),
        ],
        out_specs=[
            pl.BlockSpec((width, TILE), lambda r: (0, r)),
            pl.BlockSpec((3, TILE, cols), lambda r: (0, r, 0)),
        ],
        out_shape=[
            jax.ShapeDtypeStruct((width, rows), BF16),
            jax.ShapeDtypeStruct((3, rows, cols), BF16),
        ],
        scratch_shapes=[pltpu.VMEM((3, width, cols), BF16)],
        compiler_params=call_params(),
        cost_estimate=cost(rows * width * 3 * cols, 6 * rows * width),
        name="project",
    )(x, gain, packs)


def tile_masks():
    key = lax.broadcasted_iota(jnp.int32, (TILE, TILE), 0)
    query = lax.broadcasted_iota(jnp.int32, (TILE, TILE), 1)
    return key, query


def token_tiles(t):
    return [(j, t - j) for j in range(max(0, t - 2), t + 1)]


def masked_scores(scores, tile, behind, length, key, query):
    if behind == 0:
        scores = jnp.where(key <= query, scores, NEGATIVE)
    elif behind == 2:
        scores = jnp.where(key > query, scores, NEGATIVE)
    if tile >= 2 * (NB - 1):
        scores = jnp.where(key + tile * TILE < length, scores, NEGATIVE)
    return scores


def softmax_columns(tiles):
    peak = functools.reduce(jnp.maximum, [jnp.max(s, axis=0, keepdims=True) for s in tiles])
    peak = peak * TO_POWER
    powers = [jnp.exp2(s * TO_POWER - peak) for s in tiles]
    total = functools.reduce(jnp.add, [jnp.sum(p, axis=0, keepdims=True) for p in powers])
    return [p.astype(BF16) for p in powers], total, peak + jnp.log2(total)


def first_memory(flags_ref, carried_ref, initial_ref):
    initial = initial_ref[...].reshape(carried_ref.shape).astype(F32)
    return jnp.where(flags_ref[0, 0] > 0, initial, carried_ref[...].astype(F32))


def attend_kernel(
    flags_ref,
    q_ref,
    k_ref,
    v_ref,
    carried_ref,
    initial_ref,
    ws_ref,
    wu_ref,
    gate_ref,
    out_ref,
    state_out_ref,
    log_ref,
    state_log_ref,
    final_ref,
    vt_ref,
):
    length = flags_ref[0, 1]
    key, query = tile_masks()
    retain = jax.nn.sigmoid(gate_ref[0])
    memory = first_memory(flags_ref, carried_ref, initial_ref)
    vt_ref[...] = v_ref[0].T
    for c in range(NB):
        lo = c * BLK
        state = dot_nn(memory.astype(BF16), ws_ref[0]).astype(BF16)
        sq, sk, sv = state[:, :HD], state[:, HD : 2 * HD], state[:, 2 * HD :]
        svt = sv.T
        jobs = []
        for t in range(2 * c, 2 * c + 2):
            q = q_ref[0, t * TILE : (t + 1) * TILE]
            spans = token_tiles(t)
            tiles = [
                masked_scores(
                    dot_nt(k_ref[0, j * TILE : (j + 1) * TILE], q), j, behind, length, key, query
                )
                for j, behind in spans
            ]
            jobs.append((tiles + [dot_nt(sk, q)], spans[0][0] * TILE, (t + 1) * TILE))
        for u in range(2):
            q = sq[u * TILE : (u + 1) * TILE]
            tiles = [
                masked_scores(
                    dot_nt(k_ref[0, j * TILE : (j + 1) * TILE], q), j, 1, length, key, query
                )
                for j in (2 * c, 2 * c + 1)
            ]
            jobs.append((tiles + [dot_nt(sk, q)], lo, lo + BLK))
        shares = [softmax_columns(tiles) for tiles, _, _ in jobs]
        for u, ((powers, total, logs), (_, first, stop)) in enumerate(zip(shares, jobs)):
            out = dot_nn(vt_ref[:, first:stop], jnp.concatenate(powers[:-1], axis=0))
            out = out + dot_nn(svt, powers[-1])
            out = (out / total).T.astype(BF16)
            rows = slice(lo + u % 2 * TILE, lo + (u % 2 + 1) * TILE)
            if u < 2:
                out_ref[rows] = out
                log_ref[0, :, rows] = logs
            else:
                state_out_ref[rows] = out
                state_log_ref[0, :, rows] = logs
        update = dot_nn(state_out_ref[lo : lo + BLK], wu_ref[0])
        blended = retain * memory + (1.0 - retain) * update
        memory = jnp.where(lo < length, blended, memory)
    final_ref[...] = memory


def head_block(rows):
    return pl.BlockSpec((rows, HD), lambda h: (0, h))


def initial_block(packs, at, first=0):
    length = S // packs.shape[0]
    return pl.BlockSpec((packs.shape[0], length, HD), lambda h: (0, at // length, first + h))


def attend(flags, projected, carried, packs, initial_at, states, gate):
    rows = projected.shape[1]
    heads = states.shape[0]
    return pl.pallas_call(
        attend_kernel,
        grid=(heads,),
        in_specs=[
            pl.BlockSpec(memory_space=pltpu.SMEM),
            pl.BlockSpec((1, rows, HD), lambda h: (0, 0, h)),
            pl.BlockSpec((1, rows, HD), lambda h: (1, 0, h)),
            pl.BlockSpec((1, rows, HD), lambda h: (2, 0, h)),
            head_block(S),
            initial_block(packs, initial_at),
            pl.BlockSpec((1, HD, 3 * HD), lambda h: (h, 0, 0)),
            pl.BlockSpec((1, HD, HD), lambda h: (h, 0, 3)),
            pl.BlockSpec((1, 1, HD), lambda h: (h, 0, 0)),
        ],
        out_specs=[
            head_block(rows),
            head_block(NB * S),
            pl.BlockSpec((1, 1, rows), lambda h: (h, 0, 0)),
            pl.BlockSpec((1, 1, NB * S), lambda h: (h, 0, 0)),
            head_block(S),
        ],
        out_shape=[
            jax.ShapeDtypeStruct((rows, heads * HD), BF16),
            jax.ShapeDtypeStruct((NB * S, heads * HD), BF16),
            jax.ShapeDtypeStruct((heads, 1, rows), F32),
            jax.ShapeDtypeStruct((heads, 1, NB * S), F32),
            jax.ShapeDtypeStruct((S, heads * HD), F32),
        ],
        scratch_shapes=[pltpu.VMEM((HD, rows), BF16)],
        compiler_params=call_params(),
        cost_estimate=cost(
            heads * NB * BLK * HD * 2 * (1152 + 1024),
            heads * HD * (rows * 10 + S * 8),
            heads * NB * BLK * 2176,
        ),
        name="attend",
    )(flags, projected, projected, projected, carried, packs, states, states, gate)


def attend_back_kernel(
    spots,
    flags_ref,
    q_ref,
    k_ref,
    v_ref,
    carried_ref,
    initial_ref,
    ws_ref,
    wu_ref,
    gate_ref,
    out_ref,
    state_out_ref,
    log_ref,
    state_log_ref,
    go_ref,
    grad_final_ref,
    nt_any,
    w_ref,
    *refs,
):
    load_sems, nt_ref, *late = refs[-13:-9] if len(refs) > 17 else refs[-11:-9]
    kt_ref, dk_ref, dv_ref, dqkv_ref, acc_ref, p_ref, ds_ref, qcat_ref, gocat_ref = refs[-9:]
    last = len(refs) > 17
    if last:
        core_ref, x_any, sum_any = refs[:3]
        sum_ref, x_ref = late
        dws_ref, dwu_ref, dgate_ref, dmemory_ref, dw_ref, own_ref, give_ref, dgain_ref = refs[3:-13]
    else:
        dws_ref, dwu_ref, dgate_ref, dmemory_ref, dw_ref, out_gy_ref = refs[:-11]
    step = pl.program_id(0)
    loads = [pltpu.make_async_copy(nt_any, nt_ref, load_sems.at[0])]
    if last:
        loads += [
            pltpu.make_async_copy(sum_any, sum_ref, load_sems.at[1]),
            pltpu.make_async_copy(x_any, x_ref, load_sems.at[2]),
        ]

    @pl.when(step == 0)
    def _():
        for load in loads:
            load.start()
        acc_ref[...] = jnp.zeros_like(acc_ref)

    length = flags_ref[0, 1]
    key, query = tile_masks()
    retain = jax.nn.sigmoid(gate_ref[0])
    ws = ws_ref[0]
    wu = wu_ref[0]
    kt_ref[...] = k_ref[0].T
    dk_ref[...] = jnp.zeros_like(dk_ref)
    dv_ref[...] = jnp.zeros_like(dv_ref)
    memories = [first_memory(flags_ref, carried_ref, initial_ref)]
    for c in range(NB - 1):
        update = dot_nn(state_out_ref[c * S : (c + 1) * S], wu)
        blended = retain * memories[c] + (1.0 - retain) * update
        memories.append(jnp.where(c * BLK < length, blended, memories[c]))
    grad_memory = grad_final_ref[...].astype(F32)
    dws = jnp.zeros(ws.shape, F32)
    dwu = jnp.zeros(wu.shape, F32)
    dgate = jnp.zeros(retain.shape, F32)
    for c in reversed(range(NB)):
        lo = c * BLK
        active = lo < length
        memory = memories[c]
        memory_low = memory.astype(BF16)
        state = dot_nn(memory_low, ws).astype(BF16)
        sq, sk, sv = state[:, :HD], state[:, HD : 2 * HD], state[:, 2 * HD :]
        skt = sk.T
        state_out = state_out_ref[lo : lo + S]
        update = dot_nn(state_out, wu)
        grad_blend = jnp.where(active, grad_memory, 0.0)
        grad_update = ((1.0 - retain) * grad_blend).astype(BF16)
        dgate = dgate + jnp.sum(grad_blend * (memory - update), axis=0, keepdims=True)
        dwu = dwu + dot_nn(state_out.T, grad_update)
        grad_state_out = dot_nt(grad_update, wu).astype(BF16)
        grad_memory = jnp.where(active, retain * grad_memory, grad_memory)
        deltas = jnp.sum((grad_state_out.astype(F32) * state_out.astype(F32)).T, axis=0, keepdims=True)
        qcat_ref[:BLK] = q_ref[0, lo : lo + BLK]
        qcat_ref[BLK:] = sq
        gocat_ref[:BLK] = go_ref[lo : lo + BLK]
        gocat_ref[BLK:] = grad_state_out
        base = lo - BLK
        state_rows = slice(2 * BLK, 2 * BLK + S)
        jobs = []
        for u in range(4):
            part = slice(u * TILE, (u + 1) * TILE)
            q = qcat_ref[part]
            go = gocat_ref[part]
            if u < 2:
                t = 2 * c + u
                slots = [(j - 2 * (c - 1), j, behind) for j, behind in token_tiles(t)]
            else:
                slots = [(2, 2 * c, 1), (3, 2 * c + 1, 1)]
            tiles = []
            for slot, j, behind in slots:
                rows = slice(j * TILE, (j + 1) * TILE)
                s = masked_scores(dot_nt(k_ref[0, rows], q), j, behind, length, key, query)
                at = slice(slot * TILE, (slot + 1) * TILE)
                tiles.append((at, s, dot_nt(v_ref[0, rows], go)))
            tiles.append((state_rows, dot_nt(sk, q), dot_nt(sv, go)))
            span = slice(slots[0][0] * TILE, (slots[-1][0] + 1) * TILE)
            jobs.append((part, tiles, span))
        for u, (part, tiles, _) in enumerate(jobs):
            if u < 2:
                here = slice(lo + u * TILE, lo + (u + 1) * TILE)
                logs = log_ref[0, :, here]
                pairs = (go_ref[here].astype(F32) * out_ref[here].astype(F32)).T
                delta = jnp.sum(pairs, axis=0, keepdims=True)
            else:
                logs = state_log_ref[0, :, lo + (u - 2) * TILE : lo + (u - 1) * TILE]
                delta = deltas[:, (u - 2) * TILE : (u - 1) * TILE]
            for at, s, gp in tiles:
                p = jnp.exp2(s * TO_POWER - logs)
                p_ref[at, part] = p.astype(BF16)
                ds_ref[at, part] = (p * (gp - delta)).astype(BF16)
        dqs = []
        for u, (part, _, span) in enumerate(jobs):
            keys = slice(base + span.start, base + span.stop)
            dq = dot_nn(kt_ref[:, keys], ds_ref[span, part])
            dq = dq + dot_nn(skt, ds_ref[state_rows, part])
            if u < 2:
                here = slice(lo + u * TILE, lo + (u + 1) * TILE)
                dqkv_ref[here, :HD] = (dq.T * SCALING).astype(BF16)
            else:
                dqs.append(dq.T)
        for slot, (first, stop) in enumerate(((0, 1), (0, 2), (0, 4), (1, 4))):
            if base + slot * TILE < 0:
                continue
            rows = slice(base + slot * TILE, base + (slot + 1) * TILE)
            at = slice(slot * TILE, (slot + 1) * TILE)
            span = slice(first * TILE, stop * TILE)
            dv_ref[rows] += dot_nn(p_ref[at, span], gocat_ref[span])
            dk_ref[rows] += dot_nn(ds_ref[at, span], qcat_ref[span])
        dsv = dot_nn(p_ref[state_rows], gocat_ref[...])
        dsk = dot_nn(ds_ref[state_rows], qcat_ref[...])
        dsq = dqs
        grad_state = jnp.concatenate(
            [jnp.concatenate(dsq, axis=0) * SCALING, dsk * SCALING, dsv], axis=1
        ).astype(BF16)
        grad_memory = grad_memory + dot_nt(grad_state, ws)
        dws = dws + dot_nn(memory_low.T, grad_state)
    dqkv_ref[:, HD : 2 * HD] = (dk_ref[...] * SCALING).astype(BF16)
    dqkv_ref[:, 2 * HD :] = dv_ref[...].astype(BF16)
    dws_ref[0] = dws
    dwu_ref[0] = dwu
    dgate_ref[0] = dgate * retain * (1.0 - retain)
    dmemory_ref[...] = grad_memory
    depth = w_ref.shape[1] // 3

    @pl.when(step == 0)
    def _():
        loads[0].wait()

    wide = dqkv_ref[...]
    weights = jnp.concatenate(
        [w_ref[:, i * depth : (i + 1) * depth].reshape(nt_ref.shape[0], HD) for i in range(3)],
        axis=1,
    )
    acc_ref[...] += dot_nt(wide, weights)
    product = dot_nn(nt_ref[...], wide).astype(BF16)
    low = depth // 2
    for block in range(w_ref.shape[0]):
        chip, t = block // 2, block % 2
        lead = (spots[chip], t)
        for i in range(3):
            at = lead + (slice(i * low, (i + 1) * low),)
            piece = product[block * depth : (block + 1) * depth, i * HD : (i + 1) * HD]
            dw_ref[at + (slice(0, HD),)] = piece[:low]
            dw_ref[at + (slice(HD, 2 * HD),)] = piece[low:]

    @pl.when(step == pl.num_programs(0) - 1)
    def _():
        if not last:
            out_gy_ref[...] = acc_ref[...].astype(BF16)
            return
        for load in loads[1:]:
            load.wait()
        acc_ref[...] += sum_ref[...].astype(F32)
        half = own_ref.shape[0]
        core = core_ref[0]
        own = pl.ds(pl.multiple_of(core * half, half), half)
        give = pl.ds(pl.multiple_of((1 - core) * half, half), half)
        own_ref[...] = acc_ref[own, :].astype(BF16)
        give_ref[...] = acc_ref[give, :].astype(BF16)
        dgain = jnp.zeros_like(dgain_ref)
        for r in range(acc_ref.shape[0] // TILE):
            rows = slice(r * TILE, (r + 1) * TILE)
            x = x_ref[rows].astype(F32)
            scale = lax.rsqrt(jnp.mean(x * x, axis=-1, keepdims=True) + EPSILON)
            dgain = dgain + jnp.sum(acc_ref[rows] * x * scale, axis=0, keepdims=True)
        dgain_ref[...] = dgain


def attend_back(
    first,
    heads,
    spots,
    flags,
    projected,
    carried,
    packs,
    initial_at,
    states,
    gate,
    out,
    state_out,
    logs,
    state_logs,
    go,
    grad_final,
    normed_t,
    depth,
    more=(),
):
    rows = projected.shape[1]
    width = normed_t.shape[0]
    slices = packs.shape[0]
    chips = slices // 2
    per_head = lambda a, b: pl.BlockSpec((1, a, b), lambda h: (first + h, 0, 0))
    new_head = lambda a, b: pl.BlockSpec((1, a, b), lambda h: (h, 0, 0))
    in_head = lambda rows: pl.BlockSpec((rows, HD), lambda h: (0, first + h))
    part = lambda i: pl.BlockSpec((1, rows, HD), lambda h: (i, 0, first + h))
    lanes = 2 * HD
    piece = lambda rows: pl.BlockSpec((chips, 2, rows, lanes), lambda h: (0, 0, 0, h))
    shape = jax.ShapeDtypeStruct
    low = 3 * (depth // 2)
    lead = (chips, 2)
    if more:
        anywhere = pl.BlockSpec(memory_space=pl.ANY)
        extra = [pl.BlockSpec(memory_space=pltpu.SMEM)] + [anywhere] * 2
        late = [pltpu.VMEM((rows, width), BF16)] * 2
        operands = more
        outs = [shape((rows // 2, width), BF16)] * 2 + [shape((1, width), F32)]
    else:
        extra = []
        late = []
        operands = ()
        outs = [shape((rows, width), BF16)]
    return pl.pallas_call(
        functools.partial(attend_back_kernel, spots),
        grid=(heads,),
        in_specs=[
            pl.BlockSpec(memory_space=pltpu.SMEM),
            part(0),
            part(1),
            part(2),
            in_head(S),
            initial_block(packs, initial_at, first),
            per_head(HD, 3 * HD),
            pl.BlockSpec((1, HD, HD), lambda h: (first + h, 0, 3)),
            per_head(1, HD),
            in_head(rows),
            in_head(NB * S),
            per_head(1, rows),
            per_head(1, NB * S),
            in_head(rows),
            in_head(S),
            pl.BlockSpec(memory_space=pl.ANY),
            pl.BlockSpec((slices, 3 * depth, HD), lambda h: (0, 0, first + h)),
        ]
        + extra,
        out_specs=[
            new_head(HD, 3 * HD),
            new_head(HD, HD),
            new_head(1, HD),
            head_block(S),
            pl.BlockSpec(lead + (low, lanes), lambda h: (0, 0, 0, h)),
        ]
        + [whole(v.shape) for v in outs],
        out_shape=[
            shape((heads, HD, 3 * HD), F32),
            shape((heads, HD, HD), F32),
            shape((heads, 1, HD), F32),
            shape((S, heads * HD), F32),
            shape(lead + (low, heads * lanes), BF16),
        ]
        + outs,
        scratch_shapes=[pltpu.SemaphoreType.DMA((3,)), pltpu.VMEM(normed_t.shape, BF16)]
        + late
        + [
            pltpu.VMEM((HD, rows), BF16),
            pltpu.VMEM((rows, HD), F32),
            pltpu.VMEM((rows, HD), F32),
            pltpu.VMEM((rows, 3 * HD), BF16),
            pltpu.VMEM((rows, width), F32),
            pltpu.VMEM((2 * BLK + S, BLK + S), BF16),
            pltpu.VMEM((2 * BLK + S, BLK + S), BF16),
            pltpu.VMEM((BLK + S, HD), BF16),
            pltpu.VMEM((BLK + S, HD), BF16),
        ],
        compiler_params=call_params(),
        cost_estimate=cost(
            heads * NB * BLK * HD * (5 * (1152 + 1024) + 6 * width),
            heads * HD * (rows * 20 + S * 16) + 8 * rows * width,
            heads * NB * BLK * 2176,
        ),
        name="attend_back",
    )(
        flags,
        projected,
        projected,
        projected,
        carried,
        packs,
        states,
        states,
        gate,
        out,
        state_out,
        logs,
        state_logs,
        go,
        grad_final,
        normed_t,
        packs,
        *operands,
    )


def middle_kernel(
    core_ref,
    x_ref,
    own_ref,
    sib_ref,
    wo_own_ref,
    wo_sib_ref,
    gain_ref,
    g_here_ref,
    g_came_ref,
    g_other_ref,
    mid_ref,
    n_ref,
    g_ref,
):
    mine = pl.program_id(0) * 2 // pl.num_programs(0) == core_ref[0]
    own = jnp.where(core_ref[0] == core_ref[1], g_here_ref[...], g_came_ref[...])
    g = jnp.where(mine, own, g_other_ref[...])
    g_ref[...] = g
    wo_own = wo_own_ref[...].reshape(wo_sib_ref.shape)
    middle = x_ref[...].astype(F32) + dot_nt(own_ref[...], wo_own)
    middle = middle + dot_nt(sib_ref[...], wo_sib_ref[...])
    scale = lax.rsqrt(jnp.mean(middle * middle, axis=-1, keepdims=True) + EPSILON)
    normed = (middle * scale * gain_ref[...]).astype(BF16)
    mid_ref[...] = middle.astype(BF16)
    n_ref[...] = normed


def output_block(packs, depth):
    return pl.BlockSpec(
        (packs.shape[0], depth, packs.shape[2]),
        lambda *_: (0, 3, 0),
        pipeline_mode=pl.Buffered(1),
    )


def form_middle(core, x, own, sib, packs, depth, wo_sib, gain, *grads):
    rows, width = x.shape
    half = own.shape[1]
    row_block = lambda cols: pl.BlockSpec((TILE, cols), lambda r: (r, 0))
    half_tiles = rows // TILE // 2
    half_block = pl.BlockSpec((TILE, width), lambda r: (r % half_tiles, 0))
    return pl.pallas_call(
        middle_kernel,
        grid=(rows // TILE,),
        in_specs=[
            pl.BlockSpec(memory_space=pltpu.SMEM),
            row_block(width),
            row_block(half),
            row_block(half),
            output_block(packs, depth),
            whole(wo_sib.shape),
            whole(gain.shape),
            half_block,
            half_block,
            half_block,
        ],
        out_specs=[row_block(width)] * 3,
        out_shape=[jax.ShapeDtypeStruct((rows, width), BF16)] * 3,
        compiler_params=call_params(),
        cost_estimate=cost(2 * rows * width * half, 12 * rows * width),
        name="form_middle",
    )(core, x, own, sib, packs, wo_sib, gain, *grads)


ROOT = math.sqrt(2.0 / math.pi)
CUBIC = 0.044715


def feed_kernel(
    place, spots, core_ref, n_ref, g_ref, up_ref, dn_ref, *refs
):
    last = len(refs) > 8
    if last:
        ff_in, gn_in, ff_out, gn_out, dw_ref = refs[:5]
    else:
        ff_out, gn_out, dw_ref = refs[:3]
    w_full, hid_ref, grad_ref, nt_ref, gt_ref = refs[-5:]
    step = pl.program_id(0)
    depth = dw_ref.shape[3]

    @pl.when(step == 0)
    def _():
        for i, ref in enumerate((up_ref, dn_ref)):
            for block, p in enumerate(spots):
                w_full[i, block * depth : (block + 1) * depth] = ref[p]

    up = w_full[0]
    dn = w_full[1]
    here = pl.ds(pl.multiple_of(step * n_ref.shape[0], TILE), n_ref.shape[0])
    pre = dot_nn(n_ref[...], up)
    square = pre * pre
    bend = jnp.tanh(ROOT * pre * (1.0 + CUBIC * square))
    half = 0.5 * (1.0 + bend)
    hid = (pre * half).astype(BF16)
    slope = half + (0.5 * ROOT) * pre * (1.0 - bend * bend) * (1.0 + 3.0 * CUBIC * square)
    grad = (dot_nn(g_ref[...], dn) * slope).astype(BF16)
    hid_ref[here, :] = hid
    grad_ref[here, :] = grad
    nt_ref[:, here] = n_ref[...].T
    gt_ref[:, here] = g_ref[...].T
    ff = dot_nt(hid, dn)
    gn = dot_nt(grad, up)
    if last:
        ff = ff + ff_in[...].astype(F32)
        gn = gn + gn_in[...].astype(F32)
    ff_out[...] = ff.astype(BF16)
    gn_out[...] = gn.astype(BF16)

    @pl.when(step == pl.num_programs(0) - 1)
    def _():
        for i, (left, right) in enumerate(((nt_ref, grad_ref), (gt_ref, hid_ref))):
            for at in range(0, left.shape[0], TILE):
                product = dot_nn(left[at : at + TILE], right[...]).astype(BF16)
                for t in range(TILE // depth):
                    block = at // depth + t
                    piece = product[t * depth : (t + 1) * depth]
                    dw_ref[place[block // 2], block % 2, i] = piece


def feed(place, spots, core, normed, grad, weights, units, sums=()):
    rows, width = normed.shape
    pieces, depth = weights.shape[:2]
    row_block = pl.BlockSpec((TILE, width), lambda r: (r, 0))
    piece_block = lambda at: pl.BlockSpec(
        (pieces, depth, units), lambda r: (0, 0, at), pipeline_mode=pl.Buffered(1)
    )
    grad_shape = jax.ShapeDtypeStruct((pieces // 2, 2, 2, depth, units), BF16)
    full = jax.ShapeDtypeStruct((rows, width), BF16)
    return pl.pallas_call(
        functools.partial(feed_kernel, place, spots),
        grid=(rows // TILE,),
        in_specs=[
            pl.BlockSpec(memory_space=pltpu.SMEM),
            row_block,
            row_block,
            piece_block(0),
            piece_block(1),
        ]
        + [row_block for _ in sums],
        out_specs=[row_block, row_block, whole(grad_shape.shape)],
        out_shape=[full, full, grad_shape],
        scratch_shapes=[
            pltpu.VMEM((2, width, units), BF16),
            pltpu.VMEM((rows, units), BF16),
            pltpu.VMEM((rows, units), BF16),
            pltpu.VMEM((width, rows), BF16),
            pltpu.VMEM((width, rows), BF16),
        ],
        compiler_params=call_params(),
        cost_estimate=cost(
            6 * rows * width * units, 14 * rows * width + 8 * width * units, rows * units
        ),
        name="feed",
    )(core, normed, grad, weights, weights, *sums)


def norm_back(values, gain, grad):
    scale = lax.rsqrt(jnp.mean(values * values, axis=-1, keepdims=True) + EPSILON)
    weighted = grad * gain
    mean = jnp.mean(values * weighted, axis=-1, keepdims=True)
    out = scale * weighted - values * (scale * scale * scale * mean)
    return out, jnp.sum(grad * values * scale, axis=0, keepdims=True)


def middle_back_kernel(
    g_ref, mid_ref, own_ref, sib_ref, gain_ref, wo_ref, att_ref, gm_ref, ga_ref, dwo_ref, dgain_ref, acc
):
    step = pl.program_id(0)
    gy = own_ref[...].astype(F32) + sib_ref[...].astype(F32)
    back, dgain = norm_back(mid_ref[...].astype(F32), gain_ref[...], gy)
    grad_middle = g_ref[...].astype(F32) + back
    branch = grad_middle.astype(BF16)
    gm_ref[...] = branch
    wo = wo_ref[...].reshape(branch.shape[1], ga_ref.shape[1])
    ga_ref[...] = dot_nn(branch, wo).astype(BF16)

    @pl.when(step == 0)
    def _():
        acc[...] = jnp.zeros_like(acc)
        dgain_ref[...] = jnp.zeros_like(dgain_ref)

    acc[...] += dot_nn(branch.T, att_ref[...])
    dgain_ref[...] += dgain

    @pl.when(step == pl.num_programs(0) - 1)
    def _():
        piece = dwo_ref.shape[1]
        for chip in range(dwo_ref.shape[0]):
            dwo_ref[chip] = acc[chip * piece : (chip + 1) * piece, :].astype(BF16)


def middle_back(chips, g, middle, own, sib, gain, packs, depth, att):
    rows, width = g.shape
    half = att.shape[1]
    row_block = lambda cols: pl.BlockSpec((TILE, cols), lambda r: (r, 0))
    pieces = (chips, width // chips, half)
    return pl.pallas_call(
        middle_back_kernel,
        grid=(rows // TILE,),
        in_specs=[
            row_block(width),
            row_block(width),
            row_block(width),
            row_block(width),
            whole(gain.shape),
            output_block(packs, depth),
            row_block(half),
        ],
        out_specs=[row_block(width), row_block(half), whole(pieces), whole((1, width))],
        out_shape=[
            jax.ShapeDtypeStruct((rows, width), BF16),
            jax.ShapeDtypeStruct((rows, half), BF16),
            jax.ShapeDtypeStruct(pieces, BF16),
            jax.ShapeDtypeStruct((1, width), F32),
        ],
        scratch_shapes=[pltpu.VMEM((width, half), F32)],
        compiler_params=call_params(),
        cost_estimate=cost(2 * rows * width * half, 16 * rows * width),
        name="middle_back",
    )(g, middle, own, sib, gain, packs, att)


def ring_order(count):
    evens = list(range(0, count, 2))
    odds = list(range(1, count, 2))
    return evens + odds[::-1]


MESH = pl.DeviceIdType.MESH


def entry_kernel(
    order,
    cut,
    tok_ref,
    carried_ref,
    final_ref,
    w_ref,
    states_ref,
    updates_ref,
    gate_ref,
    gain_one_ref,
    gain_two_ref,
    initial_ref,
    wo_ref,
    up_ref,
    down_ref,
    restart_ref,
    length_ref,
    x_ref,
    memory_ref,
    grad_final_ref,
    packs_ref,
    feed_one_ref,
    feed_two_ref,
    flags_ref,
    wo_sib_ref,
    pack_ref,
    own_one_ref,
    own_two_ref,
    low_ref,
    flag_ref,
    *sems,
):
    (
        turn_send,
        turn_recv,
        rows_send,
        rows_recv,
        sib_send,
        sib_recv,
        wo_send,
        wo_recv,
        ring_send,
        ring_recv,
    ) = sems
    chips = len(order)
    dp = lax.axis_index("dp")
    y = lax.axis_index("tp")
    k = dp // 2
    c = dp % 2
    stays = c == y
    moves = jnp.logical_not(stays)
    partner = (2 * k + 1 - c, 1 - y)
    sibling = (2 * k + 1 - c, y)
    opposite = (dp, 1 - y)
    place = [order.index(i) for i in range(chips)]

    def chip_after(steps):
        found = jnp.int32(0)
        for i in range(chips):
            onward = order[(place[i] + steps) % chips]
            back = order[(place[i] - steps) % chips]
            found = jnp.where(k == i, jnp.where(c == 0, onward, back), found)
        return found

    following = (2 * chip_after(1) + c, y)
    previous = (2 * chip_after(-1) + c, y)
    barrier = pltpu.get_barrier_semaphore()
    for device in (sibling, opposite, following, previous):
        pl.semaphore_signal(barrier, inc=1, device_id=device, device_id_type=MESH)

    @pl.when(moves)
    def _():
        pl.semaphore_signal(barrier, inc=1, device_id=partner, device_id_type=MESH)

    parts, depth, cols = w_ref.shape
    heads, state_len, state_cols = states_ref.shape
    for i in range(parts):
        pack_ref[i * depth : (i + 1) * depth] = w_ref[i]
    at = parts * depth
    wo_rows = slice(at, at + depth)
    pack_ref[wo_rows] = wo_ref[...]
    at += depth
    for h in range(heads):
        rows = slice(at + h * state_len, at + (h + 1) * state_len)
        pack_ref[rows, :state_cols] = states_ref[h]
        pack_ref[rows, state_cols:] = updates_ref[h]
    at += heads * state_len
    pack_ref[at : at + initial_ref.shape[0]] = initial_ref[...]
    at += initial_ref.shape[0]
    pack_ref[at:] = jnp.zeros((pack_ref.shape[0] - at, cols), BF16)
    pack_ref[at : at + heads, :state_len] = gate_ref[...]
    pack_ref[at + heads : at + heads + 1, :depth] = gain_one_ref[...]
    pack_ref[at + heads + 1 : at + heads + 2, :depth] = gain_two_ref[...]
    lane = lax.broadcasted_iota(jnp.int32, flag_ref.shape, 1)
    flag_ref[...] = jnp.where(lane == 0, restart_ref[0], length_ref[0])

    def remote(src, dst, send_sem, recv_sem, device):
        return pltpu.make_async_remote_copy(
            src_ref=src,
            dst_ref=dst,
            send_sem=send_sem,
            recv_sem=recv_sem,
            device_id=device,
            device_id_type=MESH,
        )

    own_block = 2 * k + y
    other_block = 2 * k + 1 - y
    turns = [
        (pack_ref, packs_ref.at[2 * k + c]),
        (flag_ref, flags_ref),
        (own_one_ref, feed_one_ref.at[c]),
        (own_two_ref, feed_two_ref.at[c]),
        (low_ref, memory_ref),
        (final_ref, grad_final_ref),
    ]

    def turn(i):
        src, dst = turns[i]
        return remote(src, dst, turn_send.at[i], turn_recv.at[i], partner)

    pieces = rows_send.shape[0]
    size = tok_ref.shape[0] // pieces

    def swap(i, half):
        rows = pl.ds(i * size, size)
        return remote(
            tok_ref.at[rows], x_ref.at[half, rows], rows_send.at[i], rows_recv.at[i], partner
        )

    def share(i, source, half):
        rows = pl.ds(i * size, size)
        return remote(
            source.at[rows], x_ref.at[half, rows], sib_send.at[i], sib_recv.at[i], sibling
        )

    second = (jnp.where(stays, dp, 2 * k + 1 - c), jnp.where(stays, 1 - y, y))
    seconds = [
        (pack_ref, packs_ref, 2 * k + c, other_block),
        (own_one_ref, feed_one_ref, c, 1 - y),
        (own_two_ref, feed_two_ref, c, 1 - y),
    ]

    def aside(n, arriving=False):
        src, dst, there, here = seconds[n]
        at = here if arriving else there
        last = len(turns) + n
        return remote(src, dst.at[at], turn_send.at[last], turn_recv.at[last], second)

    wo_span = pl.ds(parts * depth, depth)

    def share_wo(block):
        return remote(
            packs_ref.at[block, wo_span],
            wo_sib_ref.at[block],
            wo_send.at[block],
            wo_recv.at[block],
            sibling,
        )

    def ring(src, block, step, j):
        return remote(
            src, packs_ref.at[block], ring_send.at[step, j], ring_recv.at[step, j], following
        )

    @pl.when(stays)
    def _():
        pl.semaphore_wait(barrier, 4)
        aside(0).start()
        ring(pack_ref, own_block, 0, 0).start()
        for i in range(pieces):
            share(i, tok_ref, c).start()

    @pl.when(moves)
    def _():
        pl.semaphore_wait(barrier, 5)
        turn(0).start()
        turn(1).start()
        aside(0).start()

    units = up_ref.shape[1]
    own_one_ref[:, :cut] = up_ref[:, :cut]
    own_one_ref[:, cut:] = down_ref[:, :cut]
    own_two_ref[:, : units - cut] = up_ref[:, cut:]
    own_two_ref[:, units - cut :] = down_ref[:, cut:]
    low_ref[...] = carried_ref[...].astype(BF16)

    @pl.when(moves)
    def _():
        remote(
            pack_ref, packs_ref.at[own_block], turn_send.at[0], turn_recv.at[0], partner
        ).wait_recv()
        ring(packs_ref.at[own_block], own_block, 0, 0).start()
        for i in range(pieces):
            swap(i, 1 - c).start()
        for i in range(2, len(turns)):
            turn(i).start()

    for n in (1, 2):
        aside(n).start()

    @pl.when(stays)
    def _():
        packs_ref[own_block] = pack_ref[...]
        flags_ref[...] = flag_ref[...]
        feed_one_ref[y] = own_one_ref[...]
        feed_two_ref[y] = own_two_ref[...]
        x_ref[c] = tok_ref[...]
        memory_ref[...] = low_ref[...]
        grad_final_ref[...] = final_ref[...]

    def forward(i):
        @pl.when(moves)
        def _():
            swap(i, c).wait_recv()
            share(i, x_ref.at[c], c).start()

    share_wo(own_block).start()
    aside(0, True).wait_recv()
    ring(packs_ref.at[other_block], other_block, 0, 1).start()
    share_wo(other_block).start()
    for step in range(1, chips):
        chip = chip_after(-step)
        for j in range(2):
            block = 2 * chip + jnp.where(j == 0, y, 1 - y)
            ring(packs_ref.at[block], block, step - 1, j).wait_recv()
            if step < chips - 1:
                ring(packs_ref.at[block], block, step, j).start()
            share_wo(block).start()
        if step >= chips - 3:
            forward(step - chips + 3)
    for i in range(3, pieces):
        forward(i)

    @pl.when(moves)
    def _():
        for i in range(1, len(turns)):
            turn(i).wait_recv()

    for i in range(pieces):
        share(i, tok_ref, 1 - c).wait_recv()
        share(i, tok_ref, c).wait_send()
    for block in range(2 * chips):
        share_wo(block).wait_recv()
        share_wo(block).wait_send()
    for n in (1, 2):
        aside(n, True).wait_recv()
    for n in range(len(seconds)):
        aside(n).wait_send()
    for step in range(chips - 1):
        for j in range(2):
            ring(pack_ref, own_block, step, j).wait_send()

    @pl.when(moves)
    def _():
        for i in range(len(turns)):
            turn(i).wait_send()
        for i in range(pieces):
            swap(i, 1 - c).wait_send()


def enter(
    order,
    cut,
    tokens,
    carried,
    grad_final,
    w_in,
    states,
    updates,
    gate,
    gain_one,
    gain_two,
    initial,
    wo,
    up,
    down,
    restart,
    lengths,
):
    chips = len(order)
    pieces = 4
    depth, cols = w_in.shape[1:]
    units = up.shape[1]
    heads, state_len = gate.shape
    pack = (4 * depth + heads * state_len + initial.shape[0] + 16, cols)
    feed_one = (depth, 2 * cut)
    feed_two = (depth, 2 * (units - cut))
    dma = pltpu.SemaphoreType.DMA
    in_vmem = pl.BlockSpec(memory_space=pltpu.VMEM)
    in_smem = pl.BlockSpec(memory_space=pltpu.SMEM)
    shape = jax.ShapeDtypeStruct
    return pl.pallas_call(
        functools.partial(entry_kernel, tuple(order), cut),
        in_specs=[in_vmem] * 13 + [in_smem] * 2,
        out_specs=[in_vmem] * 8,
        out_shape=[
            shape((2,) + tokens.shape, BF16),
            shape(carried.shape, BF16),
            shape(grad_final.shape, BF16),
            shape((2 * chips,) + pack, BF16),
            shape((2,) + feed_one, BF16),
            shape((2,) + feed_two, BF16),
            shape((1, 128), jnp.int32),
            shape((2 * chips, depth, cols), BF16),
        ],
        scratch_shapes=[
            pltpu.VMEM(pack, BF16),
            pltpu.VMEM(feed_one, BF16),
            pltpu.VMEM(feed_two, BF16),
            pltpu.VMEM(carried.shape, BF16),
            pltpu.VMEM((1, 128), jnp.int32),
            dma((9,)),
            dma((9,)),
            dma((pieces,)),
            dma((pieces,)),
            dma((pieces,)),
            dma((pieces,)),
            dma((2 * chips,)),
            dma((2 * chips,)),
            dma((chips - 1, 2)),
            dma((chips - 1, 2)),
        ],
        compiler_params=call_params(collective_id=0, has_side_effects=True),
        cost_estimate=cost(0, 16 * tokens.size),
        name="enter",
    )(
        tokens,
        carried,
        grad_final,
        w_in,
        states,
        updates,
        gate,
        gain_one.reshape(1, -1),
        gain_two.reshape(1, -1),
        initial,
        wo,
        up,
        down,
        restart,
        lengths,
    )


def exit_kernel(
    order,
    dw_ref,
    dwo_ref,
    ready_refs,
    dws_refs,
    dwu_refs,
    dgate_refs,
    dmemory_refs,
    dgain_one_ref,
    dgain_two_ref,
    flags_ref,
    gy_own_ref,
    gy_give_ref,
    gain_ref,
    x_any,
    gm_any,
    gt_ref,
    gc_ref,
    turned_ref,
    ready_turned_refs,
    piece_ref,
    initial_ref,
    gain_ref_all,
    first_ref,
    ring_ref,
    gy_sib_ref,
    result_ref,
    carried_ref,
    x_ref,
    gm_ref,
    gain_sib_ref,
    over_refs,
    beside_refs,
    ready_sems,
    load_sems,
    gain_sems,
    sib_send,
    sib_recv,
    rows_send,
    rows_recv,
    ring_send,
    ring_recv,
    carried_sems,
):
    chips = len(order)
    dp = lax.axis_index("dp")
    y = lax.axis_index("tp")
    k = dp // 2
    c = dp % 2
    stays = c == y
    moves = jnp.logical_not(stays)
    partner = (2 * k + 1 - c, 1 - y)
    sibling = (2 * k + 1 - c, y)
    opposite = (dp, 1 - y)
    place = [order.index(i) for i in range(chips)]

    def chip_after(steps):
        found = jnp.int32(0)
        for i in range(chips):
            onward = order[(place[i] + steps) % chips]
            back = order[(place[i] - steps) % chips]
            found = jnp.where(k == i, jnp.where(c == 0, onward, back), found)
        return found

    following = (2 * chip_after(1) + c, y)
    previous = (2 * chip_after(-1) + c, y)
    barrier = pltpu.get_barrier_semaphore()
    for device in (sibling, opposite, following, previous):
        pl.semaphore_signal(barrier, inc=1, device_id=device, device_id_type=MESH)

    @pl.when(moves)
    def _():
        pl.semaphore_signal(barrier, inc=1, device_id=partner, device_id_type=MESH)

    loads = [
        pltpu.make_async_copy(x_any.at[c], x_ref, load_sems.at[0]),
        pltpu.make_async_copy(gm_any.at[c], gm_ref, load_sems.at[1]),
    ]
    for load in loads:
        load.start()

    def remote(src, dst, send_sem, recv_sem, device):
        return pltpu.make_async_remote_copy(
            src_ref=src,
            dst_ref=dst,
            send_sem=send_sem,
            recv_sem=recv_sem,
            device_id=device,
            device_id_type=MESH,
        )

    pieces = sib_send.shape[0]
    size = gy_own_ref.shape[0] // pieces
    in_rows, lanes_in = dw_ref.shape[2:]
    gain_swap = remote(dgain_one_ref, gain_sib_ref, gain_sems.at[0], gain_sems.at[1], sibling)
    carried_turn = remote(carried_ref, gc_ref, carried_sems.at[0], carried_sems.at[1], partner)

    def give(i):
        rows = pl.ds(i * size, size)
        return remote(
            gy_give_ref.at[rows], gy_sib_ref.at[rows], sib_send.at[i], sib_recv.at[i], sibling
        )

    def swap(i):
        rows = pl.ds(i * size, size)
        return remote(
            result_ref.at[rows], gt_ref.at[rows], rows_send.at[i], rows_recv.at[i], partner
        )

    big_rows = in_rows + dwo_ref.shape[2]
    bounds = ((0, big_rows), (big_rows, first_ref.shape[1] - big_rows))

    def ring(src, step, j, part):
        rows = pl.ds(*bounds[part])
        return remote(
            src.at[rows],
            ring_ref.at[step, j, rows],
            ring_send.at[step, j, part],
            ring_recv.at[step, j, part],
            following,
        )

    many = len(ready_refs)

    def other_and_mine(n):
        if n < many:
            return ready_refs[n].at[1 - c], ready_refs[n].at[c]
        return ring_ref.at[chips - 2, 0], ring_ref.at[chips - 2, 1]

    def sends(n):
        sems = ready_sems.at[n]
        other, mine = other_and_mine(n)
        return (
            lambda: remote(other, beside_refs[n], sems.at[0], sems.at[3], sibling),
            lambda: remote(mine, over_refs[n], sems.at[0], sems.at[2], opposite),
            lambda: remote(other, over_refs[n], sems.at[1], sems.at[2], partner),
        )

    def deliver(n):
        beside, over, skew = sends(n)

        @pl.when(stays)
        def _():
            beside().start()

        @pl.when(moves)
        def _():
            over().start()
            skew().start()

    def collect(n, out_ref):
        beside, over, skew = sends(n)
        over().wait_recv()

        @pl.when(stays)
        def _():
            mine = other_and_mine(n)[1]
            out_ref[...] = (mine[...].astype(F32) + over_refs[n][...].astype(F32)).astype(BF16)

        @pl.when(moves)
        def _():
            beside().wait_recv()
            out_ref[...] = (
                beside_refs[n][...].astype(F32) + over_refs[n][...].astype(F32)
            ).astype(BF16)

    def delivered(n):
        beside, over, skew = sends(n)

        @pl.when(stays)
        def _():
            beside().wait_send()

        @pl.when(moves)
        def _():
            over().wait_send()
            skew().wait_send()

    @pl.when(stays)
    def _():
        pl.semaphore_wait(barrier, 4)

    @pl.when(moves)
    def _():
        pl.semaphore_wait(barrier, 5)

    slice_of = [1 - c, c]
    start = chip_after(-1)
    gain_swap.start()
    for j in range(2):
        first_ref[j, :in_rows] = dw_ref[start, slice_of[j]]
        first_ref[j, in_rows:big_rows] = dwo_ref[start, slice_of[j]]
        ring(first_ref.at[j], 0, j, 0).start()
    for i in range(pieces):
        give(i).start()
    for n in range(many):
        deliver(n)

    restarted = flags_ref[0, 0] > 0
    dmemory = jnp.concatenate([ref[...] for ref in dmemory_refs], axis=1)
    initial_ref[...] = jnp.where(restarted, dmemory, 0.0)
    kept = jnp.where(restarted, 0.0, dmemory).astype(BF16)

    part_heads, head_dim, state_cols = dws_refs[0].shape
    heads = part_heads * len(dws_refs)
    state_len = head_dim // (2 * chips)
    init_len = initial_ref.shape[0] // (2 * chips)
    cols = initial_ref.shape[1]
    states = heads * state_len
    tail = states + init_len
    piece_ref[tail:] = jnp.zeros_like(piece_ref[tail:])
    for h in range(heads):
        n, i = h // part_heads, h % part_heads
        piece_ref[tail + h : tail + h + 1, :head_dim] = dgate_refs[n][i]
    for i in range(dgain_two_ref.shape[1] // cols):
        lanes = slice(i * cols, (i + 1) * cols)
        piece_ref[tail + 6 + i : tail + 7 + i] = dgain_two_ref[:, lanes]
    gain_swap.wait_recv()
    gain_ref_all[...] = dgain_one_ref[...] + gain_sib_ref[...]
    for i in range(dgain_two_ref.shape[1] // cols):
        lanes = slice(i * cols, (i + 1) * cols)
        piece_ref[tail + 4 + i : tail + 5 + i] = gain_ref_all[:, lanes]

    def small_piece(chip, j):
        block = 2 * chip + slice_of[j]
        lines = pl.ds(pl.multiple_of(block * state_len, state_len), state_len)
        for h in range(heads):
            rows = slice(h * state_len, (h + 1) * state_len)
            n, i = h // part_heads, h % part_heads
            piece_ref[rows, :state_cols] = dws_refs[n][i, lines, :]
            piece_ref[rows, state_cols:] = dwu_refs[n][i, lines, :]
        lines = pl.ds(pl.multiple_of(block * init_len, init_len), init_len)
        piece_ref[states:tail] = initial_ref[lines, :]
        return piece_ref[...]

    for j in range(2):
        first_ref[j, big_rows:] = small_piece(start, j).astype(BF16)
        ring(first_ref.at[j], 0, j, 1).start()

    @pl.when(stays)
    def _():
        gc_ref[...] = kept

    @pl.when(moves)
    def _():
        carried_ref[...] = kept
        carried_turn.start()

    for load in loads:
        load.wait()
    gain_one = gain_ref[...]

    def token_rows(i):
        rows = slice(i * size, (i + 1) * size)
        give(i).wait_recv()
        gy = gy_own_ref[rows].astype(F32) + gy_sib_ref[rows].astype(F32)
        back, _ = norm_back(x_ref[rows].astype(F32), gain_one, gy)
        grad = (gm_ref[rows].astype(F32) + back).astype(BF16)

        @pl.when(stays)
        def _():
            gt_ref[rows] = grad

        @pl.when(moves)
        def _():
            result_ref[rows] = grad
            swap(i).start()

    token_rows(0)
    tasks = [functools.partial(token_rows, i) for i in range(1, pieces)]
    for step in range(chips - 1):
        chip = chip_after(-step - 2)
        for j in range(2):
            for part in range(2):
                ring(first_ref.at[j], step, j, part).wait_recv()
                if part == 0:
                    terms = [(0, dw_ref[chip, slice_of[j]]), (in_rows, dwo_ref[chip, slice_of[j]])]
                else:
                    terms = [(big_rows, small_piece(chip, j))]
                for at, term in terms:
                    rows = slice(at, at + term.shape[0])
                    ring_ref[step, j, rows] = (
                        ring_ref[step, j, rows].astype(F32) + term.astype(F32)
                    ).astype(BF16)
                if step < chips - 2:
                    ring(ring_ref.at[step, j], step + 1, j, part).start()
        if tasks and step < chips - 2:
            tasks.pop(0)()
    deliver(many)
    for task in tasks:
        task()
    for n in range(many):
        collect(n, ready_turned_refs[n])
    collect(many, turned_ref)

    @pl.when(moves)
    def _():
        for i in range(pieces):
            swap(i).wait_recv()
        carried_turn.wait_recv()

    gain_swap.wait_send()
    for i in range(pieces):
        give(i).wait_send()
    for n in range(many + 1):
        delivered(n)
    for step in range(chips - 1):
        for j in range(2):
            for part in range(2):
                ring(first_ref.at[j], step, j, part).wait_send()

    @pl.when(moves)
    def _():
        carried_turn.wait_send()
        for i in range(pieces):
            swap(i).wait_send()


def leave(
    order,
    dw,
    dwo,
    ready,
    dws,
    dwu,
    dgate,
    dmemory,
    dgain_one,
    dgain_two,
    flags,
    gy_own,
    gy_give,
    gain,
    x,
    gm,
):
    chips = len(order)
    pieces = 4
    many = len(ready)
    parts = len(dws)
    half, width = gy_own.shape
    in_rows, cols = dw.shape[2:]
    heads, head_dim, state_cols = dws[0].shape
    heads = heads * parts
    small = heads * head_dim // (2 * chips) + S // (2 * chips) + 16
    message = (in_rows + dwo.shape[2] + small, cols)
    dma = pltpu.SemaphoreType.DMA
    in_vmem = pl.BlockSpec(memory_space=pltpu.VMEM)
    anywhere = pl.BlockSpec(memory_space=pl.ANY)
    shape = jax.ShapeDtypeStruct
    sum_scratch = tuple(pltpu.VMEM(v.shape[1:], BF16) for v in ready) + (pltpu.VMEM(message, BF16),)
    inputs = (dw, dwo, *ready, *dws, *dwu, *dgate, *dmemory)

    def kernel(*refs):
        at = 2 + many
        groups = [refs[1], refs[2:at]]
        groups += [refs[at + parts * i : at + parts * (i + 1)] for i in range(4)]
        at = len(inputs) + 11
        rest = refs[len(inputs) : at]
        turned = refs[at : at + many]
        exit_kernel(tuple(order), refs[0], *groups, *rest, turned, *refs[at + many :])

    outs = pl.pallas_call(
        kernel,
        in_specs=[in_vmem] * (len(inputs) + 2)
        + [pl.BlockSpec(memory_space=pltpu.SMEM)]
        + [in_vmem] * 3
        + [anywhere] * 2,
        out_specs=[in_vmem] * (3 + many),
        out_shape=[shape((half, width), BF16), shape((S, cols), BF16), shape(message, BF16)]
        + [shape(v.shape[1:], BF16) for v in ready],
        scratch_shapes=[
            pltpu.VMEM((small, cols), F32),
            pltpu.VMEM((S, cols), F32),
            pltpu.VMEM((1, width), F32),
            pltpu.VMEM((2,) + message, BF16),
            pltpu.VMEM((chips - 1, 2) + message, BF16),
            pltpu.VMEM((half, width), BF16),
            pltpu.VMEM((half, width), BF16),
            pltpu.VMEM((S, cols), BF16),
            pltpu.VMEM((half, width), BF16),
            pltpu.VMEM((half, width), BF16),
            pltpu.VMEM((1, width), F32),
            sum_scratch,
            sum_scratch,
            dma((many + 1, 4)),
            dma((2,)),
            dma((2,)),
            dma((pieces,)),
            dma((pieces,)),
            dma((pieces,)),
            dma((pieces,)),
            dma((chips - 1, 2, 2)),
            dma((chips - 1, 2, 2)),
            dma((2,)),
        ],
        compiler_params=call_params(collective_id=1, has_side_effects=True),
        cost_estimate=cost(0, 30 * half * width),
        name="leave",
    )(*inputs, dgain_one, dgain_two, flags, gy_own, gy_give, gain, x, gm)
    return outs[0], outs[1], outs[2], outs[3:]


def unpack_kernel(
    core_ref,
    gt_ref,
    gc_ref,
    last_ref,
    one_ref,
    two_ref,
    first_ref,
    out_gt_ref,
    out_gc_ref,
    out_in_ref,
    out_wo_ref,
    out_ws_ref,
    out_wu_ref,
    out_gate_ref,
    out_initial_ref,
    out_one_ref,
    out_two_ref,
    out_up_ref,
    out_down_ref,
):
    out_gt_ref[...] = gt_ref[...].astype(F32)
    out_gc_ref[...] = gc_ref[...].astype(F32)

    @pl.when(pl.program_id(0) == 0)
    def _():
        unpack_shards(
            core_ref[2],
            last_ref,
            one_ref,
            two_ref,
            first_ref,
            out_in_ref,
            out_wo_ref,
            out_ws_ref,
            out_wu_ref,
            out_gate_ref,
            out_initial_ref,
            out_one_ref,
            out_two_ref,
            out_up_ref,
            out_down_ref,
        )


def unpack_shards(
    block,
    last_ref,
    one_ref,
    two_ref,
    first_ref,
    out_in_ref,
    out_wo_ref,
    out_ws_ref,
    out_wu_ref,
    out_gate_ref,
    out_initial_ref,
    out_one_ref,
    out_two_ref,
    out_up_ref,
    out_down_ref,
):
    cut = one_ref.shape[2]
    for i, out in enumerate((out_up_ref, out_down_ref)):
        out[:, :cut] = one_ref[i].astype(F32)
        out[:, cut:] = two_ref[i].astype(F32)
    parts, depth, cols = out_in_ref.shape
    low = depth // 2
    pair = cols // HD // 2
    for n, ref in enumerate((first_ref, last_ref)):
        for i in range(parts):
            for h in range(pair):
                for t in range(2):
                    at = (2 * h + t) * HD
                    lanes = slice((n * pair + h) * HD, (n * pair + h + 1) * HD)
                    piece = ref[i * low : (i + 1) * low, at : at + HD]
                    out_in_ref[i, t * low : (t + 1) * low, lanes] = piece.astype(F32)
    out_wo_ref[...] = last_ref[parts * low : parts * low + depth].astype(F32)
    rest = last_ref[parts * low + depth :].astype(F32)
    heads, state_len, state_cols = out_ws_ref.shape
    for h in range(heads):
        rows = slice(h * state_len, (h + 1) * state_len)
        out_ws_ref[h] = rest[rows, :state_cols]
        out_wu_ref[h] = rest[rows, state_cols:]
    at = heads * state_len
    out_initial_ref[...] = rest[at : at + out_initial_ref.shape[0]]
    at += out_initial_ref.shape[0]
    gates = rest[at : at + heads, :HD]
    gains = [jnp.concatenate([rest[r : r + 1], rest[r + 1 : r + 2]], axis=1) for r in (at + 4, at + 6)]
    out_gate_ref[...] = jnp.zeros_like(out_gate_ref)
    for i in range(HD // state_len):

        @pl.when(block == i)
        def _():
            out_gate_ref[...] = gates[:, i * state_len : (i + 1) * state_len]
            for out, gain in zip((out_one_ref, out_two_ref), gains):
                out[...] = gain[:, i * depth : (i + 1) * depth]


def unpack(core, arrays, shapes):
    gt, gc = arrays[:2]
    shape = lambda dims: jax.ShapeDtypeStruct(dims, F32)
    steps = 4
    rows_of = lambda v: pl.BlockSpec((v.shape[0] // steps, v.shape[1]), lambda r: (r, 0))
    return pl.pallas_call(
        unpack_kernel,
        grid=(steps,),
        in_specs=[pl.BlockSpec(memory_space=pltpu.SMEM)]
        + [rows_of(v) for v in (gt, gc)]
        + [whole(v.shape) for v in arrays[2:]],
        out_specs=[rows_of(v) for v in (gt, gc)]
        + [whole(dims) for dims in shapes],
        out_shape=[shape(v.shape) for v in (gt, gc)]
        + [shape(dims) for dims in shapes],
        compiler_params=call_params(),
        cost_estimate=cost(0, 6 * gt.size),
        name="unpack",
    )(core, *arrays)


def tie(*values):
    return lax.optimization_barrier(values)


class Paths:
    def __init__(self, chips):
        self.order = ring_order(chips)
        self.place = tuple(self.order.index(k) for k in range(chips))
        index = lambda k, c, y: (2 * k + c) * 2 + y
        every = [(k, c, y) for k in range(chips) for c in range(2) for y in range(2)]
        self.turned = [(index(k, c, y), index(k, y, c)) for k, c, y in every if c != y]
        self.other = [
            (index(k, c, y), index(k, 1 - c, y) if c == y else index(k, c, 1 - y))
            for k, c, y in every
        ]
        self.across = [(index(k, c, y), index(k, c, 1 - y)) for k, c, y in every]
        self.sibling = [(index(k, c, y), index(k, 1 - c, y)) for k, c, y in every]
        self.rings = [[2 * k + c for k in self.order] for c in range(2)]
        self.spots = tuple(2 * self.place[b // 2] + b % 2 for b in range(2 * chips))
        self.chips = chips

    def send(self, values, pairs):
        return lax.ppermute(values, ("dp", "tp"), pairs)

    def turn(self, values):
        stays = lax.axis_index("dp") % 2 == lax.axis_index("tp")
        return jnp.where(stays, values, self.send(values, self.turned))

    def gather(self, values):
        return lax.all_gather(values, "dp", axis=0, tiled=False, axis_index_groups=self.rings)

    def reduce(self, values):
        return lax.psum_scatter(
            values, "dp", scatter_dimension=0, tiled=False, axis_index_groups=self.rings
        )


def body(
    chips,
    tokens,
    carried,
    restart,
    lengths,
    gain_attend,
    input_weights,
    state_weights,
    update_weights,
    gate_bias,
    initial_state,
    output_weights,
    gain_feed,
    feed_up,
    feed_down,
    grad_mixed,
    grad_final,
):
    paths = Paths(chips)
    send, place = paths.send, paths.place
    y = lax.axis_index("tp")
    c = lax.axis_index("dp") % 2
    core = jnp.stack([c, y, lax.axis_index("dp")])
    heads, state_len = gate_bias.shape
    depth = input_weights.shape[1]
    cols = heads * HD
    slices = 2 * chips
    gate_len = heads * state_len
    half_rows = tokens.shape[0]

    units = feed_up.shape[1]
    cut = units // 2
    entered = enter(
        paths.order,
        cut,
        tokens,
        carried[0],
        grad_final[0],
        input_weights,
        state_weights,
        update_weights,
        gate_bias,
        gain_attend,
        gain_feed,
        initial_state,
        output_weights.T,
        feed_up,
        feed_down.T,
        restart,
        lengths,
    )
    entered, grad_mixed = tie(entered, grad_mixed)
    x, carried_own, grad_final_own, packs, first_feed, second_feed, flags, wo_sib = entered
    wo_sib = wo_sib.reshape(-1, cols)
    x = x.reshape(2 * half_rows, -1)
    first_feed = paths.gather(first_feed).reshape(slices, depth, -1)
    second_feed = paths.gather(second_feed).reshape(slices, depth, -1)
    states_at = 4 * depth
    initial_at = states_at + gate_len
    tail_at = initial_at + initial_state.shape[0]
    small = packs[:, tail_at : tail_at + heads + 2, :depth].astype(F32)
    gain_one = small[:, heads].reshape(1, -1)
    gain_two = small[:, heads + 1].reshape(1, -1)
    gate = jnp.moveaxis(small[:, :heads, :state_len], 1, 0).reshape(heads, 1, HD)
    states = packs[:, states_at:initial_at].reshape(slices, heads, state_len, 4 * HD)
    states = jnp.moveaxis(states, 1, 0).reshape(heads, HD, 4 * HD)
    g_came = send(grad_mixed, paths.turned)
    g_other = send(grad_mixed, paths.other)
    normed_t, projected = project(x, gain_one, packs, depth)
    attended, state_out, logs, state_logs, memory_end = attend(
        flags, projected, carried_own, packs, initial_at, states, gate
    )
    attended, g_came, g_other = tie(attended, g_came, g_other)
    attended_sib = send(attended, paths.sibling)
    middle, normed, g = form_middle(
        core, x, attended, attended_sib, packs, depth, wo_sib, gain_two, grad_mixed, g_came, g_other
    )
    ff, gn, feed_grad = feed(
        place, paths.spots, core, normed, g, first_feed, cut
    )
    feed_one = paths.reduce(feed_grad)
    ff, gn, feed_grad = feed(
        place,
        paths.spots,
        core,
        normed,
        g,
        second_feed,
        units - cut,
        (ff, gn),
    )
    feed_two = paths.reduce(feed_grad)
    half_of = lambda values, at: lax.dynamic_slice_in_dim(values, at * half_rows, half_rows)
    gn_sib = send(gn, paths.sibling)
    grad_middle, grad_attended, dwo, dgain_two = middle_back(
        chips, g, middle, gn, gn_sib, gain_two, packs, depth, attended
    )
    grad_attended, ff = tie(grad_attended, ff)
    ff_sib = send(half_of(ff, 1 - c), paths.sibling)

    pair = heads // 2

    def back(n, spots, grad, **more):
        return attend_back(
            n * pair,
            pair,
            spots,
            flags,
            projected,
            carried_own,
            packs,
            initial_at,
            states,
            gate,
            attended,
            state_out,
            logs,
            state_logs,
            grad,
            grad_final_own,
            normed_t,
            depth,
            **more,
        )

    left = back(0, place, grad_attended)
    left, ff_sib, grad_attended, feed_one = tie(left, ff_sib, grad_attended, feed_one)
    first_sum = paths.reduce(left[4])
    mixed_own = half_of(middle, c).astype(F32) + half_of(ff, c).astype(F32) + ff_sib.astype(F32)
    mixed_own, memory_end, grad_attended = tie(mixed_own.astype(BF16), memory_end, grad_attended)
    mixed_came = send(mixed_own, paths.turned)
    memory_came = send(memory_end, paths.turned)
    right = back(1, tuple(range(chips)), grad_attended, more=(core, x, left[5]))
    right, mixed_came, memory_came, feed_two = tie(right, mixed_came, memory_came, feed_two)
    stays = c == y
    mixed = jnp.where(stays, mixed_own, mixed_came)
    final_memory = jnp.where(stays, memory_end, memory_came)
    right, mixed, final_memory = tie(right, mixed, final_memory)
    dws, dwu, dgate, dmemory, (_, dw_right) = list(zip(left, right))[:5]
    gy_own, gy_give, dgain_one = right[5:]
    gt, gc, last, ready = leave(
        paths.order,
        dw_right,
        dwo.reshape(chips, 2, depth, cols),
        (feed_one, feed_two, first_sum),
        dws,
        dwu,
        dgate,
        dmemory,
        dgain_one,
        dgain_two,
        flags,
        gy_own,
        gy_give,
        gain_one,
        x.reshape(2, half_rows, -1),
        grad_middle.reshape(2, half_rows, -1),
    )
    (
        grad_tokens,
        grad_carried,
        out_input,
        out_output,
        out_state,
        out_update,
        out_gate,
        out_initial,
        out_one,
        out_two,
        out_up,
        out_down,
    ) = unpack(
        core,
        (gt, gc, last, *ready),
        (
            input_weights.shape,
            (depth, cols),
            state_weights.shape,
            update_weights.shape,
            gate_bias.shape,
            initial_state.shape,
            (1, depth),
            (1, depth),
            (depth, units),
            (depth, units),
        ),
    )
    return (
        mixed,
        final_memory[None],
        grad_tokens,
        grad_carried[None],
        out_one[0],
        out_input,
        out_state,
        out_update,
        out_gate,
        out_initial,
        out_output.T,
        out_two[0],
        out_up,
        out_down.T,
    )


def solution(mesh):
    ranks, groups = mesh.shape["dp"], mesh.shape["tp"]
    chosen = functools.partial(body, ranks // 2) if groups == 2 else general_body
    placed = (
        P(("dp", "tp"), None),
        P("dp", None, "tp"),
        P("dp"),
        P("dp"),
        P("dp"),
        P(None, "dp", "tp"),
        P("tp", "dp", None),
        P("tp", "dp", None),
        P("tp", "dp"),
        P("dp", "tp"),
        P("tp", "dp"),
        P("dp"),
        P("dp", "tp"),
        P("tp", "dp"),
        P(("dp", "tp"), None),
        P("dp", None, "tp"),
    )
    return jax.shard_map(
        chosen,
        mesh=mesh,
        in_specs=placed,
        out_specs=(
            P(("dp", "tp"), None),
            P("dp", None, "tp"),
            P(("dp", "tp"), None),
            P("dp", None, "tp"),
            P("dp"),
            P(None, "dp", "tp"),
            P("tp", "dp", None),
            P("tp", "dp", None),
            P("tp", "dp"),
            P("dp", "tp"),
            P("tp", "dp"),
            P("dp"),
            P("dp", "tp"),
            P("tp", "dp"),
        ),
        check_vma=False,
    )
```

```python
import functools
import math

import jax
import jax.numpy as jnp
from jax import lax
from jax.experimental import pallas as pl
from jax.experimental.pallas import tpu as pltpu
from jax.sharding import PartitionSpec as P

S = 512
BLK = 512
LEN = 1536
NB = 3


EPSILON = 1e-06
NEGATIVE = -1e30


def rms_scale(values, gain):
    return values * lax.rsqrt(jnp.mean(values * values, axis=-1, keepdims=True) + EPSILON) * gain


def block_masks(block_id, length, block_len, state_count):
    row_ids = jnp.arange(block_len, dtype=jnp.int32)
    places = block_id * block_len + row_ids
    key_places = jnp.concatenate([places - block_len, places])
    allowed = (
        (key_places[None, :] >= 0)
        & (key_places[None, :] < length)
        & (key_places[None, :] <= places[:, None])
        & (key_places[None, :] > places[:, None] - block_len)
    )
    state_open = jnp.ones((block_len, state_count), dtype=bool)
    allowed = jnp.concatenate([allowed, state_open], axis=1)
    usable = jnp.concatenate([places < length, jnp.ones((state_count,), dtype=bool)])
    return (allowed, usable)


def masked_softmax(scores, allowed):
    scores = jnp.where(allowed, scores, NEGATIVE)
    peak_val = jnp.max(scores, axis=-1, keepdims=True)
    powers = jnp.exp(scores - peak_val)
    totals = jnp.sum(powers, axis=-1, keepdims=True)
    return (powers / totals, peak_val + jnp.log(totals))


def recall_softmax(scores, allowed, log_total):
    return jnp.exp(jnp.where(allowed, scores, NEGATIVE) - log_total)


def state_project(memory, state_weights):
    head_dim = memory.shape[-1]
    projected = jnp.einsum(
        "shd,hde->she",
        memory.astype(jnp.bfloat16),
        state_weights,
        preferred_element_type=jnp.float32,
    ).astype(jnp.bfloat16)
    return (
        projected[..., :head_dim],
        projected[..., head_dim : 2 * head_dim],
        projected[..., 2 * head_dim :],
    )


def block_forward(
    state_weights,
    update_weights,
    retain,
    memory,
    queries,
    keys_now,
    values_now,
    keys_before,
    values_before,
    block_id,
    length,
):
    head_dim = queries.shape[-1]
    block_len = queries.shape[0]
    state_count = memory.shape[0]
    scaling = head_dim ** (-0.5)
    state_q, state_k, state_v = state_project(memory, state_weights)
    allowed, usable = block_masks(block_id, length, block_len, state_count)
    key_set = jnp.concatenate([keys_before, keys_now, state_k], axis=0)
    value_set = jnp.concatenate([values_before, values_now, state_v], axis=0)
    scores = (
        jnp.einsum("ihd,jhd->hij", queries, key_set, preferred_element_type=jnp.float32) * scaling
    )
    shares, log_total = masked_softmax(scores, allowed[None])
    outputs = jnp.einsum(
        "hij,jhd->ihd", shares.astype(jnp.bfloat16), value_set, preferred_element_type=jnp.float32
    ).astype(jnp.bfloat16)
    state_keys = jnp.concatenate([keys_now, state_k], axis=0)
    state_values = jnp.concatenate([values_now, state_v], axis=0)
    state_scores = (
        jnp.einsum("shd,jhd->hsj", state_q, state_keys, preferred_element_type=jnp.float32)
        * scaling
    )
    state_shares, state_log = masked_softmax(state_scores, usable[None, None])
    state_out = jnp.einsum(
        "hsj,jhd->shd",
        state_shares.astype(jnp.bfloat16),
        state_values,
        preferred_element_type=jnp.float32,
    ).astype(jnp.bfloat16)
    update = jnp.einsum(
        "shd,hde->she", state_out, update_weights, preferred_element_type=jnp.float32
    )
    blended = retain * memory + (1.0 - retain) * update
    active = block_id * block_len < length
    memory_next = jnp.where(active, blended, memory)
    return (memory_next, (outputs, state_out, log_total, state_log))


def block_backward(
    state_weights,
    update_weights,
    retain,
    memory,
    queries,
    keys_now,
    values_now,
    keys_before,
    values_before,
    grad_out,
    state_out,
    log_total,
    state_log,
    block_id,
    length,
    grad_next,
):
    head_dim = queries.shape[-1]
    block_len = queries.shape[0]
    state_count = memory.shape[0]
    scaling = head_dim ** (-0.5)
    span_end = 2 * block_len
    state_q, state_k, state_v = state_project(memory, state_weights)
    allowed, usable = block_masks(block_id, length, block_len, state_count)
    active = block_id * block_len < length
    update = jnp.einsum(
        "shd,hde->she", state_out, update_weights, preferred_element_type=jnp.float32
    )
    grad_blend = jnp.where(active, grad_next, 0.0)
    grad_memory = jnp.where(active, retain * grad_next, grad_next)
    grad_update = ((1.0 - retain) * grad_blend).astype(jnp.bfloat16)
    grad_gate = jnp.sum(grad_blend * (memory - update), axis=0) * retain * (1.0 - retain)
    grad_update_w = jnp.einsum(
        "shd,she->hde", state_out, grad_update, preferred_element_type=jnp.float32
    )
    grad_state_out = jnp.einsum(
        "she,hde->shd", grad_update, update_weights, preferred_element_type=jnp.float32
    ).astype(jnp.bfloat16)
    state_keys = jnp.concatenate([keys_now, state_k], axis=0)
    state_values = jnp.concatenate([values_now, state_v], axis=0)
    state_scores = (
        jnp.einsum("shd,jhd->hsj", state_q, state_keys, preferred_element_type=jnp.float32)
        * scaling
    )
    state_shares = recall_softmax(state_scores, usable[None, None], state_log)
    grad_state_shares = jnp.einsum(
        "shd,jhd->hsj", grad_state_out, state_values, preferred_element_type=jnp.float32
    )
    grad_state_scores = (
        state_shares
        * (grad_state_shares - jnp.sum(state_shares * grad_state_shares, axis=-1, keepdims=True))
    ).astype(jnp.bfloat16)
    grad_state_values = jnp.einsum(
        "hsj,shd->jhd",
        state_shares.astype(jnp.bfloat16),
        grad_state_out,
        preferred_element_type=jnp.float32,
    )
    grad_state_q = (
        jnp.einsum(
            "hsj,jhd->shd", grad_state_scores, state_keys, preferred_element_type=jnp.float32
        )
        * scaling
    )
    grad_state_keys = (
        jnp.einsum("hsj,shd->jhd", grad_state_scores, state_q, preferred_element_type=jnp.float32)
        * scaling
    )
    key_set = jnp.concatenate([keys_before, keys_now, state_k], axis=0)
    value_set = jnp.concatenate([values_before, values_now, state_v], axis=0)
    scores = (
        jnp.einsum("ihd,jhd->hij", queries, key_set, preferred_element_type=jnp.float32) * scaling
    )
    shares = recall_softmax(scores, allowed[None], log_total)
    grad_shares = jnp.einsum(
        "ihd,jhd->hij", grad_out, value_set, preferred_element_type=jnp.float32
    )
    grad_scores = (
        shares * (grad_shares - jnp.sum(shares * grad_shares, axis=-1, keepdims=True))
    ).astype(jnp.bfloat16)
    grad_values = jnp.einsum(
        "hij,ihd->jhd", shares.astype(jnp.bfloat16), grad_out, preferred_element_type=jnp.float32
    )
    grad_queries = (
        jnp.einsum("hij,jhd->ihd", grad_scores, key_set, preferred_element_type=jnp.float32)
        * scaling
    )
    grad_keys = (
        jnp.einsum("hij,ihd->jhd", grad_scores, queries, preferred_element_type=jnp.float32)
        * scaling
    )
    grad_keys_now = grad_keys[block_len:span_end] + grad_state_keys[:block_len]
    grad_values_now = grad_values[block_len:span_end] + grad_state_values[:block_len]
    grad_state_k = grad_keys[span_end:] + grad_state_keys[block_len:]
    grad_state_v = grad_values[span_end:] + grad_state_values[block_len:]
    grad_proj = jnp.concatenate([grad_state_q, grad_state_k, grad_state_v], axis=-1).astype(
        jnp.bfloat16
    )
    grad_memory = grad_memory + jnp.einsum(
        "she,hde->shd", grad_proj, state_weights, preferred_element_type=jnp.float32
    )
    grad_state_w = jnp.einsum(
        "shd,she->hde", memory.astype(jnp.bfloat16), grad_proj, preferred_element_type=jnp.float32
    )
    return (
        grad_memory,
        grad_queries,
        grad_keys_now,
        grad_values_now,
        grad_keys[:block_len],
        grad_values[:block_len],
        grad_state_w,
        grad_update_w,
        grad_gate,
    )


def general_body(
    tokens,
    carried,
    restart,
    lengths,
    gain_attend,
    input_weights,
    state_weights,
    update_weights,
    gate_bias,
    initial_state,
    output_weights,
    gain_feed,
    feed_up,
    feed_down,
    grad_mixed,
    grad_final,
):
    seq_count = lengths.shape[0]
    heads_here = gate_bias.shape[0]
    head_dim = update_weights.shape[-1]
    width_here = heads_here * head_dim
    group_rows = seq_count * LEN
    gathered = (
        lax.all_gather(gain_attend, "dp", axis=0, tiled=True),
        lax.all_gather(gain_feed, "dp", axis=0, tiled=True),
        lax.all_gather(input_weights, "dp", axis=1, tiled=True),
        lax.all_gather(output_weights, "dp", axis=1, tiled=True),
        lax.all_gather(state_weights, "dp", axis=1, tiled=True),
        lax.all_gather(update_weights, "dp", axis=1, tiled=True),
        lax.all_gather(gate_bias, "dp", axis=1, tiled=True),
        lax.all_gather(initial_state, "dp", axis=0, tiled=True),
        lax.all_gather(feed_up, "dp", axis=0, tiled=True),
        lax.all_gather(feed_down, "dp", axis=1, tiled=True),
    )
    (
        gain_attend_all,
        gain_feed_all,
        input_all,
        output_all,
        state_all,
        update_all,
        gate_all,
        initial_all,
        up_all,
        down_all,
    ) = gathered
    tokens_wide = tokens.astype(jnp.float32)
    gain_one = gain_attend_all.astype(jnp.float32)
    gain_two = gain_feed_all.astype(jnp.float32)
    normed = rms_scale(tokens_wide, gain_one).astype(jnp.bfloat16)
    normed_all = lax.all_gather(normed, "tp", axis=0, tiled=True)
    projected = jnp.einsum(
        "rd,kdc->krc", normed_all, input_all, preferred_element_type=jnp.float32
    ).astype(jnp.bfloat16)
    blocked = jnp.moveaxis(projected.reshape(3, seq_count, NB, BLK, heads_here, head_dim), 2, 1)
    earlier = jnp.concatenate([jnp.zeros_like(blocked[:, :1]), blocked[:, :-1]], axis=1)
    retain = jax.nn.sigmoid(gate_all.astype(jnp.float32))
    memory_start = jnp.where(
        restart[:, None, None] > 0, initial_all.astype(jnp.float32)[None], carried
    ).reshape(seq_count, S, heads_here, head_dim)
    forward_block = jax.vmap(block_forward, in_axes=(None, None, None, 0, 0, 0, 0, 0, 0, None, 0))
    block_ids = jnp.arange(NB, dtype=jnp.int32)

    def forward_step(memory, entries):
        queries, keys_now, values_now, keys_before, values_before, block_id = entries
        memory_next, saved = forward_block(
            state_all,
            update_all,
            retain,
            memory,
            queries,
            keys_now,
            values_now,
            keys_before,
            values_before,
            block_id,
            lengths,
        )
        return (memory_next, (memory, saved))

    memory_end, (memories, saved_all) = lax.scan(
        forward_step,
        memory_start,
        (blocked[0], blocked[1], blocked[2], earlier[1], earlier[2], block_ids),
    )
    outputs, state_outs, log_totals, state_logs = saved_all
    attended = jnp.moveaxis(outputs, 0, 1).reshape(group_rows, width_here)
    middle = tokens_wide + lax.psum_scatter(
        jnp.dot(attended, output_all, preferred_element_type=jnp.float32),
        "tp",
        scatter_dimension=0,
        tiled=True,
    )
    normed_mid = rms_scale(middle, gain_two).astype(jnp.bfloat16)
    mid_all = lax.all_gather(normed_mid, "tp", axis=0, tiled=True)
    hidden_pre = jnp.dot(mid_all, up_all, preferred_element_type=jnp.float32)
    hidden = jax.nn.gelu(hidden_pre).astype(jnp.bfloat16)
    mixed = middle + lax.psum_scatter(
        jnp.dot(hidden, down_all, preferred_element_type=jnp.float32),
        "tp",
        scatter_dimension=0,
        tiled=True,
    )
    grad_rows = lax.all_gather(grad_mixed, "tp", axis=0, tiled=True)
    grad_hidden = jnp.einsum("rd,fd->rf", grad_rows, down_all, preferred_element_type=jnp.float32)
    grad_pre = jax.vjp(jax.nn.gelu, hidden_pre)[1](grad_hidden)[0].astype(jnp.bfloat16)
    grad_down = jnp.einsum("rf,rd->fd", hidden, grad_rows, preferred_element_type=jnp.float32)
    grad_up = jnp.einsum("rd,rf->df", mid_all, grad_pre, preferred_element_type=jnp.float32)
    grad_mid_normed = lax.psum_scatter(
        jnp.einsum("rf,df->rd", grad_pre, up_all, preferred_element_type=jnp.float32),
        "tp",
        scatter_dimension=0,
        tiled=True,
    )
    grad_middle_part, grad_gain_two = jax.vjp(rms_scale, middle, gain_two)[1](grad_mid_normed)
    grad_middle = grad_mixed.astype(jnp.float32) + grad_middle_part
    grad_branch = lax.all_gather(grad_middle.astype(jnp.bfloat16), "tp", axis=0, tiled=True)
    grad_output = jnp.einsum("rc,rd->cd", attended, grad_branch, preferred_element_type=jnp.float32)
    grad_attended = jnp.einsum(
        "rd,cd->rc", grad_branch, output_all, preferred_element_type=jnp.float32
    ).astype(jnp.bfloat16)
    grad_blocks = jnp.moveaxis(
        grad_attended.reshape(seq_count, NB, BLK, heads_here, head_dim), 1, 0
    )
    backward_block = jax.vmap(
        block_backward, in_axes=(None, None, None, 0, 0, 0, 0, 0, 0, 0, 0, 0, 0, None, 0, 0)
    )

    def backward_step(carried_in, entries):
        grad_memory, keys_later, values_later, sum_state, sum_update, sum_gate = carried_in
        (
            memory,
            queries,
            keys_now,
            values_now,
            keys_before,
            values_before,
            grad_out,
            state_out,
            log_total,
            state_log,
            block_id,
        ) = entries
        results = backward_block(
            state_all,
            update_all,
            retain,
            memory,
            queries,
            keys_now,
            values_now,
            keys_before,
            values_before,
            grad_out,
            state_out,
            log_total,
            state_log,
            block_id,
            lengths,
            grad_memory,
        )
        (
            grad_prior,
            grad_queries,
            grad_keys,
            grad_values,
            grad_keys_before,
            grad_values_before,
            part_state,
            part_update,
            part_gate,
        ) = results
        carried_out = (
            grad_prior,
            grad_keys_before,
            grad_values_before,
            sum_state + jnp.sum(part_state, axis=0),
            sum_update + jnp.sum(part_update, axis=0),
            sum_gate + jnp.sum(part_gate, axis=0),
        )
        return (carried_out, (grad_queries, grad_keys + keys_later, grad_values + values_later))

    zero_block = jnp.zeros((seq_count, BLK, heads_here, head_dim), jnp.float32)
    start_carry = (
        grad_final.astype(jnp.float32).reshape(seq_count, S, heads_here, head_dim),
        zero_block,
        zero_block,
        jnp.zeros(state_all.shape, jnp.float32),
        jnp.zeros(update_all.shape, jnp.float32),
        jnp.zeros(retain.shape, jnp.float32),
    )
    final_carry, grad_parts = lax.scan(
        backward_step,
        start_carry,
        (
            memories,
            blocked[0],
            blocked[1],
            blocked[2],
            earlier[1],
            earlier[2],
            grad_blocks,
            state_outs,
            log_totals,
            state_logs,
            block_ids,
        ),
        reverse=True,
    )
    grad_memory_start, unused_keys, unused_values, grad_state_w, grad_update_w, grad_gate_w = (
        final_carry
    )
    grad_qkv = jnp.stack(
        [jnp.moveaxis(member, 0, 1).reshape(group_rows, width_here) for member in grad_parts]
    ).astype(jnp.bfloat16)
    grad_memory_start = grad_memory_start.reshape(seq_count, S, width_here)
    restarted = restart[:, None, None] > 0
    grad_carried = jnp.where(restarted, 0.0, grad_memory_start)
    grad_initial = jnp.sum(jnp.where(restarted, grad_memory_start, 0.0), axis=0)
    grad_input = jnp.einsum("rd,krc->kdc", normed_all, grad_qkv, preferred_element_type=jnp.float32)
    grad_normed = lax.psum_scatter(
        jnp.einsum("krc,kdc->rd", grad_qkv, input_all, preferred_element_type=jnp.float32),
        "tp",
        scatter_dimension=0,
        tiled=True,
    )
    grad_tokens_part, grad_gain_one = jax.vjp(rms_scale, tokens_wide, gain_one)[1](grad_normed)
    grad_tokens = grad_middle + grad_tokens_part
    gain_one_sum, gain_two_sum = lax.psum((grad_gain_one, grad_gain_two), "tp")
    summed = (
        lax.psum_scatter(gain_one_sum, "dp", scatter_dimension=0, tiled=True),
        lax.psum_scatter(gain_two_sum, "dp", scatter_dimension=0, tiled=True),
        lax.psum_scatter(grad_input, "dp", scatter_dimension=1, tiled=True),
        lax.psum_scatter(grad_output, "dp", scatter_dimension=1, tiled=True),
        lax.psum_scatter(grad_state_w, "dp", scatter_dimension=1, tiled=True),
        lax.psum_scatter(grad_update_w, "dp", scatter_dimension=1, tiled=True),
        lax.psum_scatter(grad_gate_w, "dp", scatter_dimension=1, tiled=True),
        lax.psum_scatter(grad_initial, "dp", scatter_dimension=0, tiled=True),
        lax.psum_scatter(grad_up, "dp", scatter_dimension=0, tiled=True),
        lax.psum_scatter(grad_down, "dp", scatter_dimension=1, tiled=True),
    )
    (
        out_gain_one,
        out_gain_two,
        out_input,
        out_output,
        out_state,
        out_update,
        out_gate,
        out_initial,
        out_up,
        out_down,
    ) = summed
    return (
        mixed.astype(jnp.bfloat16),
        memory_end.reshape(seq_count, S, width_here),
        grad_tokens,
        grad_carried,
        out_gain_one,
        out_input,
        out_state,
        out_update,
        out_gate,
        out_initial,
        out_output,
        out_gain_two,
        out_up,
        out_down,
    )


BF16 = jnp.bfloat16
F32 = jnp.float32
HD = 128
TILE = 256
LOG2E = math.log2(math.e)
SCALING = HD ** (-0.5)
TO_POWER = SCALING * LOG2E
VMEM_BYTES = 60 * 1024 * 1024


def dot_nn(left, right):
    return jnp.dot(left, right, preferred_element_type=F32)


def dot_nt(left, right):
    return lax.dot_general(left, right, (((1,), (1,)), ((), ())), preferred_element_type=F32)


def call_params(**more):
    return pltpu.CompilerParams(vmem_limit_bytes=VMEM_BYTES, **more)


def cost(macs, moved, powers=0):
    return pl.CostEstimate(flops=2 * macs, bytes_accessed=moved, transcendentals=powers)


def whole(shape):
    return pl.BlockSpec(shape, lambda *_: (0,) * len(shape), pipeline_mode=pl.Buffered(1))


def project_kernel(x_ref, gain_ref, w_ref, normed_t_ref, out_ref, w_full):
    depth = w_ref.shape[1] // 3

    @pl.when(pl.program_id(0) == 0)
    def _():
        for i in range(3):
            part = w_ref[:, i * depth : (i + 1) * depth]
            w_full[i] = part.reshape(w_full.shape[1:])

    x = x_ref[...].astype(F32)
    scale = lax.rsqrt(jnp.mean(x * x, axis=-1, keepdims=True) + EPSILON)
    normed = (x * scale * gain_ref[...]).astype(BF16)
    normed_t_ref[...] = normed.T
    for i in range(3):
        out_ref[i] = dot_nn(normed, w_full[i]).astype(BF16)


def project(x, gain, packs, depth):
    rows, width = x.shape
    cols = packs.shape[2]
    return pl.pallas_call(
        project_kernel,
        grid=(rows // TILE,),
        in_specs=[
            pl.BlockSpec((TILE, width), lambda r: (r, 0)),
            whole((1, width)),
            whole((packs.shape[0], 3 * depth, cols)),
        ],
        out_specs=[
            pl.BlockSpec((width, TILE), lambda r: (0, r)),
            pl.BlockSpec((3, TILE, cols), lambda r: (0, r, 0)),
        ],
        out_shape=[
            jax.ShapeDtypeStruct((width, rows), BF16),
            jax.ShapeDtypeStruct((3, rows, cols), BF16),
        ],
        scratch_shapes=[pltpu.VMEM((3, width, cols), BF16)],
        compiler_params=call_params(),
        cost_estimate=cost(rows * width * 3 * cols, 6 * rows * width),
        name="project",
    )(x, gain, packs)


def tile_masks():
    key = lax.broadcasted_iota(jnp.int32, (TILE, TILE), 0)
    query = lax.broadcasted_iota(jnp.int32, (TILE, TILE), 1)
    return key, query


def token_tiles(t):
    return [(j, t - j) for j in range(max(0, t - 2), t + 1)]


def masked_scores(scores, tile, behind, length, key, query):
    if behind == 0:
        scores = jnp.where(key <= query, scores, NEGATIVE)
    elif behind == 2:
        scores = jnp.where(key > query, scores, NEGATIVE)
    if tile >= 2 * (NB - 1):
        scores = jnp.where(key + tile * TILE < length, scores, NEGATIVE)
    return scores


def softmax_columns(tiles):
    peak = functools.reduce(jnp.maximum, [jnp.max(s, axis=0, keepdims=True) for s in tiles])
    peak = peak * TO_POWER
    powers = [jnp.exp2(s * TO_POWER - peak) for s in tiles]
    total = functools.reduce(jnp.add, [jnp.sum(p, axis=0, keepdims=True) for p in powers])
    return [p.astype(BF16) for p in powers], total, peak + jnp.log2(total)


def first_memory(flags_ref, carried_ref, initial_ref):
    initial = initial_ref[...].reshape(carried_ref.shape).astype(F32)
    return jnp.where(flags_ref[0, 0] > 0, initial, carried_ref[...].astype(F32))


def attend_kernel(
    flags_ref,
    q_ref,
    k_ref,
    v_ref,
    carried_ref,
    initial_ref,
    ws_ref,
    wu_ref,
    gate_ref,
    out_ref,
    state_out_ref,
    log_ref,
    state_log_ref,
    final_ref,
    vt_ref,
):
    length = flags_ref[0, 1]
    key, query = tile_masks()
    retain = jax.nn.sigmoid(gate_ref[0])
    memory = first_memory(flags_ref, carried_ref, initial_ref)
    vt_ref[...] = v_ref[0].T
    for c in range(NB):
        lo = c * BLK
        state = dot_nn(memory.astype(BF16), ws_ref[0]).astype(BF16)
        sq, sk, sv = state[:, :HD], state[:, HD : 2 * HD], state[:, 2 * HD :]
        svt = sv.T
        jobs = []
        for t in range(2 * c, 2 * c + 2):
            q = q_ref[0, t * TILE : (t + 1) * TILE]
            spans = token_tiles(t)
            tiles = [
                masked_scores(
                    dot_nt(k_ref[0, j * TILE : (j + 1) * TILE], q), j, behind, length, key, query
                )
                for j, behind in spans
            ]
            jobs.append((tiles + [dot_nt(sk, q)], spans[0][0] * TILE, (t + 1) * TILE))
        for u in range(2):
            q = sq[u * TILE : (u + 1) * TILE]
            tiles = [
                masked_scores(
                    dot_nt(k_ref[0, j * TILE : (j + 1) * TILE], q), j, 1, length, key, query
                )
                for j in (2 * c, 2 * c + 1)
            ]
            jobs.append((tiles + [dot_nt(sk, q)], lo, lo + BLK))
        shares = [softmax_columns(tiles) for tiles, _, _ in jobs]
        for u, ((powers, total, logs), (_, first, stop)) in enumerate(zip(shares, jobs)):
            out = dot_nn(vt_ref[:, first:stop], jnp.concatenate(powers[:-1], axis=0))
            out = out + dot_nn(svt, powers[-1])
            out = (out / total).T.astype(BF16)
            rows = slice(lo + u % 2 * TILE, lo + (u % 2 + 1) * TILE)
            if u < 2:
                out_ref[rows] = out
                log_ref[0, :, rows] = logs
            else:
                state_out_ref[rows] = out
                state_log_ref[0, :, rows] = logs
        update = dot_nn(state_out_ref[lo : lo + BLK], wu_ref[0])
        blended = retain * memory + (1.0 - retain) * update
        memory = jnp.where(lo < length, blended, memory)
    final_ref[...] = memory


def head_block(rows):
    return pl.BlockSpec((rows, HD), lambda h: (0, h))


def initial_block(packs, at, first=0):
    length = S // packs.shape[0]
    return pl.BlockSpec((packs.shape[0], length, HD), lambda h: (0, at // length, first + h))


def attend(flags, projected, carried, packs, initial_at, states, gate):
    rows = projected.shape[1]
    heads = states.shape[0]
    return pl.pallas_call(
        attend_kernel,
        grid=(heads,),
        in_specs=[
            pl.BlockSpec(memory_space=pltpu.SMEM),
            pl.BlockSpec((1, rows, HD), lambda h: (0, 0, h)),
            pl.BlockSpec((1, rows, HD), lambda h: (1, 0, h)),
            pl.BlockSpec((1, rows, HD), lambda h: (2, 0, h)),
            head_block(S),
            initial_block(packs, initial_at),
            pl.BlockSpec((1, HD, 3 * HD), lambda h: (h, 0, 0)),
            pl.BlockSpec((1, HD, HD), lambda h: (h, 0, 3)),
            pl.BlockSpec((1, 1, HD), lambda h: (h, 0, 0)),
        ],
        out_specs=[
            head_block(rows),
            head_block(NB * S),
            pl.BlockSpec((1, 1, rows), lambda h: (h, 0, 0)),
            pl.BlockSpec((1, 1, NB * S), lambda h: (h, 0, 0)),
            head_block(S),
        ],
        out_shape=[
            jax.ShapeDtypeStruct((rows, heads * HD), BF16),
            jax.ShapeDtypeStruct((NB * S, heads * HD), BF16),
            jax.ShapeDtypeStruct((heads, 1, rows), F32),
            jax.ShapeDtypeStruct((heads, 1, NB * S), F32),
            jax.ShapeDtypeStruct((S, heads * HD), F32),
        ],
        scratch_shapes=[pltpu.VMEM((HD, rows), BF16)],
        compiler_params=call_params(),
        cost_estimate=cost(
            heads * NB * BLK * HD * 2 * (1152 + 1024),
            heads * HD * (rows * 10 + S * 8),
            heads * NB * BLK * 2176,
        ),
        name="attend",
    )(flags, projected, projected, projected, carried, packs, states, states, gate)


def attend_back_kernel(
    spots,
    flags_ref,
    q_ref,
    k_ref,
    v_ref,
    carried_ref,
    initial_ref,
    ws_ref,
    wu_ref,
    gate_ref,
    out_ref,
    state_out_ref,
    log_ref,
    state_log_ref,
    go_ref,
    grad_final_ref,
    nt_any,
    w_ref,
    *refs,
):
    load_sems, nt_ref, *late = refs[-13:-9] if len(refs) > 17 else refs[-11:-9]
    kt_ref, dk_ref, dv_ref, dqkv_ref, acc_ref, p_ref, ds_ref, qcat_ref, gocat_ref = refs[-9:]
    last = len(refs) > 17
    if last:
        core_ref, x_any, sum_any = refs[:3]
        sum_ref, x_ref = late
        dws_ref, dwu_ref, dgate_ref, dmemory_ref, dw_ref, own_ref, give_ref, dgain_ref = refs[3:-13]
    else:
        dws_ref, dwu_ref, dgate_ref, dmemory_ref, dw_ref, out_gy_ref = refs[:-11]
    step = pl.program_id(0)
    loads = [pltpu.make_async_copy(nt_any, nt_ref, load_sems.at[0])]
    if last:
        loads += [
            pltpu.make_async_copy(sum_any, sum_ref, load_sems.at[1]),
            pltpu.make_async_copy(x_any, x_ref, load_sems.at[2]),
        ]

    @pl.when(step == 0)
    def _():
        for load in loads:
            load.start()
        acc_ref[...] = jnp.zeros_like(acc_ref)

    length = flags_ref[0, 1]
    key, query = tile_masks()
    retain = jax.nn.sigmoid(gate_ref[0])
    ws = ws_ref[0]
    wu = wu_ref[0]
    kt_ref[...] = k_ref[0].T
    dk_ref[...] = jnp.zeros_like(dk_ref)
    dv_ref[...] = jnp.zeros_like(dv_ref)
    memories = [first_memory(flags_ref, carried_ref, initial_ref)]
    for c in range(NB - 1):
        update = dot_nn(state_out_ref[c * S : (c + 1) * S], wu)
        blended = retain * memories[c] + (1.0 - retain) * update
        memories.append(jnp.where(c * BLK < length, blended, memories[c]))
    grad_memory = grad_final_ref[...].astype(F32)
    dws = jnp.zeros(ws.shape, F32)
    dwu = jnp.zeros(wu.shape, F32)
    dgate = jnp.zeros(retain.shape, F32)
    for c in reversed(range(NB)):
        lo = c * BLK
        active = lo < length
        memory = memories[c]
        memory_low = memory.astype(BF16)
        state = dot_nn(memory_low, ws).astype(BF16)
        sq, sk, sv = state[:, :HD], state[:, HD : 2 * HD], state[:, 2 * HD :]
        skt = sk.T
        state_out = state_out_ref[lo : lo + S]
        update = dot_nn(state_out, wu)
        grad_blend = jnp.where(active, grad_memory, 0.0)
        grad_update = ((1.0 - retain) * grad_blend).astype(BF16)
        dgate = dgate + jnp.sum(grad_blend * (memory - update), axis=0, keepdims=True)
        dwu = dwu + dot_nn(state_out.T, grad_update)
        grad_state_out = dot_nt(grad_update, wu).astype(BF16)
        grad_memory = jnp.where(active, retain * grad_memory, grad_memory)
        deltas = jnp.sum((grad_state_out.astype(F32) * state_out.astype(F32)).T, axis=0, keepdims=True)
        qcat_ref[:BLK] = q_ref[0, lo : lo + BLK]
        qcat_ref[BLK:] = sq
        gocat_ref[:BLK] = go_ref[lo : lo + BLK]
        gocat_ref[BLK:] = grad_state_out
        base = lo - BLK
        state_rows = slice(2 * BLK, 2 * BLK + S)
        jobs = []
        for u in range(4):
            part = slice(u * TILE, (u + 1) * TILE)
            q = qcat_ref[part]
            go = gocat_ref[part]
            if u < 2:
                t = 2 * c + u
                slots = [(j - 2 * (c - 1), j, behind) for j, behind in token_tiles(t)]
            else:
                slots = [(2, 2 * c, 1), (3, 2 * c + 1, 1)]
            tiles = []
            for slot, j, behind in slots:
                rows = slice(j * TILE, (j + 1) * TILE)
                s = masked_scores(dot_nt(k_ref[0, rows], q), j, behind, length, key, query)
                at = slice(slot * TILE, (slot + 1) * TILE)
                tiles.append((at, s, dot_nt(v_ref[0, rows], go)))
            tiles.append((state_rows, dot_nt(sk, q), dot_nt(sv, go)))
            span = slice(slots[0][0] * TILE, (slots[-1][0] + 1) * TILE)
            jobs.append((part, tiles, span))
        for u, (part, tiles, _) in enumerate(jobs):
            if u < 2:
                here = slice(lo + u * TILE, lo + (u + 1) * TILE)
                logs = log_ref[0, :, here]
                pairs = (go_ref[here].astype(F32) * out_ref[here].astype(F32)).T
                delta = jnp.sum(pairs, axis=0, keepdims=True)
            else:
                logs = state_log_ref[0, :, lo + (u - 2) * TILE : lo + (u - 1) * TILE]
                delta = deltas[:, (u - 2) * TILE : (u - 1) * TILE]
            for at, s, gp in tiles:
                p = jnp.exp2(s * TO_POWER - logs)
                p_ref[at, part] = p.astype(BF16)
                ds_ref[at, part] = (p * (gp - delta)).astype(BF16)
        dqs = []
        for u, (part, _, span) in enumerate(jobs):
            keys = slice(base + span.start, base + span.stop)
            dq = dot_nn(kt_ref[:, keys], ds_ref[span, part])
            dq = dq + dot_nn(skt, ds_ref[state_rows, part])
            if u < 2:
                here = slice(lo + u * TILE, lo + (u + 1) * TILE)
                dqkv_ref[here, :HD] = (dq.T * SCALING).astype(BF16)
            else:
                dqs.append(dq.T)
        for slot, (first, stop) in enumerate(((0, 1), (0, 2), (0, 4), (1, 4))):
            if base + slot * TILE < 0:
                continue
            rows = slice(base + slot * TILE, base + (slot + 1) * TILE)
            at = slice(slot * TILE, (slot + 1) * TILE)
            span = slice(first * TILE, stop * TILE)
            dv_ref[rows] += dot_nn(p_ref[at, span], gocat_ref[span])
            dk_ref[rows] += dot_nn(ds_ref[at, span], qcat_ref[span])
        dsv = dot_nn(p_ref[state_rows], gocat_ref[...])
        dsk = dot_nn(ds_ref[state_rows], qcat_ref[...])
        dsq = dqs
        grad_state = jnp.concatenate(
            [jnp.concatenate(dsq, axis=0) * SCALING, dsk * SCALING, dsv], axis=1
        ).astype(BF16)
        grad_memory = grad_memory + dot_nt(grad_state, ws)
        dws = dws + dot_nn(memory_low.T, grad_state)
    dqkv_ref[:, HD : 2 * HD] = (dk_ref[...] * SCALING).astype(BF16)
    dqkv_ref[:, 2 * HD :] = dv_ref[...].astype(BF16)
    dws_ref[0] = dws
    dwu_ref[0] = dwu
    dgate_ref[0] = dgate * retain * (1.0 - retain)
    dmemory_ref[...] = grad_memory
    depth = w_ref.shape[1] // 3

    @pl.when(step == 0)
    def _():
        loads[0].wait()

    wide = dqkv_ref[...]
    weights = jnp.concatenate(
        [w_ref[:, i * depth : (i + 1) * depth].reshape(nt_ref.shape[0], HD) for i in range(3)],
        axis=1,
    )
    acc_ref[...] += dot_nt(wide, weights)
    product = dot_nn(nt_ref[...], wide).astype(BF16)
    low = depth // 2
    for block in range(w_ref.shape[0]):
        chip, t = block // 2, block % 2
        lead = (spots[chip], t)
        for i in range(3):
            at = lead + (slice(i * low, (i + 1) * low),)
            piece = product[block * depth : (block + 1) * depth, i * HD : (i + 1) * HD]
            dw_ref[at + (slice(0, HD),)] = piece[:low]
            dw_ref[at + (slice(HD, 2 * HD),)] = piece[low:]

    @pl.when(step == pl.num_programs(0) - 1)
    def _():
        if not last:
            out_gy_ref[...] = acc_ref[...].astype(BF16)
            return
        for load in loads[1:]:
            load.wait()
        acc_ref[...] += sum_ref[...].astype(F32)
        half = own_ref.shape[0]
        core = core_ref[0]
        own = pl.ds(pl.multiple_of(core * half, half), half)
        give = pl.ds(pl.multiple_of((1 - core) * half, half), half)
        own_ref[...] = acc_ref[own, :].astype(BF16)
        give_ref[...] = acc_ref[give, :].astype(BF16)
        dgain = jnp.zeros_like(dgain_ref)
        for r in range(acc_ref.shape[0] // TILE):
            rows = slice(r * TILE, (r + 1) * TILE)
            x = x_ref[rows].astype(F32)
            scale = lax.rsqrt(jnp.mean(x * x, axis=-1, keepdims=True) + EPSILON)
            dgain = dgain + jnp.sum(acc_ref[rows] * x * scale, axis=0, keepdims=True)
        dgain_ref[...] = dgain


def attend_back(
    first,
    heads,
    spots,
    flags,
    projected,
    carried,
    packs,
    initial_at,
    states,
    gate,
    out,
    state_out,
    logs,
    state_logs,
    go,
    grad_final,
    normed_t,
    depth,
    more=(),
):
    rows = projected.shape[1]
    width = normed_t.shape[0]
    slices = packs.shape[0]
    chips = slices // 2
    per_head = lambda a, b: pl.BlockSpec((1, a, b), lambda h: (first + h, 0, 0))
    new_head = lambda a, b: pl.BlockSpec((1, a, b), lambda h: (h, 0, 0))
    in_head = lambda rows: pl.BlockSpec((rows, HD), lambda h: (0, first + h))
    part = lambda i: pl.BlockSpec((1, rows, HD), lambda h: (i, 0, first + h))
    lanes = 2 * HD
    piece = lambda rows: pl.BlockSpec((chips, 2, rows, lanes), lambda h: (0, 0, 0, h))
    shape = jax.ShapeDtypeStruct
    low = 3 * (depth // 2)
    lead = (chips, 2)
    if more:
        anywhere = pl.BlockSpec(memory_space=pl.ANY)
        extra = [pl.BlockSpec(memory_space=pltpu.SMEM)] + [anywhere] * 2
        late = [pltpu.VMEM((rows, width), BF16)] * 2
        operands = more
        outs = [shape((rows // 2, width), BF16)] * 2 + [shape((1, width), F32)]
    else:
        extra = []
        late = []
        operands = ()
        outs = [shape((rows, width), BF16)]
    return pl.pallas_call(
        functools.partial(attend_back_kernel, spots),
        grid=(heads,),
        in_specs=[
            pl.BlockSpec(memory_space=pltpu.SMEM),
            part(0),
            part(1),
            part(2),
            in_head(S),
            initial_block(packs, initial_at, first),
            per_head(HD, 3 * HD),
            pl.BlockSpec((1, HD, HD), lambda h: (first + h, 0, 3)),
            per_head(1, HD),
            in_head(rows),
            in_head(NB * S),
            per_head(1, rows),
            per_head(1, NB * S),
            in_head(rows),
            in_head(S),
            pl.BlockSpec(memory_space=pl.ANY),
            pl.BlockSpec((slices, 3 * depth, HD), lambda h: (0, 0, first + h)),
        ]
        + extra,
        out_specs=[
            new_head(HD, 3 * HD),
            new_head(HD, HD),
            new_head(1, HD),
            head_block(S),
            pl.BlockSpec(lead + (low, lanes), lambda h: (0, 0, 0, h)),
        ]
        + [whole(v.shape) for v in outs],
        out_shape=[
            shape((heads, HD, 3 * HD), F32),
            shape((heads, HD, HD), F32),
            shape((heads, 1, HD), F32),
            shape((S, heads * HD), F32),
            shape(lead + (low, heads * lanes), BF16),
        ]
        + outs,
        scratch_shapes=[pltpu.SemaphoreType.DMA((3,)), pltpu.VMEM(normed_t.shape, BF16)]
        + late
        + [
            pltpu.VMEM((HD, rows), BF16),
            pltpu.VMEM((rows, HD), F32),
            pltpu.VMEM((rows, HD), F32),
            pltpu.VMEM((rows, 3 * HD), BF16),
            pltpu.VMEM((rows, width), F32),
            pltpu.VMEM((2 * BLK + S, BLK + S), BF16),
            pltpu.VMEM((2 * BLK + S, BLK + S), BF16),
            pltpu.VMEM((BLK + S, HD), BF16),
            pltpu.VMEM((BLK + S, HD), BF16),
        ],
        compiler_params=call_params(),
        cost_estimate=cost(
            heads * NB * BLK * HD * (5 * (1152 + 1024) + 6 * width),
            heads * HD * (rows * 20 + S * 16) + 8 * rows * width,
            heads * NB * BLK * 2176,
        ),
        name="attend_back",
    )(
        flags,
        projected,
        projected,
        projected,
        carried,
        packs,
        states,
        states,
        gate,
        out,
        state_out,
        logs,
        state_logs,
        go,
        grad_final,
        normed_t,
        packs,
        *operands,
    )


def middle_kernel(
    core_ref,
    x_ref,
    own_ref,
    sib_ref,
    wo_own_ref,
    wo_sib_ref,
    gain_ref,
    g_here_ref,
    g_came_ref,
    g_other_ref,
    mid_ref,
    n_ref,
    g_ref,
):
    mine = pl.program_id(0) * 2 // pl.num_programs(0) == core_ref[0]
    own = jnp.where(core_ref[0] == core_ref[1], g_here_ref[...], g_came_ref[...])
    g = jnp.where(mine, own, g_other_ref[...])
    g_ref[...] = g
    wo_own = wo_own_ref[...].reshape(wo_sib_ref.shape)
    middle = x_ref[...].astype(F32) + dot_nt(own_ref[...], wo_own)
    middle = middle + dot_nt(sib_ref[...], wo_sib_ref[...])
    scale = lax.rsqrt(jnp.mean(middle * middle, axis=-1, keepdims=True) + EPSILON)
    normed = (middle * scale * gain_ref[...]).astype(BF16)
    mid_ref[...] = middle.astype(BF16)
    n_ref[...] = normed


def output_block(packs, depth):
    return pl.BlockSpec(
        (packs.shape[0], depth, packs.shape[2]),
        lambda *_: (0, 3, 0),
        pipeline_mode=pl.Buffered(1),
    )


def form_middle(core, x, own, sib, packs, depth, wo_sib, gain, *grads):
    rows, width = x.shape
    half = own.shape[1]
    row_block = lambda cols: pl.BlockSpec((TILE, cols), lambda r: (r, 0))
    half_tiles = rows // TILE // 2
    half_block = pl.BlockSpec((TILE, width), lambda r: (r % half_tiles, 0))
    return pl.pallas_call(
        middle_kernel,
        grid=(rows // TILE,),
        in_specs=[
            pl.BlockSpec(memory_space=pltpu.SMEM),
            row_block(width),
            row_block(half),
            row_block(half),
            output_block(packs, depth),
            whole(wo_sib.shape),
            whole(gain.shape),
            half_block,
            half_block,
            half_block,
        ],
        out_specs=[row_block(width)] * 3,
        out_shape=[jax.ShapeDtypeStruct((rows, width), BF16)] * 3,
        compiler_params=call_params(),
        cost_estimate=cost(2 * rows * width * half, 12 * rows * width),
        name="form_middle",
    )(core, x, own, sib, packs, wo_sib, gain, *grads)


ROOT = math.sqrt(2.0 / math.pi)
CUBIC = 0.044715


def feed_kernel(
    place, spots, core_ref, n_ref, g_ref, up_ref, dn_ref, *refs
):
    last = len(refs) > 8
    if last:
        ff_in, gn_in, ff_out, gn_out, dw_ref = refs[:5]
    else:
        ff_out, gn_out, dw_ref = refs[:3]
    w_full, hid_ref, grad_ref, nt_ref, gt_ref = refs[-5:]
    step = pl.program_id(0)
    depth = dw_ref.shape[2] // 2

    @pl.when(step == 0)
    def _():
        for i, ref in enumerate((up_ref, dn_ref)):
            for block, p in enumerate(spots):
                w_full[i, block * depth : (block + 1) * depth] = ref[p]

    up = w_full[0]
    dn = w_full[1]
    here = pl.ds(pl.multiple_of(step * n_ref.shape[0], TILE), n_ref.shape[0])
    pre = dot_nn(n_ref[...], up)
    square = pre * pre
    bend = jnp.tanh(ROOT * pre * (1.0 + CUBIC * square))
    half = 0.5 * (1.0 + bend)
    hid = (pre * half).astype(BF16)
    slope = half + (0.5 * ROOT) * pre * (1.0 - bend * bend) * (1.0 + 3.0 * CUBIC * square)
    grad = (dot_nn(g_ref[...], dn) * slope).astype(BF16)
    hid_ref[here, :] = hid
    grad_ref[here, :] = grad
    nt_ref[:, here] = n_ref[...].T
    gt_ref[:, here] = g_ref[...].T
    ff = dot_nt(hid, dn)
    gn = dot_nt(grad, up)
    if last:
        ff = ff + ff_in[...].astype(F32)
        gn = gn + gn_in[...].astype(F32)
    ff_out[...] = ff.astype(BF16)
    gn_out[...] = gn.astype(BF16)

    @pl.when(step == pl.num_programs(0) - 1)
    def _():
        for i, (left, right) in enumerate(((nt_ref, grad_ref), (gt_ref, hid_ref))):
            for at in range(0, left.shape[0], TILE):
                product = dot_nn(left[at : at + TILE], right[...]).astype(BF16)
                for t in range(TILE // depth):
                    block = at // depth + t
                    piece = product[t * depth : (t + 1) * depth]
                    rows = slice(i * depth, (i + 1) * depth)
                    dw_ref[place[block // 2], block % 2, rows] = piece


def feed(place, spots, core, normed, grad, weights, units, sums=(), room=0):
    rows, width = normed.shape
    pieces, depth = weights.shape[:2]
    row_block = pl.BlockSpec((TILE, width), lambda r: (r, 0))
    piece_block = lambda at: pl.BlockSpec(
        (pieces, depth, units), lambda r: (0, 0, at), pipeline_mode=pl.Buffered(1)
    )
    grad_block = (pieces // 2, 2, 2 * depth, units)
    grad_shape = jax.ShapeDtypeStruct((pieces // 2, 2, 2 * depth + room, units), BF16)
    full = jax.ShapeDtypeStruct((rows, width), BF16)
    return pl.pallas_call(
        functools.partial(feed_kernel, place, spots),
        grid=(rows // TILE,),
        in_specs=[
            pl.BlockSpec(memory_space=pltpu.SMEM),
            row_block,
            row_block,
            piece_block(0),
            piece_block(1),
        ]
        + [row_block for _ in sums],
        out_specs=[row_block, row_block, whole(grad_block)],
        out_shape=[full, full, grad_shape],
        scratch_shapes=[
            pltpu.VMEM((2, width, units), BF16),
            pltpu.VMEM((rows, units), BF16),
            pltpu.VMEM((rows, units), BF16),
            pltpu.VMEM((width, rows), BF16),
            pltpu.VMEM((width, rows), BF16),
        ],
        compiler_params=call_params(),
        cost_estimate=cost(
            6 * rows * width * units, 14 * rows * width + 8 * width * units, rows * units
        ),
        name="feed",
    )(core, normed, grad, weights, weights, *sums)


def norm_back(values, gain, grad):
    scale = lax.rsqrt(jnp.mean(values * values, axis=-1, keepdims=True) + EPSILON)
    weighted = grad * gain
    mean = jnp.mean(values * weighted, axis=-1, keepdims=True)
    out = scale * weighted - values * (scale * scale * scale * mean)
    return out, jnp.sum(grad * values * scale, axis=0, keepdims=True)


def room_rows(depth, cols, lanes):
    width = math.gcd(cols, lanes)
    return -(-depth * (cols // width) // (lanes // width) // 16) * 16


def room_spans(depth, cols, lanes):
    width = math.gcd(cols, lanes)
    room = room_rows(depth, cols, lanes)
    for half in range(cols // width):
        at = 0
        while at < depth:
            group, row = divmod(half * depth + at, room)
            length = min(depth - at, room - row)
            yield (
                slice(at, at + length),
                slice(half * width, (half + 1) * width),
                slice(row, row + length),
                slice(group * width, (group + 1) * width),
            )
            at += length


def middle_back_kernel(
    place, g_ref, mid_ref, own_ref, sib_ref, gain_ref, wo_ref, att_ref, _, gm_ref, ga_ref, sums_any, dgain_ref, acc, dwo_ref, sem
):
    step = pl.program_id(0)
    gy = own_ref[...].astype(F32) + sib_ref[...].astype(F32)
    back, dgain = norm_back(mid_ref[...].astype(F32), gain_ref[...], gy)
    grad_middle = g_ref[...].astype(F32) + back
    branch = grad_middle.astype(BF16)
    gm_ref[...] = branch
    wo = wo_ref[...].reshape(branch.shape[1], ga_ref.shape[1])
    ga_ref[...] = dot_nn(branch, wo).astype(BF16)

    @pl.when(step == 0)
    def _():
        acc[...] = jnp.zeros_like(acc)
        dgain_ref[...] = jnp.zeros_like(dgain_ref)

    acc[...] += dot_nn(branch.T, att_ref[...])
    dgain_ref[...] += dgain

    @pl.when(step == pl.num_programs(0) - 1)
    def _():
        depth = acc.shape[0] // (2 * dwo_ref.shape[0])
        room, lanes = dwo_ref.shape[2:]
        spans = list(room_spans(depth, acc.shape[1], lanes))
        dwo_ref[...] = jnp.zeros_like(dwo_ref)
        for block in range(2 * len(place)):
            piece = acc[block * depth : (block + 1) * depth, :].astype(BF16)
            at = (place[block // 2], block % 2)
            for rows, cols, to_rows, to_cols in spans:
                dwo_ref[at + (to_rows, to_cols)] = piece[rows, cols]
        first = sums_any.shape[2] - room
        copy = pltpu.make_async_copy(dwo_ref, sums_any.at[:, :, pl.ds(first, room)], sem.at[0])
        copy.start()
        copy.wait()


def middle_back(place, g, middle, own, sib, gain, packs, depth, att, feed_grad, room):
    rows, width = g.shape
    half = att.shape[1]
    row_block = lambda cols: pl.BlockSpec((TILE, cols), lambda r: (r, 0))
    block = feed_grad.shape[:2] + (room, feed_grad.shape[3])
    return pl.pallas_call(
        functools.partial(middle_back_kernel, place),
        grid=(rows // TILE,),
        in_specs=[
            row_block(width),
            row_block(width),
            row_block(width),
            row_block(width),
            whole(gain.shape),
            output_block(packs, depth),
            row_block(half),
            pl.BlockSpec(memory_space=pl.ANY),
        ],
        out_specs=[
            row_block(width),
            row_block(half),
            pl.BlockSpec(memory_space=pl.ANY),
            whole((1, width)),
        ],
        out_shape=[
            jax.ShapeDtypeStruct((rows, width), BF16),
            jax.ShapeDtypeStruct((rows, half), BF16),
            jax.ShapeDtypeStruct(feed_grad.shape, BF16),
            jax.ShapeDtypeStruct((1, width), F32),
        ],
        input_output_aliases={7: 2},
        scratch_shapes=[
            pltpu.VMEM((width, half), F32),
            pltpu.VMEM(block, BF16),
            pltpu.SemaphoreType.DMA((1,)),
        ],
        compiler_params=call_params(),
        cost_estimate=cost(2 * rows * width * half, 16 * rows * width),
        name="middle_back",
    )(g, middle, own, sib, gain, packs, att, feed_grad)


def ring_order(count):
    evens = list(range(0, count, 2))
    odds = list(range(1, count, 2))
    return evens + odds[::-1]


MESH = pl.DeviceIdType.MESH


def entry_kernel(
    order,
    cut,
    tok_ref,
    carried_ref,
    final_ref,
    w_ref,
    states_ref,
    updates_ref,
    gate_ref,
    gain_one_ref,
    gain_two_ref,
    initial_ref,
    wo_ref,
    up_ref,
    down_ref,
    restart_ref,
    length_ref,
    x_ref,
    memory_ref,
    grad_final_ref,
    packs_ref,
    feed_one_ref,
    feed_two_ref,
    flags_ref,
    wo_sib_ref,
    pack_ref,
    own_one_ref,
    own_two_ref,
    low_ref,
    flag_ref,
    *sems,
):
    (
        turn_send,
        turn_recv,
        rows_send,
        rows_recv,
        sib_send,
        sib_recv,
        wo_send,
        wo_recv,
        ring_send,
        ring_recv,
    ) = sems
    chips = len(order)
    dp = lax.axis_index("dp")
    y = lax.axis_index("tp")
    k = dp // 2
    c = dp % 2
    stays = c == y
    moves = jnp.logical_not(stays)
    partner = (2 * k + 1 - c, 1 - y)
    sibling = (2 * k + 1 - c, y)
    opposite = (dp, 1 - y)
    place = [order.index(i) for i in range(chips)]

    def chip_after(steps):
        found = jnp.int32(0)
        for i in range(chips):
            onward = order[(place[i] + steps) % chips]
            back = order[(place[i] - steps) % chips]
            found = jnp.where(k == i, jnp.where(c == 0, onward, back), found)
        return found

    following = (2 * chip_after(1) + c, y)
    previous = (2 * chip_after(-1) + c, y)
    barrier = pltpu.get_barrier_semaphore()
    for device in (sibling, opposite, following, previous):
        pl.semaphore_signal(barrier, inc=1, device_id=device, device_id_type=MESH)

    @pl.when(moves)
    def _():
        pl.semaphore_signal(barrier, inc=1, device_id=partner, device_id_type=MESH)

    parts, depth, cols = w_ref.shape
    heads, state_len, state_cols = states_ref.shape
    for i in range(parts):
        pack_ref[i * depth : (i + 1) * depth] = w_ref[i]
    at = parts * depth
    wo_rows = slice(at, at + depth)
    pack_ref[wo_rows] = wo_ref[...]
    at += depth
    for h in range(heads):
        rows = slice(at + h * state_len, at + (h + 1) * state_len)
        pack_ref[rows, :state_cols] = states_ref[h]
        pack_ref[rows, state_cols:] = updates_ref[h]
    at += heads * state_len
    pack_ref[at : at + initial_ref.shape[0]] = initial_ref[...]
    at += initial_ref.shape[0]
    pack_ref[at:] = jnp.zeros((pack_ref.shape[0] - at, cols), BF16)
    pack_ref[at : at + heads, :state_len] = gate_ref[...]
    pack_ref[at + heads : at + heads + 1, :depth] = gain_one_ref[...]
    pack_ref[at + heads + 1 : at + heads + 2, :depth] = gain_two_ref[...]
    lane = lax.broadcasted_iota(jnp.int32, flag_ref.shape, 1)
    flag_ref[...] = jnp.where(lane == 0, restart_ref[0], length_ref[0])

    def remote(src, dst, send_sem, recv_sem, device):
        return pltpu.make_async_remote_copy(
            src_ref=src,
            dst_ref=dst,
            send_sem=send_sem,
            recv_sem=recv_sem,
            device_id=device,
            device_id_type=MESH,
        )

    own_block = 2 * k + y
    other_block = 2 * k + 1 - y
    cut_row = pack_ref.shape[0] // 32 * 16
    spans = (pl.ds(0, cut_row), pl.ds(cut_row, pack_ref.shape[0] - cut_row))
    turns = [
        (pack_ref.at[spans[0]], packs_ref.at[2 * k + c, spans[0]]),
        (pack_ref.at[spans[1]], packs_ref.at[2 * k + c, spans[1]]),
        (flag_ref, flags_ref),
        (own_one_ref, feed_one_ref.at[c]),
        (own_two_ref, feed_two_ref.at[c]),
        (low_ref, memory_ref),
        (final_ref, grad_final_ref),
    ]

    def turn(i):
        src, dst = turns[i]
        return remote(src, dst, turn_send.at[i], turn_recv.at[i], partner)

    pieces = rows_send.shape[0]
    size = tok_ref.shape[0] // pieces

    def swap(i, half):
        rows = pl.ds(i * size, size)
        return remote(
            tok_ref.at[rows], x_ref.at[half, rows], rows_send.at[i], rows_recv.at[i], partner
        )

    def share(i, source, half):
        rows = pl.ds(i * size, size)
        return remote(
            source.at[rows], x_ref.at[half, rows], sib_send.at[i], sib_recv.at[i], sibling
        )

    second = (jnp.where(stays, dp, 2 * k + 1 - c), jnp.where(stays, 1 - y, y))
    seconds = [
        (pack_ref.at[span], lambda at, span=span: packs_ref.at[at, span], 2 * k + c, other_block)
        for span in spans
    ]
    seconds += [
        (own_one_ref, lambda at: feed_one_ref.at[at], c, 1 - y),
        (own_two_ref, lambda at: feed_two_ref.at[at], c, 1 - y),
    ]

    def aside(n, arriving=False):
        src, dst, there, here = seconds[n]
        at = here if arriving else there
        last = len(turns) + n
        return remote(src, dst(at), turn_send.at[last], turn_recv.at[last], second)

    wo_span = pl.ds(parts * depth, depth)

    def share_wo(block):
        return remote(
            packs_ref.at[block, wo_span],
            wo_sib_ref.at[block],
            wo_send.at[block],
            wo_recv.at[block],
            sibling,
        )

    def ring(src, block, step, j, part):
        span = spans[part]
        return remote(
            src.at[span],
            packs_ref.at[block, span],
            ring_send.at[step, j, part],
            ring_recv.at[step, j, part],
            following,
        )

    @pl.when(stays)
    def _():
        pl.semaphore_wait(barrier, 4)
        for part in range(2):
            aside(part).start()
            ring(pack_ref, own_block, 0, 0, part).start()
        for i in range(pieces):
            share(i, tok_ref, c).start()

    @pl.when(moves)
    def _():
        pl.semaphore_wait(barrier, 5)
        for i in range(3):
            turn(i).start()
        for part in range(2):
            aside(part).start()

    units = up_ref.shape[1]
    own_one_ref[:, :cut] = up_ref[:, :cut]
    own_one_ref[:, cut:] = down_ref[:, :cut]
    own_two_ref[:, : units - cut] = up_ref[:, cut:]
    own_two_ref[:, units - cut :] = down_ref[:, cut:]
    low_ref[...] = carried_ref[...].astype(BF16)

    @pl.when(moves)
    def _():
        for part in range(2):
            span = spans[part]
            remote(
                pack_ref.at[span],
                packs_ref.at[own_block, span],
                turn_send.at[part],
                turn_recv.at[part],
                partner,
            ).wait_recv()
            ring(packs_ref.at[own_block], own_block, 0, 0, part).start()
        for i in range(pieces):
            swap(i, 1 - c).start()
        for i in range(3, len(turns)):
            turn(i).start()

    for n in (2, 3):
        aside(n).start()

    @pl.when(stays)
    def _():
        packs_ref[own_block] = pack_ref[...]
        flags_ref[...] = flag_ref[...]
        feed_one_ref[y] = own_one_ref[...]
        feed_two_ref[y] = own_two_ref[...]
        x_ref[c] = tok_ref[...]
        memory_ref[...] = low_ref[...]
        grad_final_ref[...] = final_ref[...]

    def forward(i):
        @pl.when(moves)
        def _():
            swap(i, c).wait_recv()
            share(i, x_ref.at[c], c).start()

    share_wo(own_block).start()
    for part in range(2):
        aside(part, True).wait_recv()
        ring(packs_ref.at[other_block], other_block, 0, 1, part).start()
    share_wo(other_block).start()
    for step in range(1, chips):
        chip = chip_after(-step)
        for j in range(2):
            block = 2 * chip + jnp.where(j == 0, y, 1 - y)
            for part in range(2):
                ring(packs_ref.at[block], block, step - 1, j, part).wait_recv()
                if step < chips - 1:
                    ring(packs_ref.at[block], block, step, j, part).start()
            share_wo(block).start()
        if step >= chips - 3:
            forward(step - chips + 3)
    for i in range(3, pieces):
        forward(i)

    @pl.when(moves)
    def _():
        for i in range(2, len(turns)):
            turn(i).wait_recv()

    for i in range(pieces):
        share(i, tok_ref, 1 - c).wait_recv()
        share(i, tok_ref, c).wait_send()
    for block in range(2 * chips):
        share_wo(block).wait_recv()
        share_wo(block).wait_send()
    for n in (2, 3):
        aside(n, True).wait_recv()
    for n in range(len(seconds)):
        aside(n).wait_send()
    for step in range(chips - 1):
        for j in range(2):
            for part in range(2):
                ring(pack_ref, own_block, step, j, part).wait_send()

    @pl.when(moves)
    def _():
        for i in range(len(turns)):
            turn(i).wait_send()
        for i in range(pieces):
            swap(i, 1 - c).wait_send()


def enter(
    order,
    cut,
    tokens,
    carried,
    grad_final,
    w_in,
    states,
    updates,
    gate,
    gain_one,
    gain_two,
    initial,
    wo,
    up,
    down,
    restart,
    lengths,
):
    chips = len(order)
    pieces = 4
    depth, cols = w_in.shape[1:]
    units = up.shape[1]
    heads, state_len = gate.shape
    pack = (4 * depth + heads * state_len + initial.shape[0] + 16, cols)
    feed_one = (depth, 2 * cut)
    feed_two = (depth, 2 * (units - cut))
    dma = pltpu.SemaphoreType.DMA
    in_vmem = pl.BlockSpec(memory_space=pltpu.VMEM)
    in_smem = pl.BlockSpec(memory_space=pltpu.SMEM)
    shape = jax.ShapeDtypeStruct
    return pl.pallas_call(
        functools.partial(entry_kernel, tuple(order), cut),
        in_specs=[in_vmem] * 13 + [in_smem] * 2,
        out_specs=[in_vmem] * 8,
        out_shape=[
            shape((2,) + tokens.shape, BF16),
            shape(carried.shape, BF16),
            shape(grad_final.shape, BF16),
            shape((2 * chips,) + pack, BF16),
            shape((2,) + feed_one, BF16),
            shape((2,) + feed_two, BF16),
            shape((1, 128), jnp.int32),
            shape((2 * chips, depth, cols), BF16),
        ],
        scratch_shapes=[
            pltpu.VMEM(pack, BF16),
            pltpu.VMEM(feed_one, BF16),
            pltpu.VMEM(feed_two, BF16),
            pltpu.VMEM(carried.shape, BF16),
            pltpu.VMEM((1, 128), jnp.int32),
            dma((11,)),
            dma((11,)),
            dma((pieces,)),
            dma((pieces,)),
            dma((pieces,)),
            dma((pieces,)),
            dma((2 * chips,)),
            dma((2 * chips,)),
            dma((chips - 1, 2, 2)),
            dma((chips - 1, 2, 2)),
        ],
        compiler_params=call_params(collective_id=0, has_side_effects=True),
        cost_estimate=cost(0, 16 * tokens.size),
        name="enter",
    )(
        tokens,
        carried,
        grad_final,
        w_in,
        states,
        updates,
        gate,
        gain_one.reshape(1, -1),
        gain_two.reshape(1, -1),
        initial,
        wo,
        up,
        down,
        restart,
        lengths,
    )


def exit_kernel(
    order,
    dw_ref,
    dwo_ref,
    ready_refs,
    dws_refs,
    dwu_refs,
    dgate_refs,
    dmemory_refs,
    dgain_one_ref,
    dgain_two_ref,
    flags_ref,
    gy_own_any,
    gy_give_ref,
    gain_ref,
    x_any,
    gm_any,
    gt_ref,
    gc_ref,
    turned_ref,
    ready_turned_refs,
    piece_ref,
    initial_ref,
    gain_ref_all,
    first_ref,
    ring_ref,
    gy_sib_ref,
    result_ref,
    carried_ref,
    x_ref,
    gm_ref,
    gain_sib_ref,
    gy_own_ref,
    over_refs,
    beside_refs,
    ready_sems,
    load_sems,
    gain_sems,
    sib_send,
    sib_recv,
    rows_send,
    rows_recv,
    ring_send,
    ring_recv,
    carried_sems,
):
    chips = len(order)
    dp = lax.axis_index("dp")
    y = lax.axis_index("tp")
    k = dp // 2
    c = dp % 2
    stays = c == y
    moves = jnp.logical_not(stays)
    partner = (2 * k + 1 - c, 1 - y)
    sibling = (2 * k + 1 - c, y)
    opposite = (dp, 1 - y)
    place = [order.index(i) for i in range(chips)]

    def chip_after(steps):
        found = jnp.int32(0)
        for i in range(chips):
            onward = order[(place[i] + steps) % chips]
            back = order[(place[i] - steps) % chips]
            found = jnp.where(k == i, jnp.where(c == 0, onward, back), found)
        return found

    following = (2 * chip_after(1) + c, y)
    previous = (2 * chip_after(-1) + c, y)
    barrier = pltpu.get_barrier_semaphore()
    for device in (sibling, opposite, following, previous):
        pl.semaphore_signal(barrier, inc=1, device_id=device, device_id_type=MESH)

    @pl.when(moves)
    def _():
        pl.semaphore_signal(barrier, inc=1, device_id=partner, device_id_type=MESH)

    loads = [
        pltpu.make_async_copy(x_any.at[c], x_ref, load_sems.at[0]),
        pltpu.make_async_copy(gm_any.at[c], gm_ref, load_sems.at[1]),
        pltpu.make_async_copy(gy_own_any, gy_own_ref, load_sems.at[2]),
    ]
    for load in loads:
        load.start()

    def remote(src, dst, send_sem, recv_sem, device):
        return pltpu.make_async_remote_copy(
            src_ref=src,
            dst_ref=dst,
            send_sem=send_sem,
            recv_sem=recv_sem,
            device_id=device,
            device_id_type=MESH,
        )

    pieces = sib_send.shape[0]
    size = gy_own_ref.shape[0] // pieces
    in_rows, lanes_in = dw_ref.shape[2:]
    gain_swap = remote(dgain_one_ref, gain_sib_ref, gain_sems.at[0], gain_sems.at[1], sibling)
    carried_turn = remote(carried_ref, gc_ref, carried_sems.at[0], carried_sems.at[1], partner)

    def give(i):
        rows = pl.ds(i * size, size)
        return remote(
            gy_give_ref.at[rows], gy_sib_ref.at[rows], sib_send.at[i], sib_recv.at[i], sibling
        )

    def swap(i):
        rows = pl.ds(i * size, size)
        return remote(
            result_ref.at[rows], gt_ref.at[rows], rows_send.at[i], rows_recv.at[i], partner
        )

    big_rows = in_rows + dwo_ref.shape[2]
    bounds = ((0, big_rows), (big_rows, first_ref.shape[1] - big_rows))

    def ring(src, step, j, part):
        rows = pl.ds(*bounds[part])
        return remote(
            src.at[rows],
            ring_ref.at[step, j, rows],
            ring_send.at[step, j, part],
            ring_recv.at[step, j, part],
            following,
        )

    many = len(ready_refs)

    def other_and_mine(n):
        if n < many:
            return ready_refs[n].at[1 - c], ready_refs[n].at[c]
        return ring_ref.at[chips - 2, 0], ring_ref.at[chips - 2, 1]

    def sends(n):
        sems = ready_sems.at[n]
        other, mine = other_and_mine(n)
        return (
            lambda: remote(other, beside_refs[n], sems.at[0], sems.at[3], sibling),
            lambda: remote(mine, over_refs[n], sems.at[0], sems.at[2], opposite),
            lambda: remote(other, over_refs[n], sems.at[1], sems.at[2], partner),
        )

    def deliver(n):
        beside, over, skew = sends(n)

        @pl.when(stays)
        def _():
            beside().start()

        @pl.when(moves)
        def _():
            over().start()
            skew().start()

    def collect(n, out_ref):
        beside, over, skew = sends(n)
        over().wait_recv()

        @pl.when(stays)
        def _():
            mine = other_and_mine(n)[1]
            out_ref[...] = (mine[...].astype(F32) + over_refs[n][...].astype(F32)).astype(BF16)

        @pl.when(moves)
        def _():
            beside().wait_recv()
            out_ref[...] = (
                beside_refs[n][...].astype(F32) + over_refs[n][...].astype(F32)
            ).astype(BF16)

    def delivered(n):
        beside, over, skew = sends(n)

        @pl.when(stays)
        def _():
            beside().wait_send()

        @pl.when(moves)
        def _():
            over().wait_send()
            skew().wait_send()

    @pl.when(stays)
    def _():
        pl.semaphore_wait(barrier, 4)

    @pl.when(moves)
    def _():
        pl.semaphore_wait(barrier, 5)

    slice_of = [1 - c, c]
    start = chip_after(-1)
    gain_swap.start()
    for j in range(2):
        first_ref[j, :in_rows] = dw_ref[start, slice_of[j]]
        first_ref[j, in_rows:big_rows] = dwo_ref[start, slice_of[j]]
        ring(first_ref.at[j], 0, j, 0).start()
    for i in range(pieces):
        give(i).start()
    for n in range(many):
        deliver(n)

    restarted = flags_ref[0, 0] > 0
    dmemory = jnp.concatenate([ref[...] for ref in dmemory_refs], axis=1)
    initial_ref[...] = jnp.where(restarted, dmemory, 0.0)
    kept = jnp.where(restarted, 0.0, dmemory).astype(BF16)

    part_heads, head_dim, state_cols = dws_refs[0].shape
    heads = part_heads * len(dws_refs)
    state_len = head_dim // (2 * chips)
    init_len = initial_ref.shape[0] // (2 * chips)
    cols = initial_ref.shape[1]
    states = heads * state_len
    tail = states + init_len
    piece_ref[tail:] = jnp.zeros_like(piece_ref[tail:])
    for h in range(heads):
        n, i = h // part_heads, h % part_heads
        piece_ref[tail + h : tail + h + 1, :head_dim] = dgate_refs[n][i]
    for i in range(dgain_two_ref.shape[1] // cols):
        lanes = slice(i * cols, (i + 1) * cols)
        piece_ref[tail + 6 + i : tail + 7 + i] = dgain_two_ref[:, lanes]
    gain_swap.wait_recv()
    gain_ref_all[...] = dgain_one_ref[...] + gain_sib_ref[...]
    for i in range(dgain_two_ref.shape[1] // cols):
        lanes = slice(i * cols, (i + 1) * cols)
        piece_ref[tail + 4 + i : tail + 5 + i] = gain_ref_all[:, lanes]

    def small_piece(chip, j):
        block = 2 * chip + slice_of[j]
        lines = pl.ds(pl.multiple_of(block * state_len, state_len), state_len)
        for h in range(heads):
            rows = slice(h * state_len, (h + 1) * state_len)
            n, i = h // part_heads, h % part_heads
            piece_ref[rows, :state_cols] = dws_refs[n][i, lines, :]
            piece_ref[rows, state_cols:] = dwu_refs[n][i, lines, :]
        lines = pl.ds(pl.multiple_of(block * init_len, init_len), init_len)
        piece_ref[states:tail] = initial_ref[lines, :]
        return piece_ref[...]

    for j in range(2):
        first_ref[j, big_rows:] = small_piece(start, j).astype(BF16)
        ring(first_ref.at[j], 0, j, 1).start()

    @pl.when(stays)
    def _():
        gc_ref[...] = kept

    @pl.when(moves)
    def _():
        carried_ref[...] = kept
        carried_turn.start()

    for load in loads:
        load.wait()
    gain_one = gain_ref[...]

    def token_rows(i):
        rows = slice(i * size, (i + 1) * size)
        give(i).wait_recv()
        gy = gy_own_ref[rows].astype(F32) + gy_sib_ref[rows].astype(F32)
        back, _ = norm_back(x_ref[rows].astype(F32), gain_one, gy)
        grad = (gm_ref[rows].astype(F32) + back).astype(BF16)

        @pl.when(stays)
        def _():
            gt_ref[rows] = grad

        @pl.when(moves)
        def _():
            result_ref[rows] = grad
            swap(i).start()

    token_rows(0)
    tasks = [functools.partial(token_rows, i) for i in range(1, pieces)]
    for step in range(chips - 1):
        chip = chip_after(-step - 2)
        for j in range(2):
            for part in range(2):
                ring(first_ref.at[j], step, j, part).wait_recv()
                if part == 0:
                    terms = [(0, dw_ref[chip, slice_of[j]]), (in_rows, dwo_ref[chip, slice_of[j]])]
                else:
                    terms = [(big_rows, small_piece(chip, j))]
                for at, term in terms:
                    rows = slice(at, at + term.shape[0])
                    ring_ref[step, j, rows] = (
                        ring_ref[step, j, rows].astype(F32) + term.astype(F32)
                    ).astype(BF16)
                if step < chips - 2:
                    ring(ring_ref.at[step, j], step + 1, j, part).start()
        if tasks and step < chips - 2:
            tasks.pop(0)()
    deliver(many)
    for task in tasks:
        task()
    for n in range(many):
        collect(n, ready_turned_refs[n])
    collect(many, turned_ref)

    @pl.when(moves)
    def _():
        for i in range(pieces):
            swap(i).wait_recv()
        carried_turn.wait_recv()

    gain_swap.wait_send()
    for i in range(pieces):
        give(i).wait_send()
    for n in range(many + 1):
        delivered(n)
    for step in range(chips - 1):
        for j in range(2):
            for part in range(2):
                ring(first_ref.at[j], step, j, part).wait_send()

    @pl.when(moves)
    def _():
        carried_turn.wait_send()
        for i in range(pieces):
            swap(i).wait_send()


def leave(
    order,
    dw,
    dwo,
    ready,
    dws,
    dwu,
    dgate,
    dmemory,
    dgain_one,
    dgain_two,
    flags,
    gy_own,
    gy_give,
    gain,
    x,
    gm,
):
    chips = len(order)
    pieces = 4
    many = len(ready)
    parts = len(dws)
    half, width = gy_own.shape
    in_rows, cols = dw.shape[2:]
    heads, head_dim, state_cols = dws[0].shape
    heads = heads * parts
    small = heads * head_dim // (2 * chips) + S // (2 * chips) + 16
    message = (in_rows + dwo.shape[2] + small, cols)
    dma = pltpu.SemaphoreType.DMA
    in_vmem = pl.BlockSpec(memory_space=pltpu.VMEM)
    anywhere = pl.BlockSpec(memory_space=pl.ANY)
    shape = jax.ShapeDtypeStruct
    sum_scratch = tuple(pltpu.VMEM(v.shape[1:], BF16) for v in ready) + (pltpu.VMEM(message, BF16),)
    inputs = (dw, dwo, *ready, *dws, *dwu, *dgate, *dmemory)

    def kernel(*refs):
        at = 2 + many
        groups = [refs[1], refs[2:at]]
        groups += [refs[at + parts * i : at + parts * (i + 1)] for i in range(4)]
        at = len(inputs) + 11
        rest = refs[len(inputs) : at]
        turned = refs[at : at + many]
        exit_kernel(tuple(order), refs[0], *groups, *rest, turned, *refs[at + many :])

    outs = pl.pallas_call(
        kernel,
        in_specs=[in_vmem] * (len(inputs) + 2)
        + [pl.BlockSpec(memory_space=pltpu.SMEM)]
        + [anywhere] * 2
        + [in_vmem]
        + [anywhere] * 2,
        out_specs=[in_vmem] * (3 + many),
        out_shape=[shape((half, width), BF16), shape((S, cols), BF16), shape(message, BF16)]
        + [shape(v.shape[1:], BF16) for v in ready],
        scratch_shapes=[
            pltpu.VMEM((small, cols), F32),
            pltpu.VMEM((S, cols), F32),
            pltpu.VMEM((1, width), F32),
            pltpu.VMEM((2,) + message, BF16),
            pltpu.VMEM((chips - 1, 2) + message, BF16),
            pltpu.VMEM((half, width), BF16),
            pltpu.VMEM((half, width), BF16),
            pltpu.VMEM((S, cols), BF16),
            pltpu.VMEM((half, width), BF16),
            pltpu.VMEM((half, width), BF16),
            pltpu.VMEM((1, width), F32),
            pltpu.VMEM((half, width), BF16),
            sum_scratch,
            sum_scratch,
            dma((many + 1, 4)),
            dma((3,)),
            dma((2,)),
            dma((pieces,)),
            dma((pieces,)),
            dma((pieces,)),
            dma((pieces,)),
            dma((chips - 1, 2, 2)),
            dma((chips - 1, 2, 2)),
            dma((2,)),
        ],
        compiler_params=call_params(collective_id=1, has_side_effects=True),
        cost_estimate=cost(0, 30 * half * width),
        name="leave",
    )(*inputs, dgain_one, dgain_two, flags, gy_own, gy_give, gain, x, gm)
    return outs[0], outs[1], outs[2], outs[3:]


def unpack_kernel(
    core_ref,
    gt_ref,
    gc_ref,
    last_ref,
    one_ref,
    two_ref,
    out_gt_ref,
    out_gc_ref,
    out_in_ref,
    out_wo_ref,
    out_ws_ref,
    out_wu_ref,
    out_gate_ref,
    out_initial_ref,
    out_one_ref,
    out_two_ref,
    out_up_ref,
    out_down_ref,
):
    out_gt_ref[...] = gt_ref[...].astype(F32)
    out_gc_ref[...] = gc_ref[...].astype(F32)

    @pl.when(pl.program_id(0) == 0)
    def _():
        unpack_shards(
            core_ref[2],
            last_ref,
            one_ref,
            two_ref,
            out_in_ref,
            out_wo_ref,
            out_ws_ref,
            out_wu_ref,
            out_gate_ref,
            out_initial_ref,
            out_one_ref,
            out_two_ref,
            out_up_ref,
            out_down_ref,
        )


def unpack_shards(
    block,
    last_ref,
    one_ref,
    two_ref,
    out_in_ref,
    out_wo_ref,
    out_ws_ref,
    out_wu_ref,
    out_gate_ref,
    out_initial_ref,
    out_one_ref,
    out_two_ref,
    out_up_ref,
    out_down_ref,
):
    cut = one_ref.shape[1]
    parts, depth, cols = out_in_ref.shape
    for i, out in enumerate((out_up_ref, out_down_ref)):
        rows = slice(i * depth, (i + 1) * depth)
        out[:, :cut] = one_ref[rows].astype(F32)
        out[:, cut:] = two_ref[rows].astype(F32)
    for rows, lanes, at_rows, at_lanes in room_spans(depth, cols, two_ref.shape[1]):
        at_rows = slice(2 * depth + at_rows.start, 2 * depth + at_rows.stop)
        out_wo_ref[rows, lanes] = two_ref[at_rows, at_lanes].astype(F32)
    low = depth // 2
    pair = cols // HD // 2
    for n, first in enumerate((parts * low, 0)):
        for i in range(parts):
            for h in range(pair):
                for t in range(2):
                    at = (2 * h + t) * HD
                    lanes = slice((n * pair + h) * HD, (n * pair + h + 1) * HD)
                    piece = last_ref[first + i * low : first + (i + 1) * low, at : at + HD]
                    out_in_ref[i, t * low : (t + 1) * low, lanes] = piece.astype(F32)
    rest = last_ref[2 * parts * low :].astype(F32)
    heads, state_len, state_cols = out_ws_ref.shape
    for h in range(heads):
        rows = slice(h * state_len, (h + 1) * state_len)
        out_ws_ref[h] = rest[rows, :state_cols]
        out_wu_ref[h] = rest[rows, state_cols:]
    at = heads * state_len
    out_initial_ref[...] = rest[at : at + out_initial_ref.shape[0]]
    at += out_initial_ref.shape[0]
    gates = rest[at : at + heads, :HD]
    gains = [jnp.concatenate([rest[r : r + 1], rest[r + 1 : r + 2]], axis=1) for r in (at + 4, at + 6)]
    out_gate_ref[...] = jnp.zeros_like(out_gate_ref)
    for i in range(HD // state_len):

        @pl.when(block == i)
        def _():
            out_gate_ref[...] = gates[:, i * state_len : (i + 1) * state_len]
            for out, gain in zip((out_one_ref, out_two_ref), gains):
                out[...] = gain[:, i * depth : (i + 1) * depth]


def unpack(core, arrays, shapes):
    gt, gc = arrays[:2]
    shape = lambda dims: jax.ShapeDtypeStruct(dims, F32)
    steps = 4
    rows_of = lambda v: pl.BlockSpec((v.shape[0] // steps, v.shape[1]), lambda r: (r, 0))
    return pl.pallas_call(
        unpack_kernel,
        grid=(steps,),
        in_specs=[pl.BlockSpec(memory_space=pltpu.SMEM)]
        + [rows_of(v) for v in (gt, gc)]
        + [whole(v.shape) for v in arrays[2:]],
        out_specs=[rows_of(v) for v in (gt, gc)]
        + [whole(dims) for dims in shapes],
        out_shape=[shape(v.shape) for v in (gt, gc)]
        + [shape(dims) for dims in shapes],
        compiler_params=call_params(),
        cost_estimate=cost(0, 6 * gt.size),
        name="unpack",
    )(core, *arrays)


def tie(*values):
    return lax.optimization_barrier(values)


class Paths:
    def __init__(self, chips):
        self.order = ring_order(chips)
        self.place = tuple(self.order.index(k) for k in range(chips))
        index = lambda k, c, y: (2 * k + c) * 2 + y
        every = [(k, c, y) for k in range(chips) for c in range(2) for y in range(2)]
        self.turned = [(index(k, c, y), index(k, y, c)) for k, c, y in every if c != y]
        self.other = [
            (index(k, c, y), index(k, 1 - c, y) if c == y else index(k, c, 1 - y))
            for k, c, y in every
        ]
        self.across = [(index(k, c, y), index(k, c, 1 - y)) for k, c, y in every]
        self.sibling = [(index(k, c, y), index(k, 1 - c, y)) for k, c, y in every]
        self.rings = [[2 * k + c for k in self.order] for c in range(2)]
        self.spots = tuple(2 * self.place[b // 2] + b % 2 for b in range(2 * chips))
        self.chips = chips

    def send(self, values, pairs):
        return lax.ppermute(values, ("dp", "tp"), pairs)

    def turn(self, values):
        stays = lax.axis_index("dp") % 2 == lax.axis_index("tp")
        return jnp.where(stays, values, self.send(values, self.turned))

    def gather(self, values):
        return lax.all_gather(values, "dp", axis=0, tiled=False, axis_index_groups=self.rings)

    def reduce(self, values):
        return lax.psum_scatter(
            values, "dp", scatter_dimension=0, tiled=False, axis_index_groups=self.rings
        )


def body(
    chips,
    tokens,
    carried,
    restart,
    lengths,
    gain_attend,
    input_weights,
    state_weights,
    update_weights,
    gate_bias,
    initial_state,
    output_weights,
    gain_feed,
    feed_up,
    feed_down,
    grad_mixed,
    grad_final,
):
    paths = Paths(chips)
    send, place = paths.send, paths.place
    y = lax.axis_index("tp")
    c = lax.axis_index("dp") % 2
    core = jnp.stack([c, y, lax.axis_index("dp")])
    heads, state_len = gate_bias.shape
    depth = input_weights.shape[1]
    cols = heads * HD
    slices = 2 * chips
    gate_len = heads * state_len
    half_rows = tokens.shape[0]

    units = feed_up.shape[1]
    cut = units // 8 * 5
    room = room_rows(depth, cols, units - cut)
    entered = enter(
        paths.order,
        cut,
        tokens,
        carried[0],
        grad_final[0],
        input_weights,
        state_weights,
        update_weights,
        gate_bias,
        gain_attend,
        gain_feed,
        initial_state,
        output_weights.T,
        feed_up,
        feed_down.T,
        restart,
        lengths,
    )
    entered, grad_mixed = tie(entered, grad_mixed)
    x, carried_own, grad_final_own, packs, first_feed, second_feed, flags, wo_sib = entered
    wo_sib = wo_sib.reshape(-1, cols)
    x = x.reshape(2 * half_rows, -1)
    first_feed = paths.gather(first_feed).reshape(slices, depth, -1)
    second_feed = paths.gather(second_feed).reshape(slices, depth, -1)
    states_at = 4 * depth
    initial_at = states_at + gate_len
    tail_at = initial_at + initial_state.shape[0]
    small = packs[:, tail_at : tail_at + heads + 2, :depth].astype(F32)
    gain_one = small[:, heads].reshape(1, -1)
    gain_two = small[:, heads + 1].reshape(1, -1)
    gate = jnp.moveaxis(small[:, :heads, :state_len], 1, 0).reshape(heads, 1, HD)
    states = packs[:, states_at:initial_at].reshape(slices, heads, state_len, 4 * HD)
    states = jnp.moveaxis(states, 1, 0).reshape(heads, HD, 4 * HD)
    g_came = send(grad_mixed, paths.turned)
    g_other = send(grad_mixed, paths.other)
    normed_t, projected = project(x, gain_one, packs, depth)
    attended, state_out, logs, state_logs, memory_end = attend(
        flags, projected, carried_own, packs, initial_at, states, gate
    )
    attended, g_came, g_other = tie(attended, g_came, g_other)
    attended_sib = send(attended, paths.sibling)
    middle, normed, g = form_middle(
        core, x, attended, attended_sib, packs, depth, wo_sib, gain_two, grad_mixed, g_came, g_other
    )
    ff, gn, feed_grad = feed(
        place, paths.spots, core, normed, g, first_feed, cut
    )
    feed_one = paths.reduce(feed_grad)
    ff, gn, feed_grad = feed(
        place,
        paths.spots,
        core,
        normed,
        g,
        second_feed,
        units - cut,
        (ff, gn),
        room,
    )
    half_of = lambda values, at: lax.dynamic_slice_in_dim(values, at * half_rows, half_rows)
    gn_sib = send(gn, paths.sibling)
    grad_middle, grad_attended, feed_grad, dgain_two = middle_back(
        place, g, middle, gn, gn_sib, gain_two, packs, depth, attended, feed_grad, room
    )
    feed_two = paths.reduce(feed_grad)
    grad_attended, ff = tie(grad_attended, ff)
    ff_sib = send(half_of(ff, 1 - c), paths.sibling)

    pair = heads // 2

    def back(n, spots, grad, **more):
        return attend_back(
            n * pair,
            pair,
            spots,
            flags,
            projected,
            carried_own,
            packs,
            initial_at,
            states,
            gate,
            attended,
            state_out,
            logs,
            state_logs,
            grad,
            grad_final_own,
            normed_t,
            depth,
            **more,
        )

    natural = tuple(range(chips))
    left = back(0, natural, grad_attended)
    left, ff_sib, grad_attended, feed_one = tie(left, ff_sib, grad_attended, feed_one)
    mixed_own = half_of(middle, c).astype(F32) + half_of(ff, c).astype(F32) + ff_sib.astype(F32)
    mixed_own, memory_end, grad_attended = tie(mixed_own.astype(BF16), memory_end, grad_attended)
    mixed_came = send(mixed_own, paths.turned)
    memory_came = send(memory_end, paths.turned)
    right = back(1, natural, grad_attended, more=(core, x, left[5]))
    right, mixed_came, memory_came, feed_two = tie(right, mixed_came, memory_came, feed_two)
    stays = c == y
    mixed = jnp.where(stays, mixed_own, mixed_came)
    final_memory = jnp.where(stays, memory_end, memory_came)
    right, mixed, final_memory = tie(right, mixed, final_memory)
    dws, dwu, dgate, dmemory, (dw_left, dw_right) = list(zip(left, right))[:5]
    gy_own, gy_give, dgain_one = right[5:]
    gt, gc, last, ready = leave(
        paths.order,
        dw_right,
        dw_left,
        (feed_one, feed_two),
        dws,
        dwu,
        dgate,
        dmemory,
        dgain_one,
        dgain_two,
        flags,
        gy_own,
        gy_give,
        gain_one,
        x.reshape(2, half_rows, -1),
        grad_middle.reshape(2, half_rows, -1),
    )
    (
        grad_tokens,
        grad_carried,
        out_input,
        out_output,
        out_state,
        out_update,
        out_gate,
        out_initial,
        out_one,
        out_two,
        out_up,
        out_down,
    ) = unpack(
        core,
        (gt, gc, last, *ready),
        (
            input_weights.shape,
            (depth, cols),
            state_weights.shape,
            update_weights.shape,
            gate_bias.shape,
            initial_state.shape,
            (1, depth),
            (1, depth),
            (depth, units),
            (depth, units),
        ),
    )
    return (
        mixed,
        final_memory[None],
        grad_tokens,
        grad_carried[None],
        out_one[0],
        out_input,
        out_state,
        out_update,
        out_gate,
        out_initial,
        out_output.T,
        out_two[0],
        out_up,
        out_down.T,
    )


def solution(mesh):
    ranks, groups = mesh.shape["dp"], mesh.shape["tp"]
    chosen = functools.partial(body, ranks // 2) if groups == 2 else general_body
    placed = (
        P(("dp", "tp"), None),
        P("dp", None, "tp"),
        P("dp"),
        P("dp"),
        P("dp"),
        P(None, "dp", "tp"),
        P("tp", "dp", None),
        P("tp", "dp", None),
        P("tp", "dp"),
        P("dp", "tp"),
        P("tp", "dp"),
        P("dp"),
        P("dp", "tp"),
        P("tp", "dp"),
        P(("dp", "tp"), None),
        P("dp", None, "tp"),
    )
    return jax.shard_map(
        chosen,
        mesh=mesh,
        in_specs=placed,
        out_specs=(
            P(("dp", "tp"), None),
            P("dp", None, "tp"),
            P(("dp", "tp"), None),
            P("dp", None, "tp"),
            P("dp"),
            P(None, "dp", "tp"),
            P("tp", "dp", None),
            P("tp", "dp", None),
            P("tp", "dp"),
            P("dp", "tp"),
            P("tp", "dp"),
            P("dp"),
            P("dp", "tp"),
            P("tp", "dp"),
        ),
        check_vma=False,
    )
```
